32 devices in a mesh: tm: 8 (over z, y), chan: 4 (over x, core).
Axes of the slice: x: 2, y: 2, z: 4, core: 2. Of those that a mesh axis runs over, the one named last changes fastest.
Arguments:
- spectrogram_input: bfloat16 [512, 8192], P('chan', 'tm'), may hold values from -6 to 6
- upsample_direction: float32 [16, 256, 512], P(None, 'chan'), may hold values from -0.09375 to 0.09375
- upsample_magnitude: float32 [512], replicated, may hold values from 0.5 to 2
- upsample_bias: float32 [256], P('chan'), may hold values from -3 to 3
- dilated_direction: float32 [3, 3, 256, 256], P(None, None, 'chan'), may hold values from -0.21875 to 0.21875
- dilated_magnitude: float32 [3, 256], P(None, 'chan'), may hold values from 0.5 to 2
- dilated_bias: float32 [3, 256], P(None, 'chan'), may hold values from -3 to 3
- pointwise_direction: float32 [3, 256, 256], P(None, 'chan'), may hold values from -0.375 to 0.375
- pointwise_magnitude: float32 [3, 256], P(None, 'chan'), may hold values from 0.5 to 2
- block_output_bias: float32 [3, 256], P(None, 'chan'), may hold values from -3 to 3
- shortcut_direction: float32 [3, 256, 256], P(None, 'chan'), may hold values from -0.375 to 0.375
- shortcut_magnitude: float32 [3, 256], P(None, 'chan'), may hold values from 0.5 to 2
- cotangent: bfloat16 [256, 65536], P('chan', 'tm'), may hold values from -6 to 6
- silence: int32 [65536], P('tm'), may hold values 0 or 1
- segments: int32 [8192], replicated, may hold values from 0 to 4, as said below
Outputs:
- activation: bfloat16 [256, 65536], P('chan', 'tm')
- input_grad: bfloat16 [512, 8192], P('chan', 'tm')
- up_v_grad: float32 [16, 256, 512], P(None, 'chan')
- up_g_grad: float32 [512], replicated
- up_b_grad: float32 [256], P('chan')
- dilated_direction_gradient: float32 [3, 3, 256, 256], P(None, None, 'chan')
- dil_g_grad: float32 [3, 256], P(None, 'chan')
- dilated_bias_gradient: float32 [3, 256], P(None, 'chan')
- mix_v_grad: float32 [3, 256, 256], P(None, 'chan')
- mix_g_grad: float32 [3, 256], P(None, 'chan')
- out_b_grad: float32 [3, 256], P(None, 'chan')
- skip_v_grad: float32 [3, 256, 256], P(None, 'chan')
- skip_g_grad: float32 [3, 256], P(None, 'chan')
The draws below stay inside these ranges and needn't reach their ends.
Inputs may be any that keep to these rules, and one draw needn't show every extreme that they name: `segments`: segment numbers of the frames never fall; they rise by one at each segment's first frame, and such rises occur only within the first 1024 and the last 1024 frames (never at frame 0, 1024 or 8192 - 1024).
All inputs are finite; a program needn't handle non-finite values. No bound on the sum of `silence` on one device may be relied on, other than what follows from the above.
Results may differ from the reference program's by a relative error of at most 0.028.
Values may be sent and summed in bfloat16 or wider, within the bound.
No kernel may reach another device: no remote copies, remote signals or barrier semaphores. Data moves between devices by JAX's collectives and lax.ppermute only.
A program may use at most 192 MiB of HBM per device.

```python
import math
from functools import partial
import jax
import jax.numpy as jnp
from jax import lax

CIN = 512
OUTPUT_CHANNELS = 256
KERNEL = 16
DILATED_TAPS = 3
RESIDUAL_BLOCKS = 3
FD = 1024
FRAMES = 8192
SAMPLES = 65536


def draw_segments(key, part):
    key = jax.random.fold_in(key, 7)
    first_key, last_key = jax.random.split(key)
    first_cuts = jax.random.permutation(first_key, FD - 1)[:2] + 1
    last_cuts = jax.random.permutation(last_key, FD - 1)[:2] + 1 + (FRAMES - FD)
    cut_points = jnp.concatenate([first_cuts, last_cuts]).astype(jnp.int32)
    positions = jnp.arange(FRAMES, dtype=jnp.int32)
    starts = jnp.sum((positions[:, None] == cut_points[None, :]).astype(jnp.int32), axis=1)
    return jnp.cumsum(starts).astype(jnp.int32)


def place_ends(drawn, own_key, least, top_value):
    longest = drawn.shape.index(max(drawn.shape))
    spots = []
    for shift in (0, 1):
        where = [jax.random.randint(jax.random.fold_in(own_key, axis), (), 0, length) for axis, length in enumerate(drawn.shape)]
        where[longest] = (where[longest] + shift) % drawn.shape[longest]
        spots.append(tuple(where))
    return drawn.at[spots[0]].set(least).at[spots[1]].set(top_value)


def steps_of(key, dims, cuts, least, largest):
    factor_of, own = 1.0, jax.random.fold_in(key, 6)
    for position, shards_of in cuts:
        draws = jnp.exp(jax.random.uniform(jax.random.fold_in(own, position), (shards_of,), jnp.float32, least / len(cuts), largest / len(cuts)))
        factor_of = factor_of * jnp.repeat(draws, dims[position] // shards_of).reshape([-1 if axis == position else 1 for axis in range(len(dims))])
    return factor_of


def normal_values(stream_key, shape, scale, limit, pieces=(), kind=jnp.bfloat16):
    drawn = jax.random.normal(stream_key, shape, jnp.float32) * scale
    if len(pieces) > 0:
        drawn = steps_of(stream_key, shape, pieces, -0.22, 0.18) * drawn
    return jnp.clip(drawn, min=-limit, max=limit).astype(kind)


def setup_inputs(seed: int = 0) -> dict:
    seeds = jax.random.split(jax.random.key(seed), 16)
    spectrogram_input = normal_values(seeds[0], (CIN, FRAMES), 1.0, 6.0, ((0, 4), (1, 8)))
    upsample_direction = normal_values(seeds[1], (KERNEL, OUTPUT_CHANNELS, CIN), (KERNEL * OUTPUT_CHANNELS) ** -0.5, 0.09375, ((1, 4),), jnp.float32)
    upsample_magnitude = jnp.clip(jnp.exp(jax.random.uniform(seeds[2], (CIN,), jnp.float32, math.log(0.5), math.log(2.0))), 0.5, 2.0)
    upsample_bias = normal_values(seeds[3], (OUTPUT_CHANNELS,), 0.5, 3.0, ((0, 4),), jnp.float32)
    dilated_direction = normal_values(seeds[4], (RESIDUAL_BLOCKS, DILATED_TAPS, OUTPUT_CHANNELS, OUTPUT_CHANNELS), (DILATED_TAPS * OUTPUT_CHANNELS) ** -0.5, 0.21875, ((2, 4),), jnp.float32)
    dilated_magnitude = jnp.clip(jnp.exp(math.log(2.0) - 1.3862944 * jax.random.uniform(seeds[5], (RESIDUAL_BLOCKS, OUTPUT_CHANNELS), jnp.float32) ** steps_of(seeds[5], (RESIDUAL_BLOCKS, OUTPUT_CHANNELS), ((1, 4),), -0.2, 0.2)), 0.5, 2.0)
    dilated_bias = normal_values(seeds[6], (RESIDUAL_BLOCKS, OUTPUT_CHANNELS), 0.5, 3.0, ((1, 4),), jnp.float32)
    pointwise_direction = normal_values(seeds[7], (RESIDUAL_BLOCKS, OUTPUT_CHANNELS, OUTPUT_CHANNELS), OUTPUT_CHANNELS ** -0.5, 0.375, ((1, 4),), jnp.float32)
    pointwise_magnitude = jnp.clip(jnp.exp(math.log(2.0) - 1.3862944 * jax.random.uniform(seeds[8], (RESIDUAL_BLOCKS, OUTPUT_CHANNELS), jnp.float32) ** steps_of(seeds[8], (RESIDUAL_BLOCKS, OUTPUT_CHANNELS), ((1, 4),), -0.2, 0.2)), 0.5, 2.0)
    block_output_bias = normal_values(seeds[9], (RESIDUAL_BLOCKS, OUTPUT_CHANNELS), 0.5, 3.0, ((1, 4),), jnp.float32)
    shortcut_direction = normal_values(seeds[10], (RESIDUAL_BLOCKS, OUTPUT_CHANNELS, OUTPUT_CHANNELS), OUTPUT_CHANNELS ** -0.5, 0.375, ((1, 4),), jnp.float32)
    shortcut_magnitude = jnp.clip(jnp.exp(math.log(2.0) - 1.3862944 * jax.random.uniform(seeds[11], (RESIDUAL_BLOCKS, OUTPUT_CHANNELS), jnp.float32) ** steps_of(seeds[11], (RESIDUAL_BLOCKS, OUTPUT_CHANNELS), ((1, 4),), -0.2, 0.2)), 0.5, 2.0)
    cotangent = normal_values(seeds[12], (OUTPUT_CHANNELS, SAMPLES), 1.0, 6.0, ((0, 4), (1, 8)))
    silence = place_ends((jax.random.randint(seeds[13], (SAMPLES,), 0, 4) < 3).astype(jnp.int32), jax.random.fold_in(seeds[13], 1), 0, 1)
    segments = draw_segments(jax.random.fold_in(seeds[15], 71), 0)
    return {"spectrogram_input": spectrogram_input, "upsample_direction": upsample_direction, "upsample_magnitude": upsample_magnitude, "upsample_bias": upsample_bias, "dilated_direction": dilated_direction, "dilated_magnitude": dilated_magnitude, "dilated_bias": dilated_bias, "pointwise_direction": pointwise_direction, "pointwise_magnitude": pointwise_magnitude, "block_output_bias": block_output_bias, "shortcut_direction": shortcut_direction, "shortcut_magnitude": shortcut_magnitude, "cotangent": cotangent, "silence": silence, "segments": segments}


@jax.custom_vjp
def low(v):
    return lax.optimization_barrier(v.astype(jnp.bfloat16)).astype(jnp.float32)

@jax.custom_vjp
def low_back(v):
    return v

def low_keep(v):
    return (low(v), None)

def low_pass(kept, grad):
    return (grad,)

def back_keep(v):
    return (v, None)

def back_low(kept, grad):
    return (low(grad),)
low.defvjp(low_keep, low_pass)
low_back.defvjp(back_keep, back_low)
HIGHEST = lax.Precision.HIGHEST

def leaky_soft(values):
    return 0.2 * values + 0.8 * values * jax.nn.sigmoid(values)

def matrix_product(form, left_op, right_op):
    return jnp.einsum(form, left_op, right_op, precision=HIGHEST)

def weight_normalize(directions, gain_rows, reduce_axes):
    return low(gain_rows * directions / jnp.sqrt(lax.optimization_barrier(jnp.sum(directions * directions, axis=reduce_axes, keepdims=True))))

def same_segment(sample_ids, offset, signal_length):
    return (sample_ids[16 + offset:16 + offset + signal_length] == sample_ids[16:16 + signal_length]).astype(jnp.float32)

def residual_unit_block(tap_spacing, tap_mask_list, hidden_state, dilated_direction, dilated_magnitude, dilated_bias, pointwise_direction, pointwise_magnitude, block_output_bias, shortcut_direction, shortcut_magnitude):
    signal_length = hidden_state.shape[1]
    hid_low = low(hidden_state)
    padded = jnp.pad(hid_low, ((0, 0), (tap_spacing, tap_spacing)))
    activated_rows = low(leaky_soft(padded))
    dilated_weight = weight_normalize(dilated_direction, dilated_magnitude[None, :, None], (0, 2))
    pointwise_weight = weight_normalize(pointwise_direction, pointwise_magnitude[:, None], (1,))
    shortcut_weight = weight_normalize(shortcut_direction, shortcut_magnitude[:, None], (1,))
    inner_before = dilated_bias[:, None] + jnp.zeros((dilated_direction.shape[1], signal_length), jnp.float32)
    for kernel_offset in range(3):
        inner_before = inner_before + tap_mask_list[kernel_offset] * matrix_product('kt,td->kd', dilated_weight[kernel_offset], activated_rows[:, kernel_offset * tap_spacing:kernel_offset * tap_spacing + signal_length])
    inner_before = low_back(inner_before)
    middle = low(leaky_soft(inner_before))
    return low_back(matrix_product('kt,td->kd', pointwise_weight, middle) + matrix_product('kt,td->kd', shortcut_weight, hid_low) + block_output_bias[:, None])

def generator_section(silence_mask_rows, segments, mel_single_float, upsample_direction, upsample_magnitude, upsample_bias, dilated_direction, dilated_magnitude, dilated_bias, pointwise_direction, pointwise_magnitude, block_output_bias, shortcut_direction, shortcut_magnitude):
    frame_count = mel_single_float.shape[1]
    signal_length = 8 * frame_count
    segpad = jnp.pad(segments, 2, constant_values=-1)
    left_ok = (segpad[1:frame_count + 1] == segpad[2:frame_count + 2]).astype(jnp.float32)
    right_ok = (segpad[3:frame_count + 3] == segpad[2:frame_count + 2]).astype(jnp.float32)
    sample_ids = jnp.repeat(segpad, 8)
    activated_rows = low(leaky_soft(mel_single_float))
    up_w = weight_normalize(upsample_direction, upsample_magnitude[None, None, :], (0, 1))
    tap_sums = matrix_product('koi,is->kos', up_w, jnp.pad(activated_rows, ((0, 0), (1, 1))))
    side_terms = jnp.concatenate([tap_sums[12:16, :, 0:frame_count] * left_ok, tap_sums[0:4, :, 2:frame_count + 2] * right_ok], axis=0)
    joined = tap_sums[4:12, :, 1:frame_count + 1] + side_terms
    hidden_state = low_back(jnp.transpose(joined, (1, 2, 0)).reshape(joined.shape[1], signal_length) + upsample_bias[:, None])
    for dilation_level in range(dilated_direction.shape[0]):
        tap_spacing = 3 ** dilation_level
        tap_mask_list = tuple((same_segment(sample_ids, (kernel_offset - 1) * tap_spacing, signal_length) for kernel_offset in range(3)))
        block_function = jax.checkpoint(partial(residual_unit_block, tap_spacing, tap_mask_list))
        hidden_state = block_function(hidden_state, dilated_direction[dilation_level], dilated_magnitude[dilation_level], dilated_bias[dilation_level], pointwise_direction[dilation_level], pointwise_magnitude[dilation_level], block_output_bias[dilation_level], shortcut_direction[dilation_level], shortcut_magnitude[dilation_level])
    return hidden_state * silence_mask_rows[None, :]

def reference(spectrogram_input, upsample_direction, upsample_magnitude, upsample_bias, dilated_direction, dilated_magnitude, dilated_bias, pointwise_direction, pointwise_magnitude, block_output_bias, shortcut_direction, shortcut_magnitude, cotangent, silence, segments):
    silence_mask_rows = silence.astype(jnp.float32)
    forward_function = partial(generator_section, silence_mask_rows, segments)
    final_result, pullback_function = jax.vjp(forward_function, spectrogram_input.astype(jnp.float32), upsample_direction, upsample_magnitude, upsample_bias, dilated_direction, dilated_magnitude, dilated_bias, pointwise_direction, pointwise_magnitude, block_output_bias, shortcut_direction, shortcut_magnitude)
    gradients = pullback_function(cotangent.astype(jnp.float32))
    return (final_result.astype(jnp.bfloat16), gradients[0].astype(jnp.bfloat16), gradients[1], gradients[2], gradients[3], gradients[4], gradients[5], gradients[6], gradients[7], gradients[8], gradients[9], gradients[10], gradients[11])
```

```python
import functools

import jax
import jax.numpy as jnp
from jax import lax
from jax.experimental import pallas as pl
from jax.experimental.pallas import tpu as pltpu
from jax.sharding import PartitionSpec as P

BF = jnp.bfloat16
F32 = jnp.float32
LANES = 128
HALO = 128
CHUNK = 256
TAIL = 128
VMEM_LIMIT = 60 * 1024 * 1024


def swap(values, axis, bit):
    count = lax.axis_size(axis)
    return lax.ppermute(values, axis, [(k, k ^ bit) for k in range(count)])


def bits_of(count):
    bits = []
    bit = 1
    while bit < count:
        bits.append(bit)
        bit = 2 * bit
    return bits


def add_low(*terms):
    total = terms[0].astype(F32)
    for term in terms[1:]:
        total = total + term.astype(F32)
    return total.astype(BF)


def gather_chan(own):
    held = {0: own}
    for bit in reversed(bits_of(lax.axis_size("chan"))):
        for slot in list(held):
            held[slot ^ bit] = swap(held[slot], "chan", bit)
    return [held[slot] for slot in range(len(held))]


def exchange_chan(pieces):
    return [pieces[0]] + [swap(pieces[s], "chan", s) for s in range(1, len(pieces))]


def scatter_chan(pieces):
    held = dict(enumerate(pieces))
    for bit in bits_of(len(pieces)):
        for slot in sorted(held):
            if slot & bit:
                held[slot ^ bit] = add_low(held[slot ^ bit], swap(held[slot], "chan", bit))
        held = {slot: piece for slot, piece in held.items() if not slot & bit}
    return held[0]


def kernel_call(body, outs, args, scratch=(), flops=0, specs=None):
    if specs is None:
        specs = [None] * len(args)
    in_specs = [
        pl.BlockSpec(memory_space=pltpu.VMEM) if spec is None else spec for spec in specs
    ]
    moved = sum(a.size * a.dtype.itemsize for a in args)
    moved = moved + sum(o.size * o.dtype.itemsize for o in outs)
    return pl.pallas_call(
        body,
        out_shape=tuple(outs),
        in_specs=in_specs,
        out_specs=tuple(pl.BlockSpec(memory_space=pltpu.VMEM) for _ in outs),
        scratch_shapes=list(scratch),
        compiler_params=pltpu.CompilerParams(vmem_limit_bytes=VMEM_LIMIT),
        cost_estimate=pl.CostEstimate(
            flops=int(flops), bytes_accessed=int(moved), transcendentals=0
        ),
    )(*args)


SMEM = pl.BlockSpec(memory_space=pltpu.SMEM)


def shaped(shape, dtype):
    return jax.ShapeDtypeStruct(shape, dtype)


def unit(values):
    th = jnp.tanh(0.5 * values)
    base = 0.6 + 0.4 * th
    return values * base, base + 0.2 * values * (1.0 - th * th)


def unit_act(values):
    return values * (0.6 + 0.4 * jnp.tanh(0.5 * values))


def dot(left, right):
    return lax.dot_general(left, right, (((1,), (0,)), ((), ())), preferred_element_type=F32)


def dot_rt(left, right):
    return lax.dot_general(left, right, (((1,), (1,)), ((), ())), preferred_element_type=F32)


def eye_mask(count):
    rows = lax.broadcasted_iota(jnp.int32, (count, count), 0)
    cols = lax.broadcasted_iota(jnp.int32, (count, count), 1)
    return rows == cols


def to_col(row, eye):
    return jnp.sum(jnp.where(eye, row, 0.0), axis=1, keepdims=True)


def to_row(col, eye):
    return jnp.sum(jnp.where(eye, col, 0.0), axis=0, keepdims=True)


def at(start, size, step):
    return pl.ds(pl.multiple_of(start, step), size)


def prep_kernel(
    up_v, dil_v, dil_g, dil_b, mix_v, mix_g, out_b, skip_v, skip_g, cot, sil,
    up_sq, packed, order, left_edge, right_edge,
):
    taps = up_v.shape[0]
    local_out = up_v.shape[1]
    total = jnp.zeros((1, up_v.shape[2]), F32)
    for k in range(taps):
        rows = up_v[k]
        total = total + jnp.sum(rows * rows, axis=0, keepdims=True)
    up_sq[...] = total
    eye = eye_mask(local_out)
    lane = lax.broadcasted_iota(jnp.int32, (local_out, TAIL), 1)
    width = dil_v.shape[3]
    for j in range(dil_v.shape[0]):
        rows = pl.ds(j * local_out, local_out)
        square = jnp.zeros((local_out, 1), F32)
        for k in range(3):
            v = dil_v[j, k]
            square = square + jnp.sum(v * v, axis=1, keepdims=True)
        norm = jnp.sqrt(square)
        gain = to_col(dil_g[j : j + 1, :], eye)
        for k in range(3):
            packed[rows, k * width : (k + 1) * width] = (gain * dil_v[j, k] / norm).astype(BF)
        for number, (vref, gref) in enumerate(((mix_v, mix_g), (skip_v, skip_g))):
            v = vref[j]
            norm = jnp.sqrt(jnp.sum(v * v, axis=1, keepdims=True))
            gain = to_col(gref[j : j + 1, :], eye)
            packed[rows, (3 + number) * width : (4 + number) * width] = (gain * v / norm).astype(BF)
        first = to_col(dil_b[j : j + 1, :], eye)
        second = to_col(out_b[j : j + 1, :], eye)
        high_one = first.astype(BF).astype(F32)
        high_two = second.astype(BF).astype(F32)
        tail = jnp.where(lane == 0, high_one, 0.0) + jnp.where(lane == 1, first - high_one, 0.0)
        tail = tail + jnp.where(lane == 2, high_two, 0.0)
        tail = tail + jnp.where(lane == 3, second - high_two, 0.0)
        packed[rows, 5 * width : 5 * width + TAIL] = tail.astype(BF)
    size = order.shape[0]
    source = lax.broadcasted_iota(jnp.int32, (size, size), 0)
    target = lax.broadcasted_iota(jnp.int32, (size, size), 1)
    hit = target == 8 * (source & (LANES - 1)) + (source >> 7)
    order[...] = jnp.where(hit, 1.0, 0.0).astype(BF)
    count = cot.shape[1]
    left_edge[...] = (
        cot[:, 0:HALO].astype(F32) * sil[:, 0:HALO].astype(F32)
    ).astype(BF)
    right_edge[...] = (
        cot[:, count - HALO : count].astype(F32) * sil[:, count - HALO : count].astype(F32)
    ).astype(BF)


def cut_kernel(pieces, idx, cot, sil, low, high, *refs):
    outs, wide = refs[:pieces], refs[pieces]
    count = cot.shape[1]
    own = count // pieces
    wide[:, 0:HALO] = low[...]
    wide[:, HALO : HALO + count] = (cot[...].astype(F32) * sil[...].astype(F32)).astype(BF)
    wide[:, HALO + count :] = high[...]
    for s in range(pieces):
        peer = idx[1] ^ s
        outs[s][...] = wide[:, at(peer * own, own + 2 * HALO, LANES)]


def weight_kernel(pieces, blocks, idx, *refs):
    parts, (plain, dil_t, point_t) = refs[:pieces], refs[pieces:]
    rows = parts[0].shape[0] // blocks
    for s in range(pieces):
        start = (idx[1] ^ s) * rows
        for j in range(blocks):
            plain[j, at(start, rows, 16), :] = parts[s][j * rows : (j + 1) * rows, :]
    width = plain.shape[1]
    for j in range(blocks):
        for k in range(5):
            turned = jnp.transpose(plain[j, :, k * width : (k + 1) * width])
            if k < 3:
                dil_t[j, :, k * width : (k + 1) * width] = turned
            else:
                point_t[j, :, (k - 3) * width : (k - 2) * width] = turned


def up_kernel(pieces, idx, *refs):
    mains, sides = refs[:pieces], refs[pieces : 2 * pieces]
    up_v, up_sq, up_g, up_b, frame_id, order = refs[2 * pieces : 2 * pieces + 6]
    outs = refs[2 * pieces + 6 : 3 * pieces + 6]
    act_out, up_w = refs[3 * pieces + 6 : 3 * pieces + 8]
    raw, stacked, phases, wide = refs[3 * pieces + 8 :]
    rows, frames = mains[0].shape
    local_out = up_v.shape[1]
    for s in range(pieces):
        here = at((idx[1] ^ s) * rows, rows, 16)
        raw[here, 0:LANES] = sides[s][:, 0:LANES]
        raw[here, LANES : LANES + frames] = mains[s][...]
        raw[here, LANES + frames :] = sides[s][:, LANES:]
    scale = up_g[...] / jnp.sqrt(up_sq[...])
    norm = jnp.sqrt(up_sq[...])
    for k in range(up_v.shape[0]):
        up_w[k * local_out : (k + 1) * local_out, :] = (up_g[...] * up_v[k] / norm).astype(BF)
    del scale
    total = frames + 2 * LANES
    count = stacked.shape[1]
    channels = raw.shape[0]
    shift = total - (LANES - HALO // 8)
    ids = pltpu.roll(jnp.broadcast_to(frame_id[...], (8, total)), shift, axis=1)
    before = pltpu.roll(ids, 1, axis=1)
    after = pltpu.roll(ids, total - 1, axis=1)
    left = jnp.where(before == ids, 1.0, 0.0)[0:1, :]
    right = jnp.where(after == ids, 1.0, 0.0)[0:1, :]
    step = LANES
    for r0 in range(0, channels, step):
        part = pl.ds(r0, step)
        acted = unit_act(raw[part, :].astype(F32)).astype(BF)
        act_out[part, :] = acted[:, LANES : LANES + frames]
        moved = pltpu.roll(acted, shift, axis=1)
        one = pltpu.roll(moved, 1, axis=1).astype(F32) * left
        two = pltpu.roll(moved, total - 1, axis=1).astype(F32) * right
        stacked[part, :] = moved[:, 0:count]
        stacked[pl.ds(channels + r0, step), :] = one[:, 0:count].astype(BF)
        stacked[pl.ds(2 * channels + r0, step), :] = two[:, 0:count].astype(BF)
    eye = eye_mask(local_out)
    bias = to_col(up_b[...], eye)
    bias4 = jnp.concatenate([bias] * 4, axis=0)
    quarter = 4 * local_out
    for c0 in range(0, count, 3 * LANES):
        cols = pl.ds(c0, 3 * LANES)
        center = stacked[0:channels, cols]
        low = dot(up_w[quarter : 2 * quarter, :], center)
        low = low + dot(up_w[3 * quarter : 4 * quarter, :], stacked[channels : 2 * channels, cols])
        high = dot(up_w[2 * quarter : 3 * quarter, :], center)
        high = high + dot(up_w[0:quarter, :], stacked[2 * channels : 3 * channels, cols])
        low = (low + bias4).astype(BF)
        high = (high + bias4).astype(BF)
        for b in range(3):
            block = c0 // LANES + b
            if block * local_out >= phases.shape[0]:
                continue
            for r in range(8):
                source = (low, high)[r // 4]
                phases[block * local_out : (block + 1) * local_out, r * LANES : (r + 1) * LANES] = (
                    source[
                        (r % 4) * local_out : (r % 4 + 1) * local_out,
                        b * LANES : (b + 1) * LANES,
                    ]
                )
    for block in range(count // LANES):
        piece = dot(phases[block * local_out : (block + 1) * local_out, :], order[...])
        wide[:, block * 1024 : (block + 1) * 1024] = piece.astype(BF)
    own = 8 * frames // pieces
    for s in range(pieces):
        outs[s][...] = wide[:, at((idx[1] ^ s) * own, own + 2 * HALO, LANES)]


def sample_masks(sample_id, distance):
    width = sample_id.shape[1]
    ids = jnp.broadcast_to(sample_id[...], (8, width))
    back = pltpu.roll(ids, distance, axis=1)
    ahead = pltpu.roll(ids, width - distance, axis=1)
    return (
        jnp.where(back == ids, 1.0, 0.0)[0:1, :].astype(BF),
        jnp.where(ahead == ids, 1.0, 0.0)[0:1, :].astype(BF),
    )


def forward_kernel(pieces, blocks, idx, *refs):
    parts = refs[:pieces]
    plain, sample_id, silence = refs[pieces : pieces + 3]
    outs = refs[pieces + 3 : 2 * pieces + 3]
    kept = refs[2 * pieces + 3 : 2 * pieces + 8]
    hidden, taps, pair, final = refs[2 * pieces + 8 :]
    keep_h, keep_u, keep_m, keep_sh, keep_sc = kept
    rows, width = parts[0].shape
    channels = pieces * rows
    for s in range(pieces):
        hidden[at((idx[1] ^ s) * rows, rows, 16), :] = parts[s][...]
    chunks = width // CHUNK
    for j in range(blocks):
        distance = 3**j
        tail = plain[j, :, 5 * channels : 5 * channels + TAIL].astype(F32)
        dil_b = tail[:, 0:1] + tail[:, 1:2]
        out_b = tail[:, 2:3] + tail[:, 3:4]

        def first(i, carry):
            cols = at(i * CHUNK, CHUNK, CHUNK)
            low = hidden[:, cols]
            keep_h[j, :, cols] = low
            pair[channels : 2 * channels, cols] = low
            acted, slope = unit(low.astype(F32))
            acted = acted.astype(BF)
            taps[channels : 2 * channels, cols] = acted
            keep_u[j, :, cols] = acted
            keep_sh[j, :, cols] = slope.astype(BF)
            return carry

        lax.fori_loop(0, chunks, first, 0)
        back, ahead = sample_masks(sample_id, distance)
        center = taps[channels : 2 * channels, :]
        taps[0:channels, :] = pltpu.roll(center, distance, axis=1) * back
        taps[2 * channels : 3 * channels, :] = pltpu.roll(center, width - distance, axis=1) * ahead

        def second(i, carry):
            cols = at(i * CHUNK, CHUNK, CHUNK)
            inner = dot(plain[j, :, 0 : 3 * channels], taps[:, cols]) + dil_b
            acted, slope = unit(inner)
            acted = acted.astype(BF)
            pair[0:channels, cols] = acted
            keep_m[j, :, cols] = acted
            keep_sc[j, :, cols] = slope.astype(BF)
            after = dot(plain[j, :, 3 * channels : 5 * channels], pair[:, cols]) + out_b
            if j < blocks - 1:
                hidden[:, cols] = after.astype(BF)
            else:
                final[:, cols] = after
            return carry

        lax.fori_loop(0, chunks, second, 0)
    own = width - 2 * HALO
    voiced = silence[:, at(idx[1] * own, own, LANES)].astype(F32)
    for s in range(pieces):
        here = at((idx[1] ^ s) * rows, rows, 16)
        outs[s][...] = (final[here, HALO : HALO + own] * voiced).astype(BF)


def backward_kernel(pieces, blocks, idx, *refs):
    parts = refs[:pieces]
    dil_t, point_t, sample_id = refs[pieces : pieces + 3]
    keep_h, keep_u, keep_m, keep_sh, keep_sc = refs[pieces + 3 : pieces + 8]
    outs = refs[pieces + 8 : 2 * pieces + 8]
    grads = refs[2 * pieces + 8 : 3 * pieces + 8]
    err, taps, packed = refs[3 * pieces + 8 :]
    rows, width = parts[0].shape
    channels = pieces * rows
    own = width - 2 * HALO
    for s in range(pieces):
        err[at((idx[1] ^ s) * rows, rows, 16), :] = parts[s][...]
    chunks = width // CHUNK
    lane = lax.broadcasted_iota(jnp.int32, (channels, TAIL), 1)
    for j in reversed(range(blocks)):
        distance = 3**j

        def first(i, carry):
            cols = at(i * CHUNK, CHUNK, CHUNK)
            inner = dot(point_t[j, :, 0:channels], err[:, cols])
            inner = inner * keep_sc[j, :, cols].astype(F32)
            taps[channels : 2 * channels, cols] = inner.astype(BF)
            return carry

        lax.fori_loop(0, chunks, first, 0)
        back, ahead = sample_masks(sample_id, distance)
        center = taps[channels : 2 * channels, :]
        taps[0:channels, :] = pltpu.roll(center, width - distance, axis=1) * ahead
        taps[2 * channels : 3 * channels, :] = pltpu.roll(center, distance, axis=1) * back
        inside = pl.ds(HALO, own)
        err_own = err[:, inside]
        packed[:, 3 * channels : 4 * channels] = dot_rt(err_own, keep_m[j, :, inside]).astype(BF)
        packed[:, 4 * channels : 5 * channels] = dot_rt(err_own, keep_h[j, :, inside]).astype(BF)
        for k in range(3):
            packed[:, k * channels : (k + 1) * channels] = dot_rt(
                taps[k * channels : (k + 1) * channels, inside], keep_u[j, :, inside]
            ).astype(BF)
        out_sum = jnp.sum(err_own.astype(F32), axis=1, keepdims=True)
        dil_sum = jnp.sum(
            taps[channels : 2 * channels, inside].astype(F32), axis=1, keepdims=True
        )
        packed[:, 5 * channels : 5 * channels + TAIL] = (
            jnp.where(lane == 0, dil_sum, 0.0) + jnp.where(lane == 1, out_sum, 0.0)
        ).astype(BF)
        for s in range(pieces):
            grads[s][j * rows : (j + 1) * rows, :] = packed[at((idx[1] ^ s) * rows, rows, 16), :]

        def second(i, carry):
            cols = at(i * CHUNK, CHUNK, CHUNK)
            spread = dot(dil_t[j], taps[:, cols]) * keep_sh[j, :, cols].astype(F32)
            spread = spread + dot(point_t[j, :, channels : 2 * channels], err[:, cols])
            err[:, cols] = spread.astype(BF)
            return carry

        lax.fori_loop(0, chunks, second, 0)
    for s in range(pieces):
        outs[s][...] = err[at((idx[1] ^ s) * rows, rows, 16), :]


def up_back_kernel(pieces, peers, split, idx, *refs):
    parts = refs[:pieces]
    up_w, up_v, acted, frame_id, order = refs[pieces : pieces + 5]
    outs = refs[pieces + 5 :]
    half = peers // 2
    sums = outs[0]
    inputs = outs[1 : 1 + pieces]
    near = outs[1 + pieces : 1 + pieces + half]
    far = outs[1 + pieces + half]
    extra = 1 if split else 0
    duo = outs[2 + pieces + half : 2 + pieces + half + half * extra]
    wide, phases, cols_grad, weight_grad, low_grad = outs[2 + pieces + half + half * extra :]
    rows, width = parts[0].shape
    own = width - 2 * HALO
    length = pieces * own
    frames = length // 8
    wide[:, HALO + length :] = jnp.zeros((rows, wide.shape[1] - HALO - length), BF)
    for s in range(pieces):
        peer = idx[1] ^ s
        wide[:, at(HALO + peer * own, own, LANES)] = parts[s][:, HALO : HALO + own]

        @pl.when(peer == 0)
        def _():
            wide[:, 0:HALO] = parts[s][:, 0:HALO]

        @pl.when(peer == pieces - 1)
        def _():
            wide[:, HALO + length : 2 * HALO + length] = parts[s][:, HALO + own :]

    total = wide.shape[1] // 8
    for block in range(total // LANES):
        turned = dot_rt(wide[:, block * 1024 : (block + 1) * 1024], order[...]).astype(BF)
        for r in range(8):
            phases[r * rows : (r + 1) * rows, block * LANES : (block + 1) * LANES] = turned[
                :, r * LANES : (r + 1) * LANES
            ]
    ids = jnp.broadcast_to(frame_id[...], (8, frame_id.shape[1]))
    before = pltpu.roll(ids, 1, axis=1)
    after = pltpu.roll(ids, frame_id.shape[1] - 1, axis=1)
    inside = slice(LANES, LANES + frames)
    left = jnp.where(before == ids, 1.0, 0.0)[0:1, inside]
    right = jnp.where(after == ids, 1.0, 0.0)[0:1, inside]
    lead = HALO // 8
    eighth = 4 * rows
    sample_sum = jnp.zeros((rows, 1), F32)
    for part in range(2):
        base = phases[part * eighth : (part + 1) * eighth, :]
        center = pltpu.roll(base, total - lead, axis=1)[:, 0:frames]
        cols_grad[(4 + 4 * part) * rows : (8 + 4 * part) * rows, :] = center
        partial = jnp.sum(center.astype(F32), axis=1, keepdims=True)
        for r in range(4):
            sample_sum = sample_sum + partial[r * rows : (r + 1) * rows]
        if part == 1:
            moved = pltpu.roll(base, total - lead + 1, axis=1)[:, 0:frames]
            cols_grad[0:eighth, :] = (moved.astype(F32) * left).astype(BF)
        else:
            moved = pltpu.roll(base, total - lead - 1, axis=1)[:, 0:frames]
            cols_grad[12 * rows : 16 * rows, :] = (moved.astype(F32) * right).astype(BF)
    taps = up_v.shape[0]
    step = taps * rows // 4
    channels = up_v.shape[2]
    inner = jnp.zeros((1, channels), F32)
    for q in range(4):
        here = pl.ds(q * step, step)
        grad = dot_rt(cols_grad[here, :], acted[...])
        low_grad[here, :] = grad.astype(BF)
        for k in range(taps // 4):
            inner = inner + jnp.sum(
                grad[k * rows : (k + 1) * rows] * up_v[q * taps // 4 + k], axis=0, keepdims=True
            )
    sums[:, 0:channels] = inner
    sums[:, channels:] = jnp.zeros((1, sums.shape[1] - channels), F32)
    eye = eye_mask(rows)
    sums[:, channels : channels + rows] = to_row(sample_sum, eye)
    first = near[0].shape[0]
    for h in range(half):
        near[h][...] = low_grad[at((idx[0] ^ (2 * h)) * first, first, 16), :]
        far[h] = low_grad[at((idx[0] ^ (2 * h + 1)) * first, first, 16), :]
    if split:
        second = duo[0].shape[1]
        for h in range(half):
            for b in range(2):
                start = peers * first + (idx[0] ^ (2 * h + b)) * second
                duo[h][b] = low_grad[at(start, second, 16), :]
    for f in range(0, frames, CHUNK):
        cols = pl.ds(f, CHUNK)
        weight_grad[:, cols] = lax.dot_general(
            up_w[...], cols_grad[:, cols], (((0,), (0,)), ((), ())), preferred_element_type=F32
        ).astype(BF)
    piece = channels // pieces
    for s in range(pieces):
        inputs[s][...] = weight_grad[at((idx[1] ^ s) * piece, piece, 16), :]


def up_final_kernel(peers, split, idx, *refs):
    half = peers // 2
    firsts, others = refs[:half], refs[half]
    duo = refs[half + 1 : half + 1 + (half if split else 0)]
    up_v, up_sq, up_g, sums, up_v_grad, up_g_grad, whole = refs[
        half + 1 + (half if split else 0) :
    ]
    first = firsts[0].shape[0]
    for h in range(half):
        whole[at((idx[0] ^ (2 * h)) * first, first, 16), :] = firsts[h][...]
        whole[at((idx[0] ^ (2 * h + 1)) * first, first, 16), :] = others[h]
    if split:
        second = duo[0].shape[1]
        for h in range(half):
            for b in range(2):
                start = peers * first + (idx[0] ^ (2 * h + b)) * second
                whole[at(start, second, 16), :] = duo[h][b]
    channels = up_v.shape[2]
    norm = jnp.sqrt(up_sq[...])
    inner = sums[:, 0:channels]
    scale = up_g[...] / norm
    pull = up_g[...] * inner / (norm * norm * norm)
    rows = up_v.shape[1]
    for k in range(up_v.shape[0]):
        grad = whole[k * rows : (k + 1) * rows, :].astype(F32)
        up_v_grad[k] = scale * grad - pull * up_v[k]
    up_g_grad[...] = inner / norm


def block_final_kernel(count, idx, *refs):
    parts = refs[:count]
    dil_v, dil_g, mix_v, mix_g, skip_v, skip_g = refs[count : count + 6]
    outs = refs[count + 6 : count + 14]
    whole = refs[count + 14]
    dil_v_out, dil_g_out, dil_b_out, mix_v_out, mix_g_out, out_b_out, skip_v_out, skip_g_out = outs
    size = parts[0].shape[0]
    for h in range(count):
        whole[at(((idx[0] >> 1) ^ h) * size, size, 16), :] = parts[h][...]
    rows, width = dil_v.shape[2], dil_v.shape[3]
    eye = eye_mask(rows)
    for j in range(dil_v.shape[0]):
        here = pl.ds(j * rows, rows)
        square = jnp.zeros((rows, 1), F32)
        inner = jnp.zeros((rows, 1), F32)
        for k in range(3):
            v = dil_v[j, k]
            grad = whole[here, k * width : (k + 1) * width].astype(F32)
            square = square + jnp.sum(v * v, axis=1, keepdims=True)
            inner = inner + jnp.sum(v * grad, axis=1, keepdims=True)
        norm = jnp.sqrt(square)
        gain = to_col(dil_g[j : j + 1, :], eye)
        for k in range(3):
            grad = whole[here, k * width : (k + 1) * width].astype(F32)
            dil_v_out[j, k] = gain / norm * grad - gain * inner / (norm**3) * dil_v[j, k]
        dil_g_out[j : j + 1, :] = to_row(inner / norm, eye)
        for number, (vref, gref, v_out, g_out) in enumerate(
            ((mix_v, mix_g, mix_v_out, mix_g_out), (skip_v, skip_g, skip_v_out, skip_g_out))
        ):
            v = vref[j]
            grad = whole[here, (3 + number) * width : (4 + number) * width].astype(F32)
            norm = jnp.sqrt(jnp.sum(v * v, axis=1, keepdims=True))
            inner = jnp.sum(v * grad, axis=1, keepdims=True)
            gain = to_col(gref[j : j + 1, :], eye)
            v_out[j] = gain / norm * grad - gain * inner / (norm**3) * v
            g_out[j : j + 1, :] = to_row(inner / norm, eye)
        tail = whole[here, 5 * width : 5 * width + TAIL].astype(F32)
        dil_b_out[j : j + 1, :] = to_row(tail[:, 0:1], eye)
        out_b_out[j : j + 1, :] = to_row(tail[:, 1:2], eye)


def join_kernel(pieces, idx, *refs):
    parts, out = refs[:pieces], refs[pieces]
    own = parts[0].shape[1]
    for s in range(pieces):
        out[:, at((idx[1] ^ s) * own, own, LANES)] = parts[s][...]


def input_kernel(*refs):
    *terms, spectrogram, out = refs
    total = terms[0][...].astype(F32)
    for term in terms[1:]:
        total = total + term[...].astype(F32)
    out[...] = (total * unit(spectrogram[...].astype(F32))[1]).astype(BF)


def local(
    spectrogram_input,
    upsample_direction,
    upsample_magnitude,
    upsample_bias,
    dilated_direction,
    dilated_magnitude,
    dilated_bias,
    pointwise_direction,
    pointwise_magnitude,
    block_output_bias,
    shortcut_direction,
    shortcut_magnitude,
    cotangent,
    silence,
    segments,
):
    pieces, peers = lax.axis_size("chan"), lax.axis_size("tm")
    chan, tm = lax.axis_index("chan"), lax.axis_index("tm")
    idx = jnp.stack([tm, chan]).astype(jnp.int32)
    in_rows, frames = spectrogram_input.shape
    taps, rows, in_channels = upsample_direction.shape
    blocks = dilated_direction.shape[0]
    channels = dilated_direction.shape[3]
    length = 8 * frames
    own = length // pieces
    width = own + 2 * HALO
    packed_width = 5 * channels + TAIL
    half = peers // 2
    forward = [(k, k + 1) for k in range(peers - 1)]
    backward = [(k + 1, k) for k in range(peers - 1)]

    sides = jnp.concatenate(
        [
            lax.ppermute(spectrogram_input[:, frames - LANES :], "tm", forward),
            lax.ppermute(spectrogram_input[:, :LANES], "tm", backward),
        ],
        axis=1,
    )
    all_mains = gather_chan(spectrogram_input)
    all_sides = gather_chan(sides)
    silence_row = silence.reshape(1, length)
    padded_ids = jnp.pad(segments.astype(F32), LANES, constant_values=-1.0)
    frame_id = lax.dynamic_slice_in_dim(padded_ids, tm * frames, frames + 2 * LANES)
    lead = HALO // 8
    sample_id = jnp.repeat(
        lax.dynamic_slice_in_dim(
            padded_ids, LANES + tm * frames + chan * (own // 8) - lead, width // 8
        ),
        8,
    ).reshape(1, width)
    frame_id = frame_id.reshape(1, frames + 2 * LANES)

    up_sq, packed, order, left_edge, right_edge = kernel_call(
        prep_kernel,
        [
            shaped((1, in_channels), F32),
            shaped((blocks * rows, packed_width), BF),
            shaped((8 * LANES, 8 * LANES), BF),
            shaped((rows, HALO), BF),
            shaped((rows, HALO), BF),
        ],
        [
            upsample_direction,
            dilated_direction,
            dilated_magnitude,
            dilated_bias,
            pointwise_direction,
            pointwise_magnitude,
            block_output_bias,
            shortcut_direction,
            shortcut_magnitude,
            cotangent,
            silence_row,
        ],
    )
    up_sq = lax.psum(up_sq, "chan")
    up_g = upsample_magnitude.reshape(1, in_channels)
    low_edge = lax.ppermute(right_edge, "tm", forward)
    high_edge = lax.ppermute(left_edge, "tm", backward)

    all_packed = gather_chan(packed)
    count = -(-(frames + 2 * lead) // LANES) * LANES
    count = -(-count // (3 * LANES)) * 3 * LANES
    up_outs = kernel_call(
        functools.partial(up_kernel, pieces),
        [shaped((rows, width), BF)] * pieces
        + [shaped((in_channels, frames), BF), shaped((taps * rows, in_channels), BF)],
        [idx]
        + all_mains
        + all_sides
        + [upsample_direction, up_sq, up_g, upsample_bias.reshape(1, rows), frame_id, order],
        scratch=[
            pltpu.VMEM((in_channels, frames + 2 * LANES), BF),
            pltpu.VMEM((3 * in_channels, count), BF),
            pltpu.VMEM((count // LANES * rows, 8 * LANES), BF),
            pltpu.VMEM((rows, 8 * count), BF),
        ],
        flops=2 * taps * rows * in_channels * count,
        specs=[SMEM] + [None] * (2 * pieces + 6),
    )
    acted, up_w = up_outs[pieces:]
    all_hidden = exchange_chan(list(up_outs[:pieces]))

    plain, dil_t, point_t = kernel_call(
        functools.partial(weight_kernel, pieces, blocks),
        [
            shaped((blocks, channels, packed_width), BF),
            shaped((blocks, channels, 3 * channels), BF),
            shaped((blocks, channels, 2 * channels), BF),
        ],
        [idx] + all_packed,
        specs=[SMEM] + [None] * pieces,
    )
    cut = kernel_call(
        functools.partial(cut_kernel, pieces),
        [shaped((rows, width), BF)] * pieces,
        [idx, cotangent, silence_row, low_edge, high_edge],
        scratch=[pltpu.VMEM((rows, length + 2 * HALO), BF)],
        specs=[SMEM] + [None] * 4,
    )
    tied = lax.optimization_barrier((list(cut), all_hidden))
    cut, all_hidden = tied
    all_err = exchange_chan(cut)

    block_flops = 2 * blocks * 5 * channels * channels * width
    kept_shape = shaped((blocks, channels, width), BF)
    forward_outs = kernel_call(
        functools.partial(forward_kernel, pieces, blocks),
        [shaped((rows, own), BF)] * pieces + [kept_shape] * 5,
        [idx] + all_hidden + [plain, sample_id, silence_row],
        scratch=[
            pltpu.VMEM((channels, width), BF),
            pltpu.VMEM((3 * channels, width), BF),
            pltpu.VMEM((2 * channels, width), BF),
            pltpu.VMEM((channels, width), F32),
        ],
        flops=block_flops,
        specs=[SMEM] + [None] * (pieces + 3),
    )
    kept = list(forward_outs[pieces:])
    activation_parts = exchange_chan(list(forward_outs[:pieces]))

    backward_outs = kernel_call(
        functools.partial(backward_kernel, pieces, blocks),
        [shaped((rows, width), BF)] * pieces
        + [shaped((blocks * rows, packed_width), BF)] * pieces,
        [idx] + all_err + [dil_t, point_t, sample_id] + kept,
        scratch=[
            pltpu.VMEM((channels, width), BF),
            pltpu.VMEM((3 * channels, width), BF),
            pltpu.VMEM((channels, packed_width), BF),
        ],
        flops=2 * block_flops,
        specs=[SMEM] + [None] * (pieces + 8),
    )
    all_low = exchange_chan(list(backward_outs[:pieces]))
    block_grads = list(backward_outs[pieces:])

    total_rows = taps * rows
    split = total_rows % (32 * peers) == 0
    first = total_rows // peers // (2 if split else 1)
    near_shape = shaped((first, in_channels), BF)
    sums_width = in_channels + max(LANES, rows)
    back_outs = kernel_call(
        functools.partial(up_back_kernel, pieces, peers, split),
        [shaped((1, sums_width), F32)]
        + [shaped((in_rows, frames), BF)] * pieces
        + [near_shape] * half
        + [shaped((half, first, in_channels), BF)]
        + [shaped((2, first, in_channels), BF)] * (half if split else 0),
        [idx] + all_low + [up_w, upsample_direction, acted, frame_id, order],
        scratch=[
            pltpu.VMEM((rows, 8 * count), BF),
            pltpu.VMEM((8 * rows, count), BF),
            pltpu.VMEM((total_rows, frames), BF),
            pltpu.VMEM((in_channels, frames), BF),
            pltpu.VMEM((total_rows, in_channels), BF),
        ],
        flops=4 * taps * rows * in_channels * frames,
        specs=[SMEM] + [None] * (pieces + 5),
    )
    sums = back_outs[0]
    input_terms = list(back_outs[1 : 1 + pieces])
    near = list(back_outs[1 + pieces : 1 + pieces + half])
    far = back_outs[1 + pieces + half]
    duo = list(back_outs[2 + pieces + half :])

    far_got = swap(far, "tm", 1)
    if split:
        duo_got = [swap(duo[h], "tm", 2 * h) for h in range(1, half)]
        pair = add_low(duo[0], *duo_got)
        pair_high = swap(pair[1], "tm", 1)
        duo_own = add_low(pair[0], pair_high)
    near = [add_low(near[h], far_got[h]) for h in range(half)]
    near_got = [swap(near[h], "tm", 2 * h) for h in range(1, half)]
    near_own = add_low(near[0], *near_got)
    firsts = [near_own] + [swap(near_own, "tm", 2 * h) for h in range(1, half)]
    others = swap(jnp.stack(firsts), "tm", 1)
    duo_all = []
    if split:
        both = jnp.stack([duo_own, swap(duo_own, "tm", 1)])
        duo_all = [both] + [swap(both, "tm", 2 * h) for h in range(1, half)]
    inner_sum = lax.psum(sums[:, :in_channels], ("tm", "chan"))
    bias_sum = lax.psum(sums[:, in_channels:], "tm")

    input_total = scatter_chan(input_terms)
    (input_grad,) = kernel_call(
        input_kernel,
        [shaped((in_rows, frames), BF)],
        [input_total, spectrogram_input],
    )

    block_sum = scatter_chan(block_grads)
    size = -(-(blocks * rows) // (16 * half)) * 16
    block_sum = jnp.pad(block_sum, ((0, half * size - blocks * rows), (0, 0)))
    block_sum = block_sum.reshape(half, size, packed_width)
    cuts = [
        lax.dynamic_index_in_dim(block_sum, (tm >> 1) ^ h, keepdims=False) for h in range(half)
    ]
    part = add_low(cuts[0], *[swap(cuts[h], "tm", 2 * h) for h in range(1, half)])
    part = add_low(part, swap(part, "tm", 1))
    final_parts = [part] + [swap(part, "tm", 2 * h) for h in range(1, half)]
    block_outs = kernel_call(
        functools.partial(block_final_kernel, half),
        [
            shaped(dilated_direction.shape, F32),
            shaped(dilated_magnitude.shape, F32),
            shaped(dilated_bias.shape, F32),
            shaped(pointwise_direction.shape, F32),
            shaped(pointwise_magnitude.shape, F32),
            shaped(block_output_bias.shape, F32),
            shaped(shortcut_direction.shape, F32),
            shaped(shortcut_magnitude.shape, F32),
        ],
        [idx]
        + final_parts
        + [
            dilated_direction,
            dilated_magnitude,
            pointwise_direction,
            pointwise_magnitude,
            shortcut_direction,
            shortcut_magnitude,
        ],
        scratch=[pltpu.VMEM((half * size, packed_width), BF)],
        specs=[SMEM] + [None] * (half + 6),
    )
    dil_v_grad, dil_g_grad, dil_b_grad, mix_v_grad, mix_g_grad, out_b_grad = block_outs[:6]
    skip_v_grad, skip_g_grad = block_outs[6:]

    up_v_grad, up_g_grad = kernel_call(
        functools.partial(up_final_kernel, peers, split),
        [shaped(upsample_direction.shape, F32), shaped((1, in_channels), F32)],
        [idx] + firsts + [others] + duo_all + [upsample_direction, up_sq, up_g, inner_sum],
        scratch=[pltpu.VMEM((total_rows, in_channels), BF)],
        specs=[SMEM] + [None] * (half + 1 + len(duo_all) + 4),
    )
    (activation,) = kernel_call(
        functools.partial(join_kernel, pieces),
        [shaped((rows, length), BF)],
        [idx] + activation_parts,
        specs=[SMEM] + [None] * pieces,
    )
    return (
        activation,
        input_grad,
        up_v_grad,
        up_g_grad.reshape(in_channels),
        bias_sum[0, :rows],
        dil_v_grad,
        dil_g_grad,
        dil_b_grad,
        mix_v_grad,
        mix_g_grad,
        out_b_grad,
        skip_v_grad,
        skip_g_grad,
    )


def solution(mesh):
    placed = (
        P("chan", "tm"),
        P(None, "chan", None),
        P(),
        P("chan"),
        P(None, None, "chan", None),
        P(None, "chan"),
        P(None, "chan"),
        P(None, "chan", None),
        P(None, "chan"),
        P(None, "chan"),
        P(None, "chan", None),
        P(None, "chan"),
        P("chan", "tm"),
        P("tm"),
        P(),
    )
    return jax.shard_map(
        local,
        mesh=mesh,
        in_specs=placed,
        out_specs=(
            P("chan", "tm"),
            P("chan", "tm"),
            P(None, "chan", None),
            P(),
            P("chan"),
            P(None, None, "chan", None),
            P(None, "chan"),
            P(None, "chan"),
            P(None, "chan", None),
            P(None, "chan"),
            P(None, "chan"),
            P(None, "chan", None),
            P(None, "chan"),
        ),
        check_vma=False,
    )
```

```python
import functools

import jax
import jax.numpy as jnp
from jax import lax
from jax.experimental import pallas as pl
from jax.experimental.pallas import tpu as pltpu
from jax.sharding import PartitionSpec as P

BF = jnp.bfloat16
F32 = jnp.float32
LANES = 128
HALO = 128
TAIL = 128
SUMS = 16
VMEM_LIMIT = 24 * 1024 * 1024


def swap(values, axis, bit):
    count = lax.axis_size(axis)
    return lax.ppermute(values, axis, [(k, k ^ bit) for k in range(count)])


def bits_of(count):
    bits = []
    bit = 1
    while bit < count:
        bits.append(bit)
        bit = 2 * bit
    return bits


def order_of(bits):
    order = [0]
    for bit in reversed(bits):
        order = order + [slot + bit for slot in order]
    return order


def gather_chan(own):
    held = {0: own}
    for bit in reversed(bits_of(lax.axis_size("chan"))):
        for slot in list(held):
            held[slot ^ bit] = swap(held[slot], "chan", bit)
    return [held[slot] for slot in range(len(held))]


def exchange_chan(pieces):
    return [pieces[0]] + [swap(pieces[s], "chan", s) for s in range(1, len(pieces))]


HBM = pl.BlockSpec(memory_space=pltpu.HBM)
ANY = pl.BlockSpec(memory_space=pl.ANY)
VMEM = pl.BlockSpec(memory_space=pltpu.VMEM)


def kernel_call(body, outs, args, specs, scratch=(), micros=1.0):
    held = []
    in_specs = []
    operands = []
    for arg, spec in zip(args, specs, strict=True):
        in_specs.append({"H": HBM, "F": HBM, "A": ANY, "G": ANY, "R": VMEM}[spec])
        if spec in "FG":
            held.append(pltpu.VMEM(arg.shape, arg.dtype))
        if spec == "R":
            arg = pltpu.with_memory_space_constraint(arg, pltpu.VMEM)
        if spec in "HF":
            arg = pltpu.with_memory_space_constraint(arg, pltpu.HBM)
        operands.append(arg)
    out_shape = []
    out_specs = []
    for shape, dtype, spec in outs:
        out_specs.append(HBM if spec == "H" else VMEM)
        spaced = {"R": pltpu.VMEM, "H": pltpu.HBM, "V": jax.ShapeDtypeStruct}[spec]
        out_shape.append(spaced(shape, dtype))
    fetched = len(held)

    def wrapped(*refs):
        refs = list(refs)
        if fetched:
            sems = refs.pop()
            targets = refs[-fetched:]
            refs = refs[:-fetched]
            sources = [number for number, spec in enumerate(specs) if spec in "FG"]
            fetch([(refs[n], target) for n, target in zip(sources, targets)], sems)
            for n, target in zip(sources, targets):
                refs[n] = target
        body((lax.axis_index("tm"), lax.axis_index("chan")), *refs)

    extra = held + ([pltpu.SemaphoreType.DMA((fetched,))] if fetched else [])
    return pl.pallas_call(
        wrapped,
        out_shape=tuple(out_shape),
        in_specs=in_specs,
        out_specs=tuple(out_specs),
        scratch_shapes=list(scratch) + extra,
        compiler_params=pltpu.CompilerParams(vmem_limit_bytes=VMEM_LIMIT),
        cost_estimate=pl.CostEstimate(
            flops=int(micros * 1.1e9), bytes_accessed=0, transcendentals=0
        ),
    )(*operands)


def fetch(pairs, sems):
    copies = [
        pltpu.make_async_copy(source, target, sems.at[number])
        for number, (source, target) in enumerate(pairs)
    ]
    for copy in copies:
        copy.start()
    for copy in copies:
        copy.wait()


def unit(values):
    th = jnp.tanh(0.5 * values)
    base = 0.6 + 0.4 * th
    return values * base, base + 0.2 * values * (1.0 - th * th)


def unit_act(values):
    return values * (0.6 + 0.4 * jnp.tanh(0.5 * values))


def dot(left, right):
    return lax.dot_general(left, right, (((1,), (0,)), ((), ())), preferred_element_type=F32)


def dot_rt(left, right):
    return lax.dot_general(left, right, (((1,), (1,)), ((), ())), preferred_element_type=F32)


def eye_mask(count):
    rows = lax.broadcasted_iota(jnp.int32, (count, count), 0)
    cols = lax.broadcasted_iota(jnp.int32, (count, count), 1)
    return rows == cols


def to_col(row, eye):
    return jnp.sum(jnp.where(eye, row, 0.0), axis=1, keepdims=True)


def to_row(col, eye):
    return jnp.sum(jnp.where(eye, col, 0.0), axis=0, keepdims=True)


def at(start, size, step):
    return pl.ds(pl.multiple_of(start, step), size)


def edge_kernel(idx, spectrogram, cot, sil, ahead, behind, front, back, sound, mask, sems):
    rows = spectrogram.shape[0]
    frames, count = spectrogram.shape[1], cot.shape[1]
    low, high = pl.ds(0, HALO), pl.ds(count - HALO, HALO)
    fetch(
        [
            (spectrogram.at[:, frames - LANES :], front),
            (spectrogram.at[:, :LANES], back),
            (cot.at[:, high], sound.at[0]),
            (cot.at[:, low], sound.at[1]),
            (sil.at[:, high], mask.at[0]),
            (sil.at[:, low], mask.at[1]),
        ],
        sems,
    )
    ahead[0:rows, :] = front[...]
    behind[0:rows, :] = back[...]
    ahead[rows:, :] = (sound[0].astype(F32) * mask[0].astype(F32)).astype(BF)
    behind[rows:, :] = (sound[1].astype(F32) * mask[1].astype(F32)).astype(BF)


def square_kernel(idx, up_v, up_sq):
    total = jnp.zeros((up_v.shape[1], up_v.shape[2]), F32)
    for k in range(up_v.shape[0]):
        rows = up_v[k]
        total = total + rows * rows
    up_sq[...] = jnp.sum(total, axis=0, keepdims=True)


def prep_kernel(
    idx, dil_v, dil_g, dil_b, mix_v, mix_g, out_b, skip_v, skip_g, packed, near, far, order,
    held, sem
):
    size = order.shape[0]
    source = lax.broadcasted_iota(jnp.int32, (size, size), 0)
    target = lax.broadcasted_iota(jnp.int32, (size, size), 1)
    hit = target == 8 * (source & (LANES - 1)) + (source >> 7)
    held[...] = jnp.where(hit, 1.0, 0.0).astype(BF)
    copy = pltpu.make_async_copy(held, order, sem)
    copy.start()
    local_out = dil_v.shape[2]
    eye = eye_mask(local_out)
    lane = lax.broadcasted_iota(jnp.int32, (local_out, TAIL), 1)
    width = dil_v.shape[3]
    for j in range(dil_v.shape[0]):
        rows = pl.ds(j * local_out, local_out)
        square = jnp.zeros((local_out, 1), F32)
        for k in range(3):
            v = dil_v[j, k]
            square = square + jnp.sum(v * v, axis=1, keepdims=True)
        norm = jnp.sqrt(square)
        gain = to_col(dil_g[j : j + 1, :], eye)
        for k in range(3):
            packed[rows, k * width : (k + 1) * width] = (gain * dil_v[j, k] / norm).astype(BF)
        for number, (vref, gref) in enumerate(((mix_v, mix_g), (skip_v, skip_g))):
            v = vref[j]
            norm = jnp.sqrt(jnp.sum(v * v, axis=1, keepdims=True))
            gain = to_col(gref[j : j + 1, :], eye)
            packed[rows, (3 + number) * width : (4 + number) * width] = (gain * v / norm).astype(BF)
        first = to_col(dil_b[j : j + 1, :], eye)
        second = to_col(out_b[j : j + 1, :], eye)
        high_one = first.astype(BF).astype(F32)
        high_two = second.astype(BF).astype(F32)
        tail = jnp.where(lane == 0, high_one, 0.0) + jnp.where(lane == 1, first - high_one, 0.0)
        tail = tail + jnp.where(lane == 2, high_two, 0.0)
        tail = tail + jnp.where(lane == 3, second - high_two, 0.0)
        packed[rows, 5 * width : 5 * width + TAIL] = tail.astype(BF)
    half = near.shape[0]
    for number, target in enumerate((near, far)):
        target[...] = packed[at(((idx[0] ^ number) & 1) * half, half, 16), :]
    copy.wait()


def cut_kernel(pieces, idx, cot, sil, low, high, *refs):
    outs, wide, sems = refs[:pieces], refs[pieces], refs[pieces + 1]
    count = cot.shape[1]
    own = count // pieces
    rows = cot.shape[0]
    wide[:, 0:HALO] = low[low.shape[0] - rows :, :]
    wide[:, HALO : HALO + count] = (cot[...].astype(F32) * sil[...].astype(F32)).astype(BF)
    wide[:, HALO + count :] = high[high.shape[0] - rows :, :]
    fetch(
        [
            (wide.at[:, at((idx[1] ^ s) * own, own + 2 * HALO, LANES)], outs[s])
            for s in range(pieces)
        ],
        sems,
    )


def weight_kernel(pieces, blocks, idx, *refs):
    *parts, plain, dil_t, point_t, sems = refs
    rows = parts[0].shape[0] // blocks
    part = rows // 2
    pairs = []
    for s in range(pieces):
        start = (idx[1] ^ s) * rows
        if s < 2:
            for j in range(blocks):
                source = parts[s].at[j * rows : (j + 1) * rows, :]
                pairs.append((source, plain.at[j, at(start, rows, 16), :]))
            continue
        for number in range(2):
            source = parts[2 + 2 * (s - 2) + number]
            first = blocks * ((idx[0] ^ number) & 1)
            for q in range(blocks):
                place = first + q
                target = plain.at[
                    lax.div(place, 2), at(start + lax.rem(place, 2) * part, part, 16), :
                ]
                pairs.append((source.at[q * part : (q + 1) * part, :], target))
    fetch(pairs, sems)
    width = plain.shape[1]
    for j in range(blocks):
        for k in range(5):
            turned = jnp.transpose(plain[j, :, k * width : (k + 1) * width])
            if k < 3:
                dil_t[j, :, k * width : (k + 1) * width] = turned
            else:
                point_t[j, :, (k - 3) * width : (k - 2) * width] = turned


def up_kernel(pieces, idx, *refs):
    mains, sides = refs[:pieces], refs[pieces : 2 * pieces]
    up_v, up_sq, up_g, up_b, frame_id, order = refs[2 * pieces : 2 * pieces + 6]
    outs = refs[2 * pieces + 6 : 3 * pieces + 6]
    act_hbm, up_hbm = refs[3 * pieces + 6 : 3 * pieces + 8]
    raw, stacked, phases, wide, act_out, up_w, sems, out_sems = refs[3 * pieces + 8 :]
    rows, frames = mains[0].shape
    local_out = up_v.shape[1]
    copies = []
    for s in range(pieces):
        here = at((idx[1] ^ s) * rows, rows, 16)
        for source, target in (
            (sides[s].at[:, 0:LANES], raw.at[here, 0:LANES]),
            (mains[s], raw.at[here, LANES : LANES + frames]),
            (sides[s].at[:, LANES:], raw.at[here, LANES + frames :]),
        ):
            copies.append(pltpu.make_async_copy(source, target, sems.at[len(copies)]))
            copies[-1].start()
    norm = jnp.sqrt(up_sq[...])
    for k in range(up_v.shape[0]):
        up_w[k * local_out : (k + 1) * local_out, :] = (up_g[...] * up_v[k] / norm).astype(BF)
    kept = [
        pltpu.make_async_copy(up_w, up_hbm, out_sems.at[pieces]),
        pltpu.make_async_copy(act_out, act_hbm, out_sems.at[pieces + 1]),
    ]
    kept[0].start()
    for copy in copies:
        copy.wait()
    total = frames + 2 * LANES
    count = stacked.shape[1]
    channels = raw.shape[0]
    shift = total - (LANES - HALO // 8)
    ids = pltpu.roll(jnp.broadcast_to(frame_id[...], (8, total)), shift, axis=1)
    before = pltpu.roll(ids, 1, axis=1)
    after = pltpu.roll(ids, total - 1, axis=1)
    left = jnp.where(before == ids, 1.0, 0.0)[0:1, :].astype(BF)
    right = jnp.where(after == ids, 1.0, 0.0)[0:1, :].astype(BF)
    step = channels
    for r0 in range(0, channels, step):
        part = pl.ds(r0, step)
        acted = unit_act(raw[part, :].astype(F32)).astype(BF)
        act_out[part, :] = acted[:, LANES : LANES + frames]
        moved = pltpu.roll(acted, shift, axis=1)
        one = pltpu.roll(moved, 1, axis=1) * left
        two = pltpu.roll(moved, total - 1, axis=1) * right
        stacked[part, :] = moved[:, 0:count]
        stacked[pl.ds(channels + r0, step), :] = one[:, 0:count]
        stacked[pl.ds(2 * channels + r0, step), :] = two[:, 0:count]
    kept[1].start()
    eye = eye_mask(local_out)
    bias = to_col(up_b[...], eye)
    bias4 = jnp.concatenate([bias] * 4, axis=0)
    quarter = 4 * local_out
    for c0 in range(0, count, 3 * LANES):
        cols = pl.ds(c0, 3 * LANES)
        center = stacked[0:channels, cols]
        low = dot(up_w[quarter : 2 * quarter, :], center)
        low = low + dot(up_w[3 * quarter : 4 * quarter, :], stacked[channels : 2 * channels, cols])
        high = dot(up_w[2 * quarter : 3 * quarter, :], center)
        high = high + dot(up_w[0:quarter, :], stacked[2 * channels : 3 * channels, cols])
        low = (low + bias4).astype(BF)
        high = (high + bias4).astype(BF)
        for b in range(3):
            block = c0 // LANES + b
            if block * local_out >= phases.shape[0]:
                continue
            for r in range(8):
                source = (low, high)[r // 4]
                phases[block * local_out : (block + 1) * local_out, r * LANES : (r + 1) * LANES] = (
                    source[
                        (r % 4) * local_out : (r % 4 + 1) * local_out,
                        b * LANES : (b + 1) * LANES,
                    ]
                )
    turned = dot(phases[...], order[...]).astype(BF)
    for block in range(count // LANES):
        wide[:, block * 1024 : (block + 1) * 1024] = turned[
            block * local_out : (block + 1) * local_out, :
        ]
    own = 8 * frames // pieces
    fetch(
        [
            (wide.at[:, at((idx[1] ^ s) * own, own + 2 * HALO, LANES)], outs[s])
            for s in range(pieces)
        ],
        out_sems,
    )
    for copy in kept:
        copy.wait()


def sample_masks(sample_id, distance):
    width = sample_id.shape[1]
    ids = jnp.broadcast_to(sample_id[...], (8, width))
    back = pltpu.roll(ids, distance, axis=1)
    ahead = pltpu.roll(ids, width - distance, axis=1)
    return (
        jnp.where(back == ids, 1.0, 0.0)[0:1, :].astype(BF),
        jnp.where(ahead == ids, 1.0, 0.0)[0:1, :].astype(BF),
    )


def forward_kernel(pieces, blocks, idx, *refs):
    parts = refs[:pieces]
    plain, sample_id, silence = refs[pieces : pieces + 3]
    outs = refs[pieces + 3 : 2 * pieces + 3]
    kept = refs[2 * pieces + 3 : 2 * pieces + 8]
    hidden, taps, pair, final, sems, out_sems = refs[2 * pieces + 8 :]
    keep_h, keep_u, keep_m, keep_sh, keep_sc = kept
    rows, width = parts[0].shape
    channels = pieces * rows
    fetch(
        [(parts[s], hidden.at[at((idx[1] ^ s) * rows, rows, 16), :]) for s in range(pieces)], sems
    )
    for j in range(blocks):
        distance = 3**j
        tail = plain[j, :, 5 * channels : 5 * channels + TAIL].astype(F32)
        dil_b = tail[:, 0:1] + tail[:, 1:2]
        out_b = tail[:, 2:3] + tail[:, 3:4]

        low = hidden[...]
        keep_h[j] = low
        pair[channels : 2 * channels, :] = low
        acted, slope = unit(low.astype(F32))
        acted = acted.astype(BF)
        taps[channels : 2 * channels, :] = acted
        keep_u[j] = acted
        keep_sh[j] = slope.astype(BF)
        back, ahead = sample_masks(sample_id, distance)
        center = taps[channels : 2 * channels, :]
        taps[0:channels, :] = pltpu.roll(center, distance, axis=1) * back
        taps[2 * channels : 3 * channels, :] = pltpu.roll(center, width - distance, axis=1) * ahead

        inner = dot(plain[j, :, 0 : 3 * channels], taps[...]) + dil_b
        acted, slope = unit(inner)
        acted = acted.astype(BF)
        pair[0:channels, :] = acted
        keep_m[j] = acted
        keep_sc[j] = slope.astype(BF)
        after = dot(plain[j, :, 3 * channels : 5 * channels], pair[...]) + out_b
        if j < blocks - 1:
            hidden[...] = after.astype(BF)
        else:
            final[...] = after
    own = width - 2 * HALO
    voiced = silence[:, at(idx[1] * own, own, LANES)].astype(F32)
    hidden[:, 0:own] = (final[:, HALO : HALO + own] * voiced).astype(BF)
    fetch(
        [
            (hidden.at[at((idx[1] ^ s) * rows, rows, 16), 0:own], outs[s])
            for s in range(pieces)
        ],
        out_sems,
    )


def spread_taps(j, center, sample_id, taps):
    channels, width = center.shape
    distance = 3**j
    back, ahead = sample_masks(sample_id, distance)
    taps[channels : 2 * channels, :] = center
    taps[0:channels, :] = pltpu.roll(center, width - distance, axis=1) * ahead
    taps[2 * channels : 3 * channels, :] = pltpu.roll(center, distance, axis=1) * back


def edge_start(pieces, peer):
    return jnp.where(peer < pieces // 2, 0, HALO)


def backward_kernel(pieces, idx, *refs):
    parts = refs[:pieces]
    dil_t, point_t, sample_id, keep_sh, keep_sc = refs[pieces : pieces + 5]
    outs = refs[pieces + 5 : 2 * pieces + 5]
    errs, inners, taps, low, sems, out_sems = refs[2 * pieces + 5 :]
    rows = parts[0].shape[0]
    blocks, channels, width = errs.shape
    last = blocks - 1
    fetch(
        [(parts[s], errs.at[last, at((idx[1] ^ s) * rows, rows, 16), :]) for s in range(pieces)],
        sems,
    )
    for j in reversed(range(blocks)):
        err = errs[j]
        inner = dot(point_t[j, :, 0:channels], err) * keep_sc[j].astype(F32)
        inner = inner.astype(BF)
        inners[j] = inner
        spread_taps(j, inner, sample_id, taps)
        spread = dot(dil_t[j], taps[...]) * keep_sh[j].astype(F32)
        after = (spread + dot(point_t[j, :, channels : 2 * channels], err)).astype(BF)
        if j > 0:
            errs[j - 1] = after
        else:
            low[...] = after
    lanes = at(edge_start(pieces, idx[1]), width - HALO, LANES)
    fetch(
        [(low.at[at((idx[1] ^ s) * rows, rows, 16), lanes], outs[s]) for s in range(pieces)],
        out_sems,
    )


def grad_kernel(pieces, order, idx, errs, inners, sample_id, keep_h, keep_u, keep_m, *refs):
    keep, send, taps, mats, sems = refs
    blocks, channels, width = errs.shape
    inside = pl.ds(HALO, width - 2 * HALO)
    rows = channels // pieces
    lane = lax.broadcasted_iota(jnp.int32, (channels, channels), 1)
    tail = jnp.zeros((channels, channels), F32)
    size = mats.shape[0] * rows
    copies = []

    def ship(m):
        for position, s in enumerate(order):
            target = (keep, send)[position // (pieces // 2)]
            start = position % (pieces // 2) * size + m * rows
            copies.append(
                pltpu.make_async_copy(
                    mats.at[m, at((idx[1] ^ s) * rows, rows, 16), :],
                    target.at[start : start + rows, :],
                    sems.at[len(copies)],
                )
            )
            copies[-1].start()

    for j in range(blocks):
        spread_taps(j, inners[j], sample_id, taps)
        err = errs[j, :, inside]
        mats[5 * j + 3] = dot_rt(err, keep_m[j, :, inside]).astype(BF)
        ship(5 * j + 3)
        mats[5 * j + 4] = dot_rt(err, keep_h[j, :, inside]).astype(BF)
        ship(5 * j + 4)
        for k in range(3):
            mats[5 * j + k] = dot_rt(
                taps[k * channels : (k + 1) * channels, inside], keep_u[j, :, inside]
            ).astype(BF)
            ship(5 * j + k)
        dil_sum = jnp.sum(inners[j, :, inside].astype(F32), axis=1, keepdims=True)
        out_sum = jnp.sum(err.astype(F32), axis=1, keepdims=True)
        tail = tail + jnp.where(lane == 2 * j, dil_sum, 0.0)
        tail = tail + jnp.where(lane == 2 * j + 1, out_sum, 0.0)
    mats[5 * blocks] = tail.astype(BF)
    ship(5 * blocks)
    for copy in copies:
        copy.wait()


def halve_kernel(idx, keep, got, next_keep, next_send):
    half = next_keep.shape[0]
    total = keep[...].astype(F32) + got[...].astype(F32)
    next_keep[...] = total[:half].astype(BF)
    next_send[...] = total[half:].astype(BF)


def up_back_kernel(pieces, peers, orders, idx, *refs):
    parts = refs[:pieces]
    up_v, acted, frame_id, order = refs[pieces : pieces + 4]
    cols_grad, *streams = refs[pieces + 4 : pieces + 9]
    wide, stacked, phases, low_grad, sems = refs[pieces + 9 :]
    rows = parts[0].shape[0]
    own = parts[0].shape[1] - HALO
    length = pieces * own
    frames = length // 8
    copies = []
    for s in range(pieces):
        peer = idx[1] ^ s
        target = wide.at[:, at(HALO + peer * own, own, LANES)]
        source = parts[s].at[:, at(HALO - edge_start(pieces, peer), own, LANES)]
        copies.append(pltpu.make_async_copy(source, target, sems.at[s]))
        copies[-1].start()
    wide[:, HALO + length :] = jnp.zeros((rows, wide.shape[1] - HALO - length), BF)
    for copy in copies:
        copy.wait()
    for s in range(pieces):
        peer = idx[1] ^ s

        @pl.when(peer == 0)
        def _():
            pltpu.sync_copy(parts[s].at[:, 0:HALO], wide.at[:, 0:HALO])

        @pl.when(peer == pieces - 1)
        def _():
            pltpu.sync_copy(
                parts[s].at[:, own:], wide.at[:, HALO + length : 2 * HALO + length]
            )

    total = wide.shape[1] // 8
    blocks = total // LANES
    for block in range(blocks):
        stacked[block * rows : (block + 1) * rows, :] = wide[:, block * 1024 : (block + 1) * 1024]
    turned = dot_rt(stacked[...], order[...]).astype(BF)
    for block in range(blocks):
        for r in range(8):
            phases[r * rows : (r + 1) * rows, block * LANES : (block + 1) * LANES] = turned[
                block * rows : (block + 1) * rows, r * LANES : (r + 1) * LANES
            ]
    ids = jnp.broadcast_to(frame_id[...], (8, frame_id.shape[1]))
    before = pltpu.roll(ids, 1, axis=1)
    after = pltpu.roll(ids, frame_id.shape[1] - 1, axis=1)
    inside = slice(LANES, LANES + frames)
    left = jnp.where(before == ids, 1.0, 0.0)[0:1, inside]
    right = jnp.where(after == ids, 1.0, 0.0)[0:1, inside]
    lead = HALO // 8
    eighth = 4 * rows
    sample_sum = jnp.zeros((rows, 1), F32)
    for part in range(2):
        base = phases[part * eighth : (part + 1) * eighth, :]
        center = pltpu.roll(base, total - lead, axis=1)[:, 0:frames]
        cols_grad[(4 + 4 * part) * rows : (8 + 4 * part) * rows, :] = center
        partial = jnp.sum(center.astype(F32), axis=1, keepdims=True)
        for r in range(4):
            sample_sum = sample_sum + partial[r * rows : (r + 1) * rows]
        if part == 1:
            moved = pltpu.roll(base, total - lead + 1, axis=1)[:, 0:frames]
            cols_grad[0:eighth, :] = (moved.astype(F32) * left).astype(BF)
        else:
            moved = pltpu.roll(base, total - lead - 1, axis=1)[:, 0:frames]
            cols_grad[12 * rows : 16 * rows, :] = (moved.astype(F32) * right).astype(BF)
    taps = up_v.shape[0]
    channels = up_v.shape[2]
    inner = jnp.zeros((rows, channels), F32)
    grad = dot_rt(cols_grad[...], acted[...])
    low_grad[...] = grad.astype(BF)
    for k in range(taps):
        inner = inner + grad[k * rows : (k + 1) * rows] * up_v[k]
    inner = jnp.sum(inner, axis=0, keepdims=True)
    bias = jnp.concatenate(
        [to_row(sample_sum, eye_mask(rows)), jnp.zeros((1, channels - rows), F32)], axis=1
    )
    side = channels // 2
    line = lax.broadcasted_iota(jnp.int32, (SUMS, side), 0)
    sums = jnp.zeros((SUMS, side), F32)
    for number, value in enumerate((inner[:, :side], inner[:, side:], bias[:, :side])):
        high = value.astype(BF).astype(F32)
        sums = sums + jnp.where(line == 2 * number, high, 0.0)
        sums = sums + jnp.where(line == 2 * number + 1, value - high, 0.0)
    half = peers // 2
    size = streams[2].shape[0] // half
    streams[0][half * size :, :] = sums.astype(BF)
    streams[1][half * size :, :] = sums.astype(BF)
    for number, sequence in enumerate(orders):
        lanes = pl.ds(number * side, side)
        for position, s in enumerate(sequence):
            target = streams[2 * number + position // half]
            start = position % half * size
            target[start : start + size, :] = low_grad[at((idx[0] ^ s) * size, size, 16), lanes]


def input_back_kernel(pieces, order, idx, up_w, cols_grad, keep, send, total, sems):
    total[...] = lax.dot_general(
        up_w[...], cols_grad[...], (((0,), (0,)), ((), ())), preferred_element_type=F32
    ).astype(BF)
    size = total.shape[0] // pieces
    pairs = []
    for position, s in enumerate(order):
        target = (keep, send)[position // (pieces // 2)]
        start = position % (pieces // 2) * size
        pairs.append(
            (total.at[at((idx[1] ^ s) * size, size, 16), :], target.at[start : start + size, :])
        )
    fetch(pairs, sems)


def join_kernel(order, idx, keep, got, term, other, next_keep, next_send, whole):
    rows = keep.shape[0] - SUMS
    half = rows // 2
    total = keep[...].astype(F32) + got[...].astype(F32)
    whole[...] = (term[...].astype(F32) + other[...].astype(F32)).astype(BF)
    sums = total[rows:].astype(BF)
    size = whole.shape[0] // len(order)
    count = len(order) // 2
    for number, target in enumerate((next_keep, next_send)):
        target[0:half, :] = total[number * half : (number + 1) * half].astype(BF)
        for position in range(count):
            s = order[number * count + position]
            start = half + position * size
            target[start : start + size, :] = whole[
                at(((idx[0] ^ s) >> 1) * size, size, 16), :
            ]
        target[half + count * size :, :] = sums


def step_kernel(rows, last, idx, keep, got, *outs):
    total = keep[...].astype(F32) + got[...].astype(F32)
    grads = total.shape[0] - rows - SUMS
    if last:
        outs[0][...] = total[:rows].astype(BF)
        outs[1][...] = total[rows : rows + grads].astype(BF)
        outs[2][...] = total[rows + grads :]
        return
    for number, target in enumerate(outs):
        half, part = rows // 2, grads // 2
        target[0:half, :] = total[number * half : (number + 1) * half].astype(BF)
        start = rows + number * part
        target[half : half + part, :] = total[start : start + part].astype(BF)
        target[half + part :, :] = total[rows + grads :].astype(BF)


def meet_kernel(idx, keep, got, grads, out):
    rows = keep.shape[0]
    out[0:rows, :] = (keep[...].astype(F32) + got[...].astype(F32)).astype(BF)
    out[rows:, :] = grads[...]


def double_kernel(rows, add, idx, own, got, out):
    grads = own.shape[0] - rows
    out[0:rows, :] = own[0:rows, :]
    out[rows : 2 * rows, :] = got[0:rows, :]
    if add:
        out[2 * rows :, :] = (own[rows:, :].astype(F32) + got[rows:, :].astype(F32)).astype(BF)
    else:
        out[2 * rows : 2 * rows + grads, :] = own[rows:, :]
        out[2 * rows + grads :, :] = got[rows:, :]


def final_kernel(orders, grad_order, offset, idx, *refs):
    streams = refs[:4]
    up_v, up_sq, up_g, inner_sum, dil_v, dil_g, mix_v, mix_g, skip_v, skip_g = refs[4:14]
    up_v_grad, up_g_grad, *outs = refs[14:24]
    whole, blocks_whole, staged, *block_staged, in_sems, grad_sems, out_sems = refs[24:]
    half = len(orders[0]) // 2
    size = whole.shape[0] // (2 * half)
    side = whole.shape[1] // 2
    copies = []
    for number, sequence in enumerate(orders):
        for position, s in enumerate(sequence):
            source = streams[2 * number + position // half]
            start = position % half * size
            target = whole.at[
                at((idx[0] ^ s) * size, size, 16), number * side : (number + 1) * side
            ]
            copies.append(
                pltpu.make_async_copy(
                    source.at[start : start + size, :], target, in_sems.at[len(copies)]
                )
            )
            copies[-1].start()
    grad_half = len(grad_order) // 2
    size = blocks_whole.shape[0] // len(grad_order)
    grads = []
    for position, s in enumerate(grad_order):
        start = offset + position % grad_half * size
        grads.append(
            pltpu.make_async_copy(
                streams[2 + position // grad_half].at[start : start + size, :],
                blocks_whole.at[at(((idx[0] ^ s) >> 1) * size, size, 16), :],
                grad_sems.at[len(grads)],
            )
        )
        grads[-1].start()
    for copy in copies:
        copy.wait()
    sent = []

    def ship(source, target):
        sent.append(pltpu.make_async_copy(source, target, out_sems.at[len(sent)]))
        sent[-1].start()

    norm = jnp.sqrt(up_sq[...])
    inner = inner_sum[...]
    scale = up_g[...] / norm
    pull = up_g[...] * inner / (norm * norm * norm)
    rows = up_v.shape[1]
    for k in range(up_v.shape[0]):
        grad = whole[k * rows : (k + 1) * rows, :].astype(F32)
        staged[k] = scale * grad - pull * up_v[k]
        ship(staged.at[k], up_v_grad.at[k])
    up_g_grad[...] = inner / norm
    for copy in grads:
        copy.wait()
    dil_v_hbm, dil_g_out, dil_b_out, mix_v_hbm, mix_g_out, out_b_out, skip_v_hbm, skip_g_out = outs
    dil_v_out, mix_v_out, skip_v_out = block_staged
    eye = eye_mask(rows)
    blocks = dil_v.shape[0]
    tail = blocks_whole[5 * blocks * rows :, :].astype(F32)
    for j in range(blocks):

        def mat(m):
            start = (5 * j + m) * rows
            return blocks_whole[start : start + rows, :].astype(F32)

        square = jnp.zeros((rows, 1), F32)
        inner = jnp.zeros((rows, 1), F32)
        for k in range(3):
            v = dil_v[j, k]
            square = square + jnp.sum(v * v, axis=1, keepdims=True)
            inner = inner + jnp.sum(v * mat(k), axis=1, keepdims=True)
        norm = jnp.sqrt(square)
        gain = to_col(dil_g[j : j + 1, :], eye)
        for k in range(3):
            dil_v_out[j, k] = gain / norm * mat(k) - gain * inner / (norm**3) * dil_v[j, k]
        ship(dil_v_out.at[j], dil_v_hbm.at[j])
        dil_g_out[j : j + 1, :] = to_row(inner / norm, eye)
        for number, (vref, gref, v_out, v_hbm, g_out) in enumerate(
            (
                (mix_v, mix_g, mix_v_out, mix_v_hbm, mix_g_out),
                (skip_v, skip_g, skip_v_out, skip_v_hbm, skip_g_out),
            )
        ):
            v = vref[j]
            grad = mat(3 + number)
            norm = jnp.sqrt(jnp.sum(v * v, axis=1, keepdims=True))
            inner = jnp.sum(v * grad, axis=1, keepdims=True)
            gain = to_col(gref[j : j + 1, :], eye)
            v_out[j] = gain / norm * grad - gain * inner / (norm**3) * v
            ship(v_out.at[j], v_hbm.at[j])
            g_out[j : j + 1, :] = to_row(inner / norm, eye)
        dil_b_out[j : j + 1, :] = to_row(tail[:, 2 * j : 2 * j + 1], eye)
        out_b_out[j : j + 1, :] = to_row(tail[:, 2 * j + 1 : 2 * j + 2], eye)
    for copy in sent:
        copy.wait()


def place_kernel(pieces, idx, *refs):
    parts, out, sems = refs[:pieces], refs[pieces], refs[pieces + 1]
    own = parts[0].shape[1]
    fetch(
        [(parts[s], out.at[:, at((idx[1] ^ s) * own, own, LANES)]) for s in range(pieces)], sems
    )


def input_kernel(idx, *refs):
    *terms, spectrogram, out = refs
    total = terms[0][...].astype(F32)
    for term in terms[1:]:
        total = total + term[...].astype(F32)
    out[...] = (total * unit(spectrogram[...].astype(F32))[1]).astype(BF)


def local(
    spectrogram_input,
    upsample_direction,
    upsample_magnitude,
    upsample_bias,
    dilated_direction,
    dilated_magnitude,
    dilated_bias,
    pointwise_direction,
    pointwise_magnitude,
    block_output_bias,
    shortcut_direction,
    shortcut_magnitude,
    cotangent,
    silence,
    segments,
):
    pieces, peers = lax.axis_size("chan"), lax.axis_size("tm")
    chan, tm = lax.axis_index("chan"), lax.axis_index("tm")
    in_rows, frames = spectrogram_input.shape
    taps, rows, in_channels = upsample_direction.shape
    blocks = dilated_direction.shape[0]
    channels = dilated_direction.shape[3]
    length = 8 * frames
    own = length // pieces
    width = own + 2 * HALO
    packed_width = 5 * channels + TAIL
    forward = [(k, k + 1) for k in range(peers - 1)]
    backward = [(k + 1, k) for k in range(peers - 1)]
    dma = pltpu.SemaphoreType.DMA
    lead = HALO // 8
    tie = lax.optimization_barrier

    silence_row = silence.reshape(1, length)
    up_g = upsample_magnitude.reshape(1, in_channels)
    edge_rows = in_rows + rows
    ahead, behind = kernel_call(
        edge_kernel,
        [((edge_rows, LANES), BF, "V")] * 2,
        [spectrogram_input, cotangent, silence_row],
        "HHH",
        scratch=[
            pltpu.VMEM((in_rows, LANES), BF),
            pltpu.VMEM((in_rows, LANES), BF),
            pltpu.VMEM((2, rows, HALO), BF),
            pltpu.VMEM((2, 1, HALO), jnp.int32),
            dma((6,)),
        ],
    )
    low_edge = lax.ppermute(ahead, "tm", forward)
    high_edge = lax.ppermute(behind, "tm", backward)
    all_mains = gather_chan(spectrogram_input)
    up_v_late, ahead = tie((upsample_direction, ahead))
    (up_sq,) = kernel_call(
        square_kernel, [((1, in_channels), F32, "V")], [up_v_late], "F", micros=2
    )
    block_args = [
        dilated_direction,
        dilated_magnitude,
        dilated_bias,
        pointwise_direction,
        pointwise_magnitude,
        block_output_bias,
        shortcut_direction,
        shortcut_magnitude,
    ]
    sides = jnp.concatenate([low_edge[:in_rows], high_edge[:in_rows]], axis=1)
    block_args, sides = tie((block_args, sides))
    packed_half = ((blocks * rows // 2, packed_width), BF, "V")
    packed, near, far, order = kernel_call(
        prep_kernel,
        [((blocks * rows, packed_width), BF, "V"), packed_half, packed_half]
        + [((8 * LANES, 8 * LANES), BF, "H")],
        block_args,
        "FFFFFFFF",
        scratch=[pltpu.VMEM((8 * LANES, 8 * LANES), BF), dma],
        micros=3,
    )
    all_sides = gather_chan(sides)
    for bit in bits_of(pieces):
        up_sq = up_sq + swap(up_sq, "chan", bit)
    padded_ids = jnp.pad(segments.astype(F32), LANES, constant_values=-1.0)
    frame_id = lax.dynamic_slice_in_dim(padded_ids, tm * frames, frames + 2 * LANES)
    sample_id = jnp.repeat(
        lax.dynamic_slice_in_dim(
            padded_ids, LANES + tm * frames + chan * (own // 8) - lead, width // 8
        ),
        8,
    ).reshape(1, width)
    frame_id = frame_id.reshape(1, frames + 2 * LANES)
    near, low_edge = tie((near, low_edge))
    cut = kernel_call(
        functools.partial(cut_kernel, pieces),
        [((rows, width), BF, "H")] * pieces,
        [cotangent, silence_row, low_edge, high_edge],
        "FFGG",
        scratch=[pltpu.VMEM((rows, length + 2 * HALO), BF), dma((pieces,))],
        micros=2,
    )
    top = pieces // 2
    near, cut, all_sides[top], up_sq = tie((near, list(cut), all_sides[top], up_sq))

    count = -(-(frames + 2 * lead) // LANES) * LANES
    count = -(-count // (3 * LANES)) * 3 * LANES
    up_outs = kernel_call(
        functools.partial(up_kernel, pieces),
        [((rows, width), BF, "H")] * pieces
        + [((in_channels, frames), BF, "H"), ((taps * rows, in_channels), BF, "H")],
        all_mains
        + all_sides
        + [upsample_direction, up_sq, up_g, upsample_bias.reshape(1, rows), frame_id, order],
        "A" * (2 * pieces) + "FGFFGF",
        scratch=[
            pltpu.VMEM((in_channels, frames + 2 * LANES), BF),
            pltpu.VMEM((3 * in_channels, count), BF),
            pltpu.VMEM((count // LANES * rows, 8 * LANES), BF),
            pltpu.VMEM((rows, 8 * count), BF),
            pltpu.VMEM((in_channels, frames), BF),
            pltpu.VMEM((taps * rows, in_channels), BF),
            dma((3 * pieces,)),
            dma((pieces + 2,)),
        ],
        micros=6,
    )
    acted, up_w = up_outs[pieces:]
    chan_bits = bits_of(pieces)
    held_near = {0: near}
    for bit in reversed(chan_bits[1:]):
        for slot in list(held_near):
            held_near[slot ^ bit] = swap(held_near[slot], "chan", bit)
    all_packed = [packed, swap(packed, "chan", 1)]
    for slot in range(2, pieces, 2):
        two = [held_near[slot], swap(held_near[slot], "tm", 1)]
        all_packed += two + [swap(value, "chan", 1) for value in two]
    all_hidden = exchange_chan(list(up_outs[:pieces]))
    all_packed, all_hidden[top] = tie((all_packed, all_hidden[top]))

    plain, dil_t, point_t = kernel_call(
        functools.partial(weight_kernel, pieces, blocks),
        [
            ((blocks, channels, packed_width), BF, "R"),
            ((blocks, channels, 3 * channels), BF, "R"),
            ((blocks, channels, 2 * channels), BF, "R"),
        ],
        all_packed,
        "A" * len(all_packed),
        scratch=[dma((2 * blocks * pieces,))],
        micros=3,
    )
    cut, all_hidden = tie((cut, all_hidden))
    all_err = exchange_chan(cut)

    kept_shape = ((blocks, channels, width), BF, "R")
    forward_outs = kernel_call(
        functools.partial(forward_kernel, pieces, blocks),
        [((rows, own), BF, "H")] * pieces + [kept_shape] * 5,
        all_hidden + [plain, sample_id, silence_row],
        "A" * pieces + "RGF",
        scratch=[
            pltpu.VMEM((channels, width), BF),
            pltpu.VMEM((3 * channels, width), BF),
            pltpu.VMEM((2 * channels, width), BF),
            pltpu.VMEM((channels, width), F32),
            dma((pieces,)),
            dma((pieces,)),
        ],
        micros=10,
    )
    keep_h, keep_u, keep_m, keep_sh, keep_sc = forward_outs[pieces:]
    activation_parts = list(forward_outs[:pieces])

    backward_outs = kernel_call(
        functools.partial(backward_kernel, pieces),
        [((rows, width - HALO), BF, "H")] * pieces + [kept_shape] * 2,
        all_err + [dil_t, point_t, sample_id, keep_sh, keep_sc],
        "A" * pieces + "RRGRR",
        scratch=[
            pltpu.VMEM((3 * channels, width), BF),
            pltpu.VMEM((channels, width), BF),
            dma((pieces,)),
            dma((pieces,)),
        ],
        micros=10,
    )
    errs, inners = backward_outs[pieces:]
    all_low = exchange_chan(list(backward_outs[:pieces]))
    errs, all_low[top] = tie((errs, all_low[top]))

    chan_order = order_of(chan_bits)
    mats = 5 * blocks + 1
    share = pieces // 2 * mats * rows
    keep, send = kernel_call(
        functools.partial(grad_kernel, pieces, chan_order),
        [((share, channels), BF, "H")] * 2,
        [errs, inners, sample_id, keep_h, keep_u, keep_m],
        "RRGRRR",
        scratch=[
            pltpu.VMEM((3 * channels, width), BF),
            pltpu.VMEM((mats, channels, channels), BF),
            dma((mats * pieces,)),
        ],
        micros=8,
    )

    def scatter_chan(keep, send):
        for bit in chan_bits[:-1]:
            got = swap(send, "chan", bit)
            next_shape = ((keep.shape[0] // 2, keep.shape[1]), BF, "V")
            keep, send = kernel_call(halve_kernel, [next_shape] * 2, [keep, got], "GG")
        return keep, swap(send, "chan", chan_bits[-1])

    block_terms = scatter_chan(keep, send)

    tm_bits = bits_of(peers)
    turned_bits = tm_bits[1:] + tm_bits[:1]
    orders = (order_of(tm_bits), order_of(turned_bits))
    half = peers // 2
    total_rows = taps * rows
    size = total_rows // peers
    side = in_channels // 2
    cols_grad, keep_one, send_one, keep_two, send_two = kernel_call(
        functools.partial(up_back_kernel, pieces, peers, orders),
        [((total_rows, frames), BF, "R")]
        + [((half * size + SUMS, side), BF, "V")] * 2
        + [((half * size, side), BF, "V")] * 2,
        all_low + [upsample_direction, acted, frame_id, order],
        "A" * pieces + "FFGF",
        scratch=[
            pltpu.VMEM((rows, 8 * count), BF),
            pltpu.VMEM((count // LANES * rows, 8 * LANES), BF),
            pltpu.VMEM((8 * rows, count), BF),
            pltpu.VMEM((total_rows, in_channels), BF),
            dma((pieces,)),
        ],
        micros=5,
    )

    steps = len(tm_bits)
    grad_order = order_of(tm_bits[1:])
    block_rows = mats * rows
    one_rows, two_rows = half * size, half * size
    grads = None
    for step in range(steps):
        got_one = swap(send_one, "tm", tm_bits[step])
        got_two = swap(send_two, "tm", turned_bits[step])
        got_one, got_two = tie((got_one, got_two))
        last = step == steps - 1
        if step == 0:
            next_rows = one_rows // 2 + block_rows // 2 + SUMS
            keep_one, send_one = kernel_call(
                functools.partial(join_kernel, grad_order),
                [((next_rows, side), BF, "V")] * 2,
                [keep_one, got_one, *block_terms],
                "GGGG",
                scratch=[pltpu.VMEM((block_rows, side), BF)],
            )
            one_rows, block_rows = one_rows // 2, block_rows // 2
        elif not last:
            next_rows = one_rows // 2 + block_rows // 2 + SUMS
            keep_one, send_one = kernel_call(
                functools.partial(step_kernel, one_rows, False),
                [((next_rows, side), BF, "V")] * 2,
                [keep_one, got_one],
                "GG",
            )
            one_rows, block_rows = one_rows // 2, block_rows // 2
        else:
            own_one, grads, sums = kernel_call(
                functools.partial(step_kernel, one_rows, True),
                [((one_rows, side), BF, "V"), ((block_rows, side), BF, "V")]
                + [((SUMS, side), F32, "V")],
                [keep_one, got_one],
                "GG",
            )
        if not last:
            two_rows = two_rows // 2
            keep_two, send_two = kernel_call(
                halve_kernel, [((two_rows, side), BF, "V")] * 2, [keep_two, got_two], "GG"
            )
        else:
            (own_two,) = kernel_call(
                meet_kernel,
                [((two_rows + block_rows, side), BF, "V")],
                [keep_two, got_two, grads],
                "GGG",
            )
    for step in reversed(range(steps)):
        got_one = swap(own_one, "tm", tm_bits[step])
        got_two = swap(own_two, "tm", turned_bits[step])
        got_one, got_two = tie((got_one, got_two))
        if step > 0:
            own_one = jnp.concatenate([own_one, got_one], axis=0)
            add = step == steps - 1
            grown = 2 * two_rows + (block_rows if add else 2 * block_rows)
            (own_two,) = kernel_call(
                functools.partial(double_kernel, two_rows, add),
                [((grown, side), BF, "V")],
                [own_two, got_two],
                "GG",
            )
            two_rows = 2 * two_rows
            block_rows = block_rows if add else 2 * block_rows

    pair = sums[0:6:2] + sums[1:6:2]
    inner_sum = pair[0:2].reshape(1, in_channels)
    for bit in chan_bits:
        inner_sum = inner_sum + swap(inner_sum, "chan", bit)

    piece_rows = pieces // 2 * in_rows
    keep, send = kernel_call(
        functools.partial(input_back_kernel, pieces, chan_order),
        [((piece_rows, frames), BF, "H")] * 2,
        [up_w, cols_grad],
        "FR",
        scratch=[pltpu.VMEM((in_channels, frames), BF), dma((pieces,))],
        micros=3,
    )
    input_terms = scatter_chan(keep, send)
    (input_grad,) = kernel_call(
        input_kernel,
        [((in_rows, frames), BF, "V")],
        [*input_terms, spectrogram_input],
        "GGF",
    )
    activation_parts, input_terms = tie((activation_parts, input_terms))
    activation_parts = exchange_chan(activation_parts)
    (activation,) = kernel_call(
        functools.partial(place_kernel, pieces),
        [((rows, length), BF, "V")],
        activation_parts,
        "A" * pieces,
        scratch=[dma((pieces,))],
        micros=2,
    )

    final_outs = kernel_call(
        functools.partial(final_kernel, orders, grad_order, two_rows),
        [
            (upsample_direction.shape, F32, "H"),
            ((1, in_channels), F32, "V"),
            (dilated_direction.shape, F32, "H"),
            (dilated_magnitude.shape, F32, "V"),
            (dilated_bias.shape, F32, "V"),
            (pointwise_direction.shape, F32, "H"),
            (pointwise_magnitude.shape, F32, "V"),
            (block_output_bias.shape, F32, "V"),
            (shortcut_direction.shape, F32, "H"),
            (shortcut_magnitude.shape, F32, "V"),
        ],
        [
            own_one,
            got_one,
            own_two,
            got_two,
            upsample_direction,
            up_sq,
            up_g,
            inner_sum,
            dilated_direction,
            dilated_magnitude,
            pointwise_direction,
            pointwise_magnitude,
            shortcut_direction,
            shortcut_magnitude,
        ],
        "AAAAFGFGFFFFFF",
        scratch=[
            pltpu.VMEM((total_rows, in_channels), BF),
            pltpu.VMEM((mats * rows, channels), BF),
            pltpu.VMEM(upsample_direction.shape, F32),
            pltpu.VMEM(dilated_direction.shape, F32),
            pltpu.VMEM(pointwise_direction.shape, F32),
            pltpu.VMEM(shortcut_direction.shape, F32),
            dma((2 * peers,)),
            dma((half,)),
            dma((taps + 3 * blocks,)),
        ],
        micros=5,
    )
    up_v_grad, up_g_grad, dil_v_grad, dil_g_grad, dil_b_grad = final_outs[:5]
    mix_v_grad, mix_g_grad, out_b_grad, skip_v_grad, skip_g_grad = final_outs[5:]
    return (
        activation,
        input_grad,
        up_v_grad,
        up_g_grad.reshape(in_channels),
        pair[2, :rows],
        dil_v_grad,
        dil_g_grad,
        dil_b_grad,
        mix_v_grad,
        mix_g_grad,
        out_b_grad,
        skip_v_grad,
        skip_g_grad,
    )


def solution(mesh):
    placed = (
        P("chan", "tm"),
        P(None, "chan", None),
        P(),
        P("chan"),
        P(None, None, "chan", None),
        P(None, "chan"),
        P(None, "chan"),
        P(None, "chan", None),
        P(None, "chan"),
        P(None, "chan"),
        P(None, "chan", None),
        P(None, "chan"),
        P("chan", "tm"),
        P("tm"),
        P(),
    )
    return jax.shard_map(
        local,
        mesh=mesh,
        in_specs=placed,
        out_specs=(
            P("chan", "tm"),
            P("chan", "tm"),
            P(None, "chan", None),
            P(),
            P("chan"),
            P(None, None, "chan", None),
            P(None, "chan"),
            P(None, "chan"),
            P(None, "chan", None),
            P(None, "chan"),
            P(None, "chan"),
            P(None, "chan", None),
            P(None, "chan"),
        ),
        check_vma=False,
    )
```

```python
import functools

import jax
import jax.numpy as jnp
import numpy as np
from jax import lax
from jax.experimental import pallas as pl
from jax.experimental.pallas import tpu as pltpu
from jax.sharding import PartitionSpec as P

BF = jnp.bfloat16
F32 = jnp.float32
LANES = 128
HALO = 128
TAIL = 128
SUMS = 16
VMEM_LIMIT = 20 * 1024 * 1024


def swap(values, axis, bit):
    count = lax.axis_size(axis)
    return lax.ppermute(values, axis, [(k, k ^ bit) for k in range(count)])


def bits_of(count):
    bits = []
    bit = 1
    while bit < count:
        bits.append(bit)
        bit = 2 * bit
    return bits


def order_of(bits):
    order = [0]
    for bit in reversed(bits):
        order = order + [slot + bit for slot in order]
    return order


def gather_chan(own):
    held = {0: own}
    for bit in reversed(bits_of(lax.axis_size("chan"))):
        for slot in list(held):
            held[slot ^ bit] = swap(held[slot], "chan", bit)
    return [held[slot] for slot in range(len(held))]


def exchange_chan(pieces):
    return [pieces[0]] + [swap(pieces[s], "chan", s) for s in range(1, len(pieces))]


HBM = pl.BlockSpec(memory_space=pltpu.HBM)
ANY = pl.BlockSpec(memory_space=pl.ANY)
VMEM = pl.BlockSpec(memory_space=pltpu.VMEM)


def kernel_call(body, outs, args, specs, scratch=(), micros=1.0):
    held = []
    in_specs = []
    operands = []
    for arg, spec in zip(args, specs, strict=True):
        in_specs.append({"H": HBM, "F": HBM, "A": ANY, "G": ANY, "R": VMEM}[spec])
        if spec in "FG":
            held.append(pltpu.VMEM(arg.shape, arg.dtype))
        if spec == "R":
            arg = pltpu.with_memory_space_constraint(arg, pltpu.VMEM)
        if spec in "HF":
            arg = pltpu.with_memory_space_constraint(arg, pltpu.HBM)
        operands.append(arg)
    out_shape = []
    out_specs = []
    for shape, dtype, spec in outs:
        out_specs.append(HBM if spec == "H" else VMEM)
        spaced = {"R": pltpu.VMEM, "H": pltpu.HBM, "V": jax.ShapeDtypeStruct}[spec]
        out_shape.append(spaced(shape, dtype))
    fetched = len(held)

    def wrapped(*refs):
        refs = list(refs)
        if fetched:
            sems = refs.pop()
            targets = refs[-fetched:]
            refs = refs[:-fetched]
            sources = [number for number, spec in enumerate(specs) if spec in "FG"]
            fetch([(refs[n], target) for n, target in zip(sources, targets)], sems)
            for n, target in zip(sources, targets):
                refs[n] = target
        body((lax.axis_index("tm"), lax.axis_index("chan")), *refs)

    extra = held + ([pltpu.SemaphoreType.DMA((fetched,))] if fetched else [])
    return pl.pallas_call(
        wrapped,
        out_shape=tuple(out_shape),
        in_specs=in_specs,
        out_specs=tuple(out_specs),
        scratch_shapes=list(scratch) + extra,
        compiler_params=pltpu.CompilerParams(vmem_limit_bytes=VMEM_LIMIT),
        cost_estimate=pl.CostEstimate(
            flops=int(micros * 1.1e9), bytes_accessed=0, transcendentals=0
        ),
    )(*operands)


def fetch(pairs, sems):
    copies = [
        pltpu.make_async_copy(source, target, sems.at[number])
        for number, (source, target) in enumerate(pairs)
    ]
    for copy in copies:
        copy.start()
    for copy in copies:
        copy.wait()


def unit(values):
    th = jnp.tanh(0.5 * values)
    base = 0.6 + 0.4 * th
    return values * base, base + 0.2 * values * (1.0 - th * th)


def unit_act(values):
    return values * (0.6 + 0.4 * jnp.tanh(0.5 * values))


def dot(left, right):
    return lax.dot_general(left, right, (((1,), (0,)), ((), ())), preferred_element_type=F32)


def dot_rt(left, right):
    return lax.dot_general(left, right, (((1,), (1,)), ((), ())), preferred_element_type=F32)


def eye_mask(count):
    rows = lax.broadcasted_iota(jnp.int32, (count, count), 0)
    cols = lax.broadcasted_iota(jnp.int32, (count, count), 1)
    return rows == cols


def to_col(row, eye):
    return jnp.sum(jnp.where(eye, row, 0.0), axis=1, keepdims=True)


def to_row(col, eye):
    return jnp.sum(jnp.where(eye, col, 0.0), axis=0, keepdims=True)


def at(start, size, step):
    return pl.ds(pl.multiple_of(start, step), size)


def edge_kernel(idx, spectrogram, cot, sil, ahead, behind, front, back, sound, mask, sems):
    rows = spectrogram.shape[0]
    frames, count = spectrogram.shape[1], cot.shape[1]
    low, high = pl.ds(0, HALO), pl.ds(count - HALO, HALO)
    fetch(
        [
            (spectrogram.at[:, frames - LANES :], front),
            (spectrogram.at[:, :LANES], back),
            (cot.at[:, high], sound.at[0]),
            (cot.at[:, low], sound.at[1]),
            (sil.at[:, high], mask.at[0]),
            (sil.at[:, low], mask.at[1]),
        ],
        sems,
    )
    ahead[0:rows, :] = front[...]
    behind[0:rows, :] = back[...]
    ahead[rows:, :] = (sound[0].astype(F32) * mask[0].astype(F32)).astype(BF)
    behind[rows:, :] = (sound[1].astype(F32) * mask[1].astype(F32)).astype(BF)


def square_kernel(idx, up_v, up_sq):
    total = jnp.zeros((up_v.shape[1], up_v.shape[2]), F32)
    for k in range(up_v.shape[0]):
        rows = up_v[k]
        total = total + rows * rows
    up_sq[...] = jnp.sum(total, axis=0, keepdims=True)


def prep_kernel(
    idx, dil_v, dil_g, dil_b, mix_v, mix_g, out_b, skip_v, skip_g, packed, near, far
):
    local_out = dil_v.shape[2]
    eye = eye_mask(local_out)
    lane = lax.broadcasted_iota(jnp.int32, (local_out, TAIL), 1)
    width = dil_v.shape[3]
    for j in range(dil_v.shape[0]):
        rows = pl.ds(j * local_out, local_out)
        square = jnp.zeros((local_out, 1), F32)
        for k in range(3):
            v = dil_v[j, k]
            square = square + jnp.sum(v * v, axis=1, keepdims=True)
        norm = jnp.sqrt(square)
        scale = to_col(dil_g[j : j + 1, :], eye) / norm
        for k in range(3):
            packed[rows, k * width : (k + 1) * width] = (dil_v[j, k] * scale).astype(BF)
        for number, (vref, gref) in enumerate(((mix_v, mix_g), (skip_v, skip_g))):
            v = vref[j]
            norm = jnp.sqrt(jnp.sum(v * v, axis=1, keepdims=True))
            scale = to_col(gref[j : j + 1, :], eye) / norm
            packed[rows, (3 + number) * width : (4 + number) * width] = (v * scale).astype(BF)
        first = to_col(dil_b[j : j + 1, :], eye)
        second = to_col(out_b[j : j + 1, :], eye)
        high_one = first.astype(BF).astype(F32)
        high_two = second.astype(BF).astype(F32)
        tail = jnp.where(lane == 0, high_one, 0.0) + jnp.where(lane == 1, first - high_one, 0.0)
        tail = tail + jnp.where(lane == 2, high_two, 0.0)
        tail = tail + jnp.where(lane == 3, second - high_two, 0.0)
        packed[rows, 5 * width : 5 * width + TAIL] = tail.astype(BF)
    half = near.shape[0]
    for number, target in enumerate((near, far)):
        target[...] = packed[at(((idx[0] ^ number) & 1) * half, half, 16), :]


def cut_kernel(pieces, idx, cot, sil, low, high, *refs):
    outs, wide, sems = refs[:pieces], refs[pieces], refs[pieces + 1]
    count = cot.shape[1]
    own = count // pieces
    rows = cot.shape[0]
    wide[:, 0:HALO] = low[low.shape[0] - rows :, :]
    wide[:, HALO : HALO + count] = (cot[...].astype(F32) * sil[...].astype(F32)).astype(BF)
    wide[:, HALO + count :] = high[high.shape[0] - rows :, :]
    fetch(
        [
            (wide.at[:, at((idx[1] ^ s) * own, own + 2 * HALO, LANES)], outs[s])
            for s in range(pieces)
        ],
        sems,
    )


def weight_kernel(pieces, blocks, idx, *refs):
    *parts, plain, dil_t, point_t, sems = refs
    rows = parts[0].shape[0] // blocks
    part = rows // 2
    pairs = []
    for s in range(pieces):
        start = (idx[1] ^ s) * rows
        if s < 2:
            for j in range(blocks):
                source = parts[s].at[j * rows : (j + 1) * rows, :]
                pairs.append((source, plain.at[j, at(start, rows, 16), :]))
            continue
        for number in range(2):
            source = parts[2 + 2 * (s - 2) + number]
            first = blocks * ((idx[0] ^ number) & 1)
            for q in range(blocks):
                place = first + q
                target = plain.at[
                    lax.div(place, 2), at(start + lax.rem(place, 2) * part, part, 16), :
                ]
                pairs.append((source.at[q * part : (q + 1) * part, :], target))
    fetch(pairs, sems)
    width = plain.shape[1]
    unit_matrix = jnp.where(eye_mask(width), 1.0, 0.0).astype(BF)
    for j in range(blocks):
        for k in range(5):
            turned = dot_rt(unit_matrix, plain[j, :, k * width : (k + 1) * width]).astype(BF)
            if k < 3:
                dil_t[j, :, k * width : (k + 1) * width] = turned
            else:
                point_t[j, :, (k - 3) * width : (k - 2) * width] = turned


def up_kernel(pieces, idx, *refs):
    mains, sides = refs[:pieces], refs[pieces : 2 * pieces]
    up_v, up_sq, up_g, up_b, frame_id, order = refs[2 * pieces : 2 * pieces + 6]
    outs = refs[2 * pieces + 6 : 3 * pieces + 6]
    act_hbm, up_hbm = refs[3 * pieces + 6 : 3 * pieces + 8]
    raw, stacked, phases, wide, act_out, up_w, held_v, held_order, *sems = refs[3 * pieces + 8 :]
    sems, out_sems = sems
    rows, frames = mains[0].shape
    local_out = up_v.shape[1]
    copies = []
    for s in range(pieces):
        here = at((idx[1] ^ s) * rows, rows, 16)
        for source, target in (
            (sides[s].at[:, 0:LANES], raw.at[here, 0:LANES]),
            (mains[s], raw.at[here, LANES : LANES + frames]),
            (sides[s].at[:, LANES:], raw.at[here, LANES + frames :]),
        ):
            copies.append(pltpu.make_async_copy(source, target, sems.at[len(copies)]))
            copies[-1].start()
    early = [
        pltpu.make_async_copy(up_v, held_v, sems.at[len(copies)]),
        pltpu.make_async_copy(order, held_order, sems.at[len(copies) + 1]),
    ]
    for copy in early:
        copy.start()
    kept = [
        pltpu.make_async_copy(up_w, up_hbm, out_sems.at[pieces]),
        pltpu.make_async_copy(act_out, act_hbm, out_sems.at[pieces + 1]),
    ]
    for copy in copies:
        copy.wait()
    total = frames + 2 * LANES
    count = stacked.shape[1]
    channels = raw.shape[0]
    shift = total - (LANES - HALO // 8)
    ids = pltpu.roll(jnp.broadcast_to(frame_id[...], (8, total)), shift, axis=1)
    before = pltpu.roll(ids, 1, axis=1)
    after = pltpu.roll(ids, total - 1, axis=1)
    left = jnp.where(before == ids, 1.0, 0.0)[0:1, :].astype(BF)
    right = jnp.where(after == ids, 1.0, 0.0)[0:1, :].astype(BF)
    step = channels
    for r0 in range(0, channels, step):
        part = pl.ds(r0, step)
        acted = unit_act(raw[part, :].astype(F32)).astype(BF)
        act_out[part, :] = acted[:, LANES : LANES + frames]
        moved = pltpu.roll(acted, shift, axis=1)
        one = pltpu.roll(moved, 1, axis=1) * left
        two = pltpu.roll(moved, total - 1, axis=1) * right
        stacked[part, :] = moved[:, 0:count]
        stacked[pl.ds(channels + r0, step), :] = one[:, 0:count]
        stacked[pl.ds(2 * channels + r0, step), :] = two[:, 0:count]
    kept[1].start()
    early[0].wait()
    scale = up_g[...] / jnp.sqrt(up_sq[...])
    for k in range(up_v.shape[0]):
        up_w[k * local_out : (k + 1) * local_out, :] = (held_v[k] * scale).astype(BF)
    kept[0].start()
    eye = eye_mask(local_out)
    bias = to_col(up_b[...], eye)
    bias4 = jnp.concatenate([bias] * 4, axis=0)
    quarter = 4 * local_out
    for c0 in range(0, count, 3 * LANES):
        cols = pl.ds(c0, 3 * LANES)
        center = stacked[0:channels, cols]
        low = dot(up_w[quarter : 2 * quarter, :], center)
        low = low + dot(up_w[3 * quarter : 4 * quarter, :], stacked[channels : 2 * channels, cols])
        high = dot(up_w[2 * quarter : 3 * quarter, :], center)
        high = high + dot(up_w[0:quarter, :], stacked[2 * channels : 3 * channels, cols])
        low = (low + bias4).astype(BF)
        high = (high + bias4).astype(BF)
        for b in range(3):
            block = c0 // LANES + b
            if block * local_out >= phases.shape[0]:
                continue
            for r in range(8):
                source = (low, high)[r // 4]
                phases[block * local_out : (block + 1) * local_out, r * LANES : (r + 1) * LANES] = (
                    source[
                        (r % 4) * local_out : (r % 4 + 1) * local_out,
                        b * LANES : (b + 1) * LANES,
                    ]
                )
    early[1].wait()
    turned = dot(phases[...], held_order[...]).astype(BF)
    for block in range(count // LANES):
        wide[:, block * 1024 : (block + 1) * 1024] = turned[
            block * local_out : (block + 1) * local_out, :
        ]
    own = 8 * frames // pieces
    fetch(
        [
            (wide.at[:, at((idx[1] ^ s) * own, own + 2 * HALO, LANES)], outs[s])
            for s in range(pieces)
        ],
        out_sems,
    )
    for copy in kept:
        copy.wait()


def sample_masks(sample_id, distance):
    width = sample_id.shape[1]
    ids = jnp.broadcast_to(sample_id[...], (8, width))
    back = pltpu.roll(ids, distance, axis=1)
    ahead = pltpu.roll(ids, width - distance, axis=1)
    return (
        jnp.where(back == ids, 1.0, 0.0)[0:1, :].astype(BF),
        jnp.where(ahead == ids, 1.0, 0.0)[0:1, :].astype(BF),
    )


def forward_kernel(pieces, blocks, idx, *refs):
    parts = refs[:pieces]
    plain, sample_id, silence = refs[pieces : pieces + 3]
    outs = refs[pieces + 3 : 2 * pieces + 3]
    kept = refs[2 * pieces + 3 : 2 * pieces + 8]
    hidden, taps, pair, final, sems, out_sems = refs[2 * pieces + 8 :]
    keep_h, keep_u, keep_m, keep_sh, keep_sc = kept
    rows, width = parts[0].shape
    channels = pieces * rows
    fetch(
        [(parts[s], hidden.at[at((idx[1] ^ s) * rows, rows, 16), :]) for s in range(pieces)], sems
    )
    for j in range(blocks):
        distance = 3**j
        tail = plain[j, :, 5 * channels : 5 * channels + TAIL].astype(F32)
        dil_b = tail[:, 0:1] + tail[:, 1:2]
        out_b = tail[:, 2:3] + tail[:, 3:4]

        low = hidden[...]
        keep_h[j] = low
        pair[channels : 2 * channels, :] = low
        acted, slope = unit(low.astype(F32))
        acted = acted.astype(BF)
        taps[channels : 2 * channels, :] = acted
        keep_u[j] = acted
        keep_sh[j] = slope.astype(BF)
        back, ahead = sample_masks(sample_id, distance)
        center = taps[channels : 2 * channels, :]
        taps[0:channels, :] = pltpu.roll(center, distance, axis=1) * back
        taps[2 * channels : 3 * channels, :] = pltpu.roll(center, width - distance, axis=1) * ahead

        inner = dot(plain[j, :, 0 : 3 * channels], taps[...]) + dil_b
        acted, slope = unit(inner)
        acted = acted.astype(BF)
        pair[0:channels, :] = acted
        keep_m[j] = acted
        keep_sc[j] = slope.astype(BF)
        after = dot(plain[j, :, 3 * channels : 5 * channels], pair[...]) + out_b
        if j < blocks - 1:
            hidden[...] = after.astype(BF)
        else:
            final[...] = after
    own = width - 2 * HALO
    voiced = silence[:, at(idx[1] * own, own, LANES)].astype(F32)
    hidden[:, 0:own] = (final[:, HALO : HALO + own] * voiced).astype(BF)
    fetch(
        [
            (hidden.at[at((idx[1] ^ s) * rows, rows, 16), 0:own], outs[s])
            for s in range(pieces)
        ],
        out_sems,
    )


def spread_taps(j, center, sample_id, taps):
    channels, width = center.shape
    distance = 3**j
    back, ahead = sample_masks(sample_id, distance)
    taps[channels : 2 * channels, :] = center
    taps[0:channels, :] = pltpu.roll(center, width - distance, axis=1) * ahead
    taps[2 * channels : 3 * channels, :] = pltpu.roll(center, distance, axis=1) * back


def edge_start(pieces, peer):
    return jnp.where(peer < pieces // 2, 0, HALO)


def backward_kernel(pieces, idx, *refs):
    parts = refs[:pieces]
    dil_t, point_t, sample_id, keep_sh, keep_sc = refs[pieces : pieces + 5]
    outs = refs[pieces + 5 : 2 * pieces + 5]
    errs, inners, taps, low, sems, out_sems = refs[2 * pieces + 5 :]
    rows = parts[0].shape[0]
    blocks, channels, width = errs.shape
    last = blocks - 1
    fetch(
        [(parts[s], errs.at[last, at((idx[1] ^ s) * rows, rows, 16), :]) for s in range(pieces)],
        sems,
    )
    for j in reversed(range(blocks)):
        err = errs[j]
        inner = dot(point_t[j, :, 0:channels], err) * keep_sc[j].astype(F32)
        inner = inner.astype(BF)
        inners[j] = inner
        spread_taps(j, inner, sample_id, taps)
        spread = dot(dil_t[j], taps[...]) * keep_sh[j].astype(F32)
        after = (spread + dot(point_t[j, :, channels : 2 * channels], err)).astype(BF)
        if j > 0:
            errs[j - 1] = after
        else:
            low[...] = after
    lanes = at(edge_start(pieces, idx[1]), width - HALO, LANES)
    fetch(
        [(low.at[at((idx[1] ^ s) * rows, rows, 16), lanes], outs[s]) for s in range(pieces)],
        out_sems,
    )


def grad_kernel(pieces, sequence, idx, errs, inners, sample_id, keep_h, keep_u, keep_m, *refs):
    keep, send, taps, mats, sems = refs
    blocks, channels, width = errs.shape
    inside = pl.ds(HALO, width - 2 * HALO)
    rows = channels // pieces
    lane = lax.broadcasted_iota(jnp.int32, (channels, channels), 1)
    tail = jnp.zeros((channels, channels), F32)
    for j in range(blocks):
        spread_taps(j, inners[j], sample_id, taps)
        err = errs[j, :, inside]
        mats[5 * j + 3] = dot_rt(err, keep_m[j, :, inside]).astype(BF)
        mats[5 * j + 4] = dot_rt(err, keep_h[j, :, inside]).astype(BF)
        for k in range(3):
            mats[5 * j + k] = dot_rt(
                taps[k * channels : (k + 1) * channels, inside], keep_u[j, :, inside]
            ).astype(BF)
        dil_sum = jnp.sum(inners[j, :, inside].astype(F32), axis=1, keepdims=True)
        out_sum = jnp.sum(err.astype(F32), axis=1, keepdims=True)
        tail = tail + jnp.where(lane == 2 * j, dil_sum, 0.0)
        tail = tail + jnp.where(lane == 2 * j + 1, out_sum, 0.0)
    mats[5 * blocks] = tail.astype(BF)
    size = (5 * blocks + 1) * rows * pieces // len(sequence)
    part = min(size, rows)
    half = len(sequence) // 2
    pairs = []
    for position, (s, t) in enumerate(sequence):
        target = (keep, send)[position // half]
        for q in range(size // part):
            place = (idx[0] ^ t) * (size // part) + q
            row = (idx[1] ^ s) * rows + lax.rem(place, rows // part) * part
            start = position % half * size + q * part
            pairs.append(
                (
                    mats.at[lax.div(place, rows // part), at(row, part, 16), :],
                    target.at[start : start + part, :],
                )
            )
    fetch(pairs, sems)


def halve_kernel(idx, keep, got, next_keep, next_send):
    half = next_keep.shape[0]
    total = keep[...].astype(F32) + got[...].astype(F32)
    next_keep[...] = total[:half].astype(BF)
    next_send[...] = total[half:].astype(BF)


def up_back_kernel(pieces, peers, orders, idx, *refs):
    parts = refs[:pieces]
    up_v, acted, frame_id, order = refs[pieces : pieces + 4]
    cols_grad, *streams = refs[pieces + 4 : pieces + 9]
    wide, stacked, phases, low_grad, held_v, held_act, held_order, sems = refs[pieces + 9 :]
    rows = parts[0].shape[0]
    own = parts[0].shape[1] - HALO
    length = pieces * own
    frames = length // 8
    copies = []
    for s in range(pieces):
        peer = idx[1] ^ s
        target = wide.at[:, at(HALO + peer * own, own, LANES)]
        source = parts[s].at[:, at(HALO - edge_start(pieces, peer), own, LANES)]
        copies.append(pltpu.make_async_copy(source, target, sems.at[s]))
        copies[-1].start()
    late = []
    for source, target in ((order, held_order), (acted, held_act), (up_v, held_v)):
        late.append(pltpu.make_async_copy(source, target, sems.at[pieces + len(late)]))
        late[-1].start()
    wide[:, HALO + length :] = jnp.zeros((rows, wide.shape[1] - HALO - length), BF)
    for copy in copies:
        copy.wait()
    for s in range(pieces):
        peer = idx[1] ^ s

        @pl.when(peer == 0)
        def _():
            pltpu.sync_copy(parts[s].at[:, 0:HALO], wide.at[:, 0:HALO])

        @pl.when(peer == pieces - 1)
        def _():
            pltpu.sync_copy(
                parts[s].at[:, own:], wide.at[:, HALO + length : 2 * HALO + length]
            )

    total = wide.shape[1] // 8
    blocks = total // LANES
    for block in range(blocks):
        stacked[block * rows : (block + 1) * rows, :] = wide[:, block * 1024 : (block + 1) * 1024]
    late[0].wait()
    turned = dot_rt(stacked[...], held_order[...]).astype(BF)
    for block in range(blocks):
        for r in range(8):
            phases[r * rows : (r + 1) * rows, block * LANES : (block + 1) * LANES] = turned[
                block * rows : (block + 1) * rows, r * LANES : (r + 1) * LANES
            ]
    ids = jnp.broadcast_to(frame_id[...], (8, frame_id.shape[1]))
    before = pltpu.roll(ids, 1, axis=1)
    after = pltpu.roll(ids, frame_id.shape[1] - 1, axis=1)
    inside = slice(LANES, LANES + frames)
    left = jnp.where(before == ids, 1.0, 0.0)[0:1, inside]
    right = jnp.where(after == ids, 1.0, 0.0)[0:1, inside]
    lead = HALO // 8
    eighth = 4 * rows
    sample_sum = jnp.zeros((rows, 1), F32)
    for part in range(2):
        base = phases[part * eighth : (part + 1) * eighth, :]
        center = pltpu.roll(base, total - lead, axis=1)[:, 0:frames]
        cols_grad[(4 + 4 * part) * rows : (8 + 4 * part) * rows, :] = center
        partial = jnp.sum(center.astype(F32), axis=1, keepdims=True)
        for r in range(4):
            sample_sum = sample_sum + partial[r * rows : (r + 1) * rows]
        if part == 1:
            moved = pltpu.roll(base, total - lead + 1, axis=1)[:, 0:frames]
            cols_grad[0:eighth, :] = (moved.astype(F32) * left).astype(BF)
        else:
            moved = pltpu.roll(base, total - lead - 1, axis=1)[:, 0:frames]
            cols_grad[12 * rows : 16 * rows, :] = (moved.astype(F32) * right).astype(BF)
    taps = up_v.shape[0]
    channels = up_v.shape[2]
    inner = jnp.zeros((rows, channels), F32)
    late[1].wait()
    grad = dot_rt(cols_grad[...], held_act[...])
    low_grad[...] = grad.astype(BF)
    late[2].wait()
    for k in range(taps):
        inner = inner + grad[k * rows : (k + 1) * rows] * held_v[k]
    inner = jnp.sum(inner, axis=0, keepdims=True)
    bias = jnp.concatenate(
        [to_row(sample_sum, eye_mask(rows)), jnp.zeros((1, channels - rows), F32)], axis=1
    )
    side = channels // 2
    line = lax.broadcasted_iota(jnp.int32, (SUMS, side), 0)
    sums = jnp.zeros((SUMS, side), F32)
    for number, value in enumerate((inner[:, :side], inner[:, side:], bias[:, :side])):
        high = value.astype(BF).astype(F32)
        sums = sums + jnp.where(line == 2 * number, high, 0.0)
        sums = sums + jnp.where(line == 2 * number + 1, value - high, 0.0)
    half = peers // 2
    size = taps * rows // peers
    first = (streams[0].shape[0] - SUMS) // half
    second = 2 * size - first
    streams[0][half * first :, :] = sums.astype(BF)
    streams[1][half * first :, :] = sums.astype(BF)
    for position, s in enumerate(orders[0]):
        target = streams[position // half]
        start = position % half * first
        target[start : start + first, :] = low_grad[at((idx[0] ^ s) * size, first, 16), 0:side]
    for position, s in enumerate(orders[1]):
        target = streams[2 + position // half]
        start = position % half * second
        piece = (idx[0] ^ s) * size
        target[start : start + size, :] = low_grad[at(piece, size, 16), side:]
        if size > first:
            target[start + size : start + second, :] = low_grad[
                at(piece + first, size - first, 16), 0:side
            ]


def input_back_kernel(pieces, order, idx, up_w, cols_grad, keep, send, total, sems):
    total[...] = lax.dot_general(
        up_w[...], cols_grad[...], (((0,), (0,)), ((), ())), preferred_element_type=F32
    ).astype(BF)
    size = total.shape[0] // pieces
    pairs = []
    for position, s in enumerate(order):
        target = (keep, send)[position // (pieces // 2)]
        start = position % (pieces // 2) * size
        pairs.append(
            (total.at[at((idx[1] ^ s) * size, size, 16), :], target.at[start : start + size, :])
        )
    fetch(pairs, sems)


def join_kernel(idx, keep, got, term, other, next_keep, next_send):
    rows = keep.shape[0] - SUMS
    half, part = rows // 2, term.shape[0] // 2
    total = keep[...].astype(F32) + got[...].astype(F32)
    grads = (term[...].astype(F32) + other[...].astype(F32)).astype(BF)
    for number, target in enumerate((next_keep, next_send)):
        target[0:half, :] = total[number * half : (number + 1) * half].astype(BF)
        target[half : half + part, :] = grads[number * part : (number + 1) * part]
        target[half + part :, :] = total[rows:].astype(BF)


def step_kernel(rows, last, idx, keep, got, *outs):
    total = keep[...].astype(F32) + got[...].astype(F32)
    grads = total.shape[0] - rows - SUMS
    if last:
        outs[0][...] = total[: rows + grads].astype(BF)
        outs[1][...] = total[rows + grads :]
        return
    for number, target in enumerate(outs):
        half, part = rows // 2, grads // 2
        target[0:half, :] = total[number * half : (number + 1) * half].astype(BF)
        start = rows + number * part
        target[half : half + part, :] = total[start : start + part].astype(BF)
        target[half + part :, :] = total[rows + grads :].astype(BF)


def add_kernel(idx, keep, got, out):
    out[...] = (keep[...].astype(F32) + got[...].astype(F32)).astype(BF)


def double_kernel(rows, idx, own, got, out):
    grads = own.shape[0] - rows
    out[0:rows, :] = own[0:rows, :]
    out[rows : 2 * rows, :] = got[0:rows, :]
    out[2 * rows : 2 * rows + grads, :] = own[rows:, :]
    out[2 * rows + grads :, :] = got[rows:, :]


def final_kernel(orders, first, idx, *refs):
    streams = refs[:4]
    up_v, up_sq, up_g, inner_sum, dil_v, dil_g, mix_v, mix_g, skip_v, skip_g = refs[4:14]
    up_v_grad, up_g_grad, *outs = refs[14:24]
    whole, blocks_whole, staged, *block_staged, in_sems, grad_sems, out_sems = refs[24:]
    half = len(orders[0]) // 2
    size = whole.shape[0] // (2 * half)
    side = whole.shape[1] // 2
    second = 2 * size - first
    copies = []

    def move(source, start, count, target):
        copies.append(
            pltpu.make_async_copy(
                source.at[start : start + count, :], target, in_sems.at[len(copies)]
            )
        )
        copies[-1].start()

    for position, s in enumerate(orders[0]):
        target = whole.at[at((idx[0] ^ s) * size, first, 16), 0:side]
        move(streams[position // half], position % half * first, first, target)
    for position, s in enumerate(orders[1]):
        source = streams[2 + position // half]
        start = position % half * second
        piece = (idx[0] ^ s) * size
        move(source, start, size, whole.at[at(piece, size, 16), side:])
        if size > first:
            target = whole.at[at(piece + first, size - first, 16), 0:side]
            move(source, start + size, size - first, target)
    size = blocks_whole.shape[0] // (2 * half)
    grads = []
    for position, s in enumerate(orders[0]):
        start = half * first + position % half * size
        grads.append(
            pltpu.make_async_copy(
                streams[position // half].at[start : start + size, :],
                blocks_whole.at[at((idx[0] ^ s) * size, size, 16), :],
                grad_sems.at[len(grads)],
            )
        )
        grads[-1].start()
    for copy in copies:
        copy.wait()
    sent = []

    def ship(source, target):
        sent.append(pltpu.make_async_copy(source, target, out_sems.at[len(sent)]))
        sent[-1].start()

    norm = jnp.sqrt(up_sq[...])
    inner = inner_sum[...]
    scale = up_g[...] / norm
    pull = up_g[...] * inner / (norm * norm * norm)
    rows = up_v.shape[1]
    for k in range(up_v.shape[0]):
        grad = whole[k * rows : (k + 1) * rows, :].astype(F32)
        staged[k] = scale * grad - pull * up_v[k]
        ship(staged.at[k], up_v_grad.at[k])
    up_g_grad[...] = inner / norm
    for copy in grads:
        copy.wait()
    dil_v_hbm, dil_g_out, dil_b_out, mix_v_hbm, mix_g_out, out_b_out, skip_v_hbm, skip_g_out = outs
    dil_v_out, mix_v_out, skip_v_out = block_staged
    eye = eye_mask(rows)
    blocks = dil_v.shape[0]
    tail = blocks_whole[5 * blocks * rows :, :].astype(F32)
    for j in range(blocks):

        def mat(m):
            start = (5 * j + m) * rows
            return blocks_whole[start : start + rows, :].astype(F32)

        square = jnp.zeros((rows, 1), F32)
        inner = jnp.zeros((rows, 1), F32)
        for k in range(3):
            v = dil_v[j, k]
            square = square + jnp.sum(v * v, axis=1, keepdims=True)
            inner = inner + jnp.sum(v * mat(k), axis=1, keepdims=True)
        norm = jnp.sqrt(square)
        gain = to_col(dil_g[j : j + 1, :], eye)
        for k in range(3):
            dil_v_out[j, k] = gain / norm * mat(k) - gain * inner / (norm**3) * dil_v[j, k]
        ship(dil_v_out.at[j], dil_v_hbm.at[j])
        dil_g_out[j : j + 1, :] = to_row(inner / norm, eye)
        for number, (vref, gref, v_out, v_hbm, g_out) in enumerate(
            (
                (mix_v, mix_g, mix_v_out, mix_v_hbm, mix_g_out),
                (skip_v, skip_g, skip_v_out, skip_v_hbm, skip_g_out),
            )
        ):
            v = vref[j]
            grad = mat(3 + number)
            norm = jnp.sqrt(jnp.sum(v * v, axis=1, keepdims=True))
            inner = jnp.sum(v * grad, axis=1, keepdims=True)
            gain = to_col(gref[j : j + 1, :], eye)
            v_out[j] = gain / norm * grad - gain * inner / (norm**3) * v
            ship(v_out.at[j], v_hbm.at[j])
            g_out[j : j + 1, :] = to_row(inner / norm, eye)
        dil_b_out[j : j + 1, :] = to_row(tail[:, 2 * j : 2 * j + 1], eye)
        out_b_out[j : j + 1, :] = to_row(tail[:, 2 * j + 1 : 2 * j + 2], eye)
    for copy in sent:
        copy.wait()


def place_kernel(pieces, idx, *refs):
    parts, out, sems = refs[:pieces], refs[pieces], refs[pieces + 1]
    own = parts[0].shape[1]
    fetch(
        [(parts[s], out.at[:, at((idx[1] ^ s) * own, own, LANES)]) for s in range(pieces)], sems
    )


def input_kernel(idx, *refs):
    *terms, spectrogram, out = refs
    total = terms[0][...].astype(F32)
    for term in terms[1:]:
        total = total + term[...].astype(F32)
    out[...] = (total * unit(spectrogram[...].astype(F32))[1]).astype(BF)


def local(
    spectrogram_input,
    upsample_direction,
    upsample_magnitude,
    upsample_bias,
    dilated_direction,
    dilated_magnitude,
    dilated_bias,
    pointwise_direction,
    pointwise_magnitude,
    block_output_bias,
    shortcut_direction,
    shortcut_magnitude,
    cotangent,
    silence,
    segments,
):
    pieces, peers = lax.axis_size("chan"), lax.axis_size("tm")
    chan, tm = lax.axis_index("chan"), lax.axis_index("tm")
    in_rows, frames = spectrogram_input.shape
    taps, rows, in_channels = upsample_direction.shape
    blocks = dilated_direction.shape[0]
    channels = dilated_direction.shape[3]
    length = 8 * frames
    own = length // pieces
    width = own + 2 * HALO
    packed_width = 5 * channels + TAIL
    forward = [(k, k + 1) for k in range(peers - 1)]
    backward = [(k + 1, k) for k in range(peers - 1)]
    dma = pltpu.SemaphoreType.DMA
    lead = HALO // 8
    tie = lax.optimization_barrier

    spread = np.arange(8 * LANES)
    order = np.zeros((8 * LANES, 8 * LANES), np.float32)
    order[spread, 8 * (spread % LANES) + spread // LANES] = 1.0
    order = jnp.asarray(order, BF)

    silence_row = silence.reshape(1, length)
    up_g = upsample_magnitude.reshape(1, in_channels)
    edge_rows = in_rows + rows
    ahead, behind = kernel_call(
        edge_kernel,
        [((edge_rows, LANES), BF, "V")] * 2,
        [spectrogram_input, cotangent, silence_row],
        "HHH",
        scratch=[
            pltpu.VMEM((in_rows, LANES), BF),
            pltpu.VMEM((in_rows, LANES), BF),
            pltpu.VMEM((2, rows, HALO), BF),
            pltpu.VMEM((2, 1, HALO), jnp.int32),
            dma((6,)),
        ],
    )
    low_edge = lax.ppermute(ahead, "tm", forward)
    high_edge = lax.ppermute(behind, "tm", backward)
    all_mains = gather_chan(spectrogram_input)
    up_v_late, ahead = tie((upsample_direction, ahead))
    (up_sq,) = kernel_call(
        square_kernel, [((1, in_channels), F32, "V")], [up_v_late], "F", micros=2
    )
    block_args = [
        dilated_direction,
        dilated_magnitude,
        dilated_bias,
        pointwise_direction,
        pointwise_magnitude,
        block_output_bias,
        shortcut_direction,
        shortcut_magnitude,
    ]
    sides = jnp.concatenate([low_edge[:in_rows], high_edge[:in_rows]], axis=1)
    block_args, sides = tie((block_args, sides))
    packed_half = ((blocks * rows // 2, packed_width), BF, "V")
    packed, near, far = kernel_call(
        prep_kernel,
        [((blocks * rows, packed_width), BF, "V"), packed_half, packed_half],
        block_args,
        "FFFFFFFF",
        micros=3,
    )
    all_sides = gather_chan(sides)
    for bit in bits_of(pieces):
        up_sq = up_sq + swap(up_sq, "chan", bit)
    padded_ids = jnp.pad(segments.astype(F32), LANES, constant_values=-1.0)
    frame_id = lax.dynamic_slice_in_dim(padded_ids, tm * frames, frames + 2 * LANES)
    sample_id = jnp.repeat(
        lax.dynamic_slice_in_dim(
            padded_ids, LANES + tm * frames + chan * (own // 8) - lead, width // 8
        ),
        8,
    ).reshape(1, width)
    frame_id = frame_id.reshape(1, frames + 2 * LANES)
    top = pieces // 2
    near, all_sides[top], up_sq = tie((near, all_sides[top], up_sq))

    count = -(-(frames + 2 * lead) // LANES) * LANES
    count = -(-count // (3 * LANES)) * 3 * LANES
    up_outs = kernel_call(
        functools.partial(up_kernel, pieces),
        [((rows, width), BF, "H")] * pieces
        + [((in_channels, frames), BF, "H"), ((taps * rows, in_channels), BF, "H")],
        all_mains
        + all_sides
        + [upsample_direction, up_sq, up_g, upsample_bias.reshape(1, rows), frame_id, order],
        "A" * (2 * pieces) + "HGFFGH",
        scratch=[
            pltpu.VMEM((in_channels, frames + 2 * LANES), BF),
            pltpu.VMEM((3 * in_channels, count), BF),
            pltpu.VMEM((count // LANES * rows, 8 * LANES), BF),
            pltpu.VMEM((rows, 8 * count), BF),
            pltpu.VMEM((in_channels, frames), BF),
            pltpu.VMEM((taps * rows, in_channels), BF),
            pltpu.VMEM(upsample_direction.shape, F32),
            pltpu.VMEM(order.shape, BF),
            dma((3 * pieces + 2,)),
            dma((pieces + 2,)),
        ],
        micros=6,
    )
    acted, up_w = up_outs[pieces:]
    chan_bits = bits_of(pieces)
    held_near = {0: near}
    for bit in reversed(chan_bits[1:]):
        for slot in list(held_near):
            held_near[slot ^ bit] = swap(held_near[slot], "chan", bit)
    hidden_parts, held_near, low_edge = tie((list(up_outs[:pieces]), held_near, low_edge))
    cut = kernel_call(
        functools.partial(cut_kernel, pieces),
        [((rows, width), BF, "H")] * pieces,
        [cotangent, silence_row, low_edge, high_edge],
        "FFGG",
        scratch=[pltpu.VMEM((rows, length + 2 * HALO), BF), dma((pieces,))],
        micros=2,
    )
    all_hidden = exchange_chan(hidden_parts)
    all_packed = [packed, swap(packed, "chan", 1)]
    for slot in range(2, pieces, 2):
        two = [held_near[slot], swap(held_near[slot], "tm", 1)]
        two, all_hidden[top], cut = tie((two, all_hidden[top], list(cut)))
        all_packed += two + [swap(value, "chan", 1) for value in two]

    plain, dil_t, point_t = kernel_call(
        functools.partial(weight_kernel, pieces, blocks),
        [
            ((blocks, channels, packed_width), BF, "R"),
            ((blocks, channels, 3 * channels), BF, "R"),
            ((blocks, channels, 2 * channels), BF, "R"),
        ],
        all_packed,
        "A" * len(all_packed),
        scratch=[dma((2 * blocks * pieces,))],
        micros=3,
    )
    cut, plain = tie((list(cut), plain))
    all_err = exchange_chan(cut)

    kept_shape = ((blocks, channels, width), BF, "R")
    forward_outs = kernel_call(
        functools.partial(forward_kernel, pieces, blocks),
        [((rows, own), BF, "H")] * pieces + [kept_shape] * 5,
        all_hidden + [plain, sample_id, silence_row],
        "A" * pieces + "RGF",
        scratch=[
            pltpu.VMEM((channels, width), BF),
            pltpu.VMEM((3 * channels, width), BF),
            pltpu.VMEM((2 * channels, width), BF),
            pltpu.VMEM((channels, width), F32),
            dma((pieces,)),
            dma((pieces,)),
        ],
        micros=10,
    )
    keep_h, keep_u, keep_m, keep_sh, keep_sc = forward_outs[pieces:]
    activation_parts = list(forward_outs[:pieces])

    backward_outs = kernel_call(
        functools.partial(backward_kernel, pieces),
        [((rows, width - HALO), BF, "H")] * pieces + [kept_shape] * 2,
        all_err + [dil_t, point_t, sample_id, keep_sh, keep_sc],
        "A" * pieces + "RRGRR",
        scratch=[
            pltpu.VMEM((3 * channels, width), BF),
            pltpu.VMEM((channels, width), BF),
            dma((pieces,)),
            dma((pieces,)),
        ],
        micros=10,
    )
    errs, inners = backward_outs[pieces:]
    all_low = exchange_chan(list(backward_outs[:pieces]))

    chan_order = order_of(chan_bits)
    tm_bits = bits_of(peers)
    path = [("chan", 1), ("tm", 1)] + [("chan", bit) for bit in chan_bits[1:]]
    path_order = [(0, 0)]
    for axis, bit in reversed(path + [("tm", bit) for bit in tm_bits[1:]]):
        other = [
            (s + bit, t) if axis == "chan" else (s, t + bit) for s, t in path_order
        ]
        path_order = path_order + other
    mats = 5 * blocks + 1
    share = pieces // 2 * mats * rows
    keep, send = kernel_call(
        functools.partial(grad_kernel, pieces, path_order),
        [((share, channels), BF, "H")] * 2,
        [errs, inners, sample_id, keep_h, keep_u, keep_m],
        "RRGRRR",
        scratch=[
            pltpu.VMEM((3 * channels, width), BF),
            pltpu.VMEM((mats, channels, channels), BF),
            dma((max(mats * pieces, peers * pieces),)),
        ],
        micros=8,
    )

    def scatter(keep, send, path):
        for axis, bit in path[:-1]:
            got = swap(send, axis, bit)
            next_shape = ((keep.shape[0] // 2, keep.shape[1]), BF, "V")
            keep, send = kernel_call(halve_kernel, [next_shape] * 2, [keep, got], "GG")
        return keep, swap(send, *path[-1])

    keep, send, all_low[top] = tie((keep, send, all_low[top]))
    got = swap(send, *path[0])
    keep, send = kernel_call(
        halve_kernel, [((share // 2, channels), BF, "V")] * 2, [keep, got], "GG"
    )
    block_terms = scatter(keep, send, path[1:])
    send, all_low = tie((send, all_low))

    turned_bits = tm_bits[1:] + tm_bits[:1]
    orders = (order_of(tm_bits), order_of(turned_bits))
    half = peers // 2
    total_rows = taps * rows
    size = total_rows // peers
    side = in_channels // 2
    first = max(16, size // 2 // 16 * 16)
    second = 2 * size - first
    cols_grad, keep_one, send_one, keep_two, send_two = kernel_call(
        functools.partial(up_back_kernel, pieces, peers, orders),
        [((total_rows, frames), BF, "R")]
        + [((half * first + SUMS, side), BF, "V")] * 2
        + [((half * second, side), BF, "V")] * 2,
        all_low + [upsample_direction, acted, frame_id, order],
        "A" * pieces + "HHGH",
        scratch=[
            pltpu.VMEM((rows, 8 * count), BF),
            pltpu.VMEM((count // LANES * rows, 8 * LANES), BF),
            pltpu.VMEM((8 * rows, count), BF),
            pltpu.VMEM((total_rows, in_channels), BF),
            pltpu.VMEM(upsample_direction.shape, F32),
            pltpu.VMEM((in_channels, frames), BF),
            pltpu.VMEM(order.shape, BF),
            dma((pieces + 3,)),
        ],
        micros=5,
    )

    piece_rows = pieces // 2 * in_rows
    keep, send = kernel_call(
        functools.partial(input_back_kernel, pieces, chan_order),
        [((piece_rows, frames), BF, "H")] * 2,
        [up_w, cols_grad],
        "FR",
        scratch=[pltpu.VMEM((in_channels, frames), BF), dma((pieces,))],
        micros=3,
    )
    steps = len(tm_bits)
    block_rows = mats * rows
    one_rows, two_rows = half * first, half * second
    for step in range(steps):
        got_one = swap(send_one, "tm", tm_bits[step])
        got_two = swap(send_two, "tm", turned_bits[step])
        if step == 0:
            got_one, got_two, keep, send = tie((got_one, got_two, keep, send))
            input_terms = scatter(keep, send, [("chan", bit) for bit in chan_bits])
        elif step == steps - 1:
            got_one, got_two, input_terms = tie((got_one, got_two, input_terms))
            activation_parts, got_one = tie((activation_parts, got_one))
            activation_parts = exchange_chan(activation_parts)
        else:
            got_one, got_two = tie((got_one, got_two))
        last = step == steps - 1
        if not last:
            one_rows, two_rows, block_rows = one_rows // 2, two_rows // 2, block_rows // 2
            ride = block_rows // 2
            next_shape = ((one_rows + ride + SUMS, side), BF, "V")
            if step == 0:
                keep_one, send_one = kernel_call(
                    join_kernel, [next_shape] * 2, [keep_one, got_one, *block_terms], "GGGG"
                )
            else:
                keep_one, send_one = kernel_call(
                    functools.partial(step_kernel, 2 * one_rows, False),
                    [next_shape] * 2,
                    [keep_one, got_one],
                    "GG",
                )
            keep_two, send_two = kernel_call(
                halve_kernel, [((two_rows, side), BF, "V")] * 2, [keep_two, got_two], "GG"
            )
        else:
            block_rows = block_rows // 2
            own_one, sums = kernel_call(
                functools.partial(step_kernel, one_rows, True),
                [((one_rows + block_rows, side), BF, "V"), ((SUMS, side), F32, "V")],
                [keep_one, got_one],
                "GG",
            )
            (own_two,) = kernel_call(
                add_kernel, [((two_rows, side), BF, "V")], [keep_two, got_two], "GG"
            )
    for step in reversed(range(steps)):
        got_one = swap(own_one, "tm", tm_bits[step])
        got_two = swap(own_two, "tm", turned_bits[step])
        if step == 1:
            got_one, got_two, activation_parts = tie((got_one, got_two, activation_parts))
        else:
            got_one, got_two = tie((got_one, got_two))
        if step > 0:
            (own_one,) = kernel_call(
                functools.partial(double_kernel, one_rows),
                [((2 * own_one.shape[0], side), BF, "V")],
                [own_one, got_one],
                "GG",
            )
            one_rows = 2 * one_rows
            own_two = jnp.concatenate([own_two, got_two], axis=0)

    pair = sums[0:6:2] + sums[1:6:2]
    inner_sum = pair[0:2].reshape(1, in_channels)
    for bit in chan_bits:
        inner_sum = inner_sum + swap(inner_sum, "chan", bit)

    (input_grad,) = kernel_call(
        input_kernel,
        [((in_rows, frames), BF, "V")],
        [*input_terms, spectrogram_input],
        "GGF",
    )
    (activation,) = kernel_call(
        functools.partial(place_kernel, pieces),
        [((rows, length), BF, "V")],
        activation_parts,
        "A" * pieces,
        scratch=[dma((pieces,))],
        micros=2,
    )

    final_outs = kernel_call(
        functools.partial(final_kernel, orders, first),
        [
            (upsample_direction.shape, F32, "H"),
            ((1, in_channels), F32, "V"),
            (dilated_direction.shape, F32, "H"),
            (dilated_magnitude.shape, F32, "V"),
            (dilated_bias.shape, F32, "V"),
            (pointwise_direction.shape, F32, "H"),
            (pointwise_magnitude.shape, F32, "V"),
            (block_output_bias.shape, F32, "V"),
            (shortcut_direction.shape, F32, "H"),
            (shortcut_magnitude.shape, F32, "V"),
        ],
        [
            own_one,
            got_one,
            own_two,
            got_two,
            upsample_direction,
            up_sq,
            up_g,
            inner_sum,
            dilated_direction,
            dilated_magnitude,
            pointwise_direction,
            pointwise_magnitude,
            shortcut_direction,
            shortcut_magnitude,
        ],
        "AAAAFGFGFFFFFF",
        scratch=[
            pltpu.VMEM((total_rows, in_channels), BF),
            pltpu.VMEM((mats * rows, channels), BF),
            pltpu.VMEM(upsample_direction.shape, F32),
            pltpu.VMEM(dilated_direction.shape, F32),
            pltpu.VMEM(pointwise_direction.shape, F32),
            pltpu.VMEM(shortcut_direction.shape, F32),
            dma((3 * peers,)),
            dma((peers,)),
            dma((taps + 3 * blocks,)),
        ],
        micros=5,
    )
    up_v_grad, up_g_grad, dil_v_grad, dil_g_grad, dil_b_grad = final_outs[:5]
    mix_v_grad, mix_g_grad, out_b_grad, skip_v_grad, skip_g_grad = final_outs[5:]
    return (
        activation,
        input_grad,
        up_v_grad,
        up_g_grad.reshape(in_channels),
        pair[2, :rows],
        dil_v_grad,
        dil_g_grad,
        dil_b_grad,
        mix_v_grad,
        mix_g_grad,
        out_b_grad,
        skip_v_grad,
        skip_g_grad,
    )


def solution(mesh):
    placed = (
        P("chan", "tm"),
        P(None, "chan", None),
        P(),
        P("chan"),
        P(None, None, "chan", None),
        P(None, "chan"),
        P(None, "chan"),
        P(None, "chan", None),
        P(None, "chan"),
        P(None, "chan"),
        P(None, "chan", None),
        P(None, "chan"),
        P("chan", "tm"),
        P("tm"),
        P(),
    )
    return jax.shard_map(
        local,
        mesh=mesh,
        in_specs=placed,
        out_specs=(
            P("chan", "tm"),
            P("chan", "tm"),
            P(None, "chan", None),
            P(),
            P("chan"),
            P(None, None, "chan", None),
            P(None, "chan"),
            P(None, "chan"),
            P(None, "chan", None),
            P(None, "chan"),
            P(None, "chan"),
            P(None, "chan", None),
            P(None, "chan"),
        ),
        check_vma=False,
    )
```

```python
import functools

import jax
import jax.numpy as jnp
import numpy as np
from jax import lax
from jax.experimental import pallas as pl
from jax.experimental.pallas import tpu as pltpu
from jax.sharding import PartitionSpec as P

BF = jnp.bfloat16
F32 = jnp.float32
LANES = 128
HALO = 128
TAIL = 128
SUMS = 16
VMEM_LIMIT = 20 * 1024 * 1024


def swap(values, axis, bit):
    count = lax.axis_size(axis)
    return lax.ppermute(values, axis, [(k, k ^ bit) for k in range(count)])


def bits_of(count):
    bits = []
    bit = 1
    while bit < count:
        bits.append(bit)
        bit = 2 * bit
    return bits


def order_of(bits):
    order = [0]
    for bit in reversed(bits):
        order = order + [slot + bit for slot in order]
    return order


def gather_chan(own):
    held = {0: own}
    for bit in reversed(bits_of(lax.axis_size("chan"))):
        for slot in list(held):
            held[slot ^ bit] = swap(held[slot], "chan", bit)
    return [held[slot] for slot in range(len(held))]


def exchange_chan(pieces):
    return [pieces[0]] + [swap(pieces[s], "chan", s) for s in range(1, len(pieces))]


HBM = pl.BlockSpec(memory_space=pltpu.HBM)
VMEM = pl.BlockSpec(memory_space=pltpu.VMEM)


def kernel_call(body, outs, args, specs, scratch=(), micros=1.0):
    held = []
    in_specs = []
    operands = []
    for arg, spec in zip(args, specs, strict=True):
        in_specs.append({"H": HBM, "F": HBM, "R": VMEM, "V": VMEM}[spec])
        if spec == "F":
            held.append(pltpu.VMEM(arg.shape, arg.dtype))
        if spec == "R":
            arg = pltpu.with_memory_space_constraint(arg, pltpu.VMEM)
        if spec in "HF":
            arg = pltpu.with_memory_space_constraint(arg, pltpu.HBM)
        operands.append(arg)
    out_shape = []
    out_specs = []
    for shape, dtype, spec in outs:
        out_specs.append(HBM if spec == "H" else VMEM)
        spaced = {"R": pltpu.VMEM, "H": pltpu.HBM, "V": jax.ShapeDtypeStruct}[spec]
        out_shape.append(spaced(shape, dtype))
    fetched = len(held)

    def wrapped(*refs):
        refs = list(refs)
        if fetched:
            sems = refs.pop()
            targets = refs[-fetched:]
            refs = refs[:-fetched]
            sources = [number for number, spec in enumerate(specs) if spec == "F"]
            fetch([(refs[n], target) for n, target in zip(sources, targets)], sems)
            for n, target in zip(sources, targets):
                refs[n] = target
        body((lax.axis_index("tm"), lax.axis_index("chan")), *refs)

    extra = held + ([pltpu.SemaphoreType.DMA((fetched,))] if fetched else [])
    return pl.pallas_call(
        wrapped,
        out_shape=tuple(out_shape),
        in_specs=in_specs,
        out_specs=tuple(out_specs),
        scratch_shapes=list(scratch) + extra,
        compiler_params=pltpu.CompilerParams(vmem_limit_bytes=VMEM_LIMIT),
        cost_estimate=pl.CostEstimate(
            flops=int(micros * 1.1e9), bytes_accessed=0, transcendentals=0
        ),
    )(*operands)


def fetch(pairs, sems):
    copies = [
        pltpu.make_async_copy(source, target, sems.at[number])
        for number, (source, target) in enumerate(pairs)
    ]
    for copy in copies:
        copy.start()
    for copy in copies:
        copy.wait()


def unit(values):
    th = jnp.tanh(0.5 * values)
    base = 0.6 + 0.4 * th
    return values * base, base + 0.2 * values * (1.0 - th * th)


def unit_act(values):
    return values * (0.6 + 0.4 * jnp.tanh(0.5 * values))


def dot(left, right):
    return lax.dot_general(left, right, (((1,), (0,)), ((), ())), preferred_element_type=F32)


def dot_rt(left, right):
    return lax.dot_general(left, right, (((1,), (1,)), ((), ())), preferred_element_type=F32)


def eye_mask(count):
    rows = lax.broadcasted_iota(jnp.int32, (count, count), 0)
    cols = lax.broadcasted_iota(jnp.int32, (count, count), 1)
    return rows == cols


def to_col(row, eye):
    return jnp.sum(jnp.where(eye, row, 0.0), axis=1, keepdims=True)


def to_row(col, eye):
    return jnp.sum(jnp.where(eye, col, 0.0), axis=0, keepdims=True)


def at(start, size, step):
    return pl.ds(pl.multiple_of(start, step), size)


def edge_kernel(idx, spectrogram, cot, sil, ahead, behind, front, back, sound, mask, sems):
    rows = spectrogram.shape[0]
    frames, count = spectrogram.shape[1], cot.shape[1]
    low, high = pl.ds(0, HALO), pl.ds(count - HALO, HALO)
    fetch(
        [
            (spectrogram.at[:, frames - LANES :], front),
            (spectrogram.at[:, :LANES], back),
            (cot.at[:, high], sound.at[0]),
            (cot.at[:, low], sound.at[1]),
            (sil.at[:, high], mask.at[0]),
            (sil.at[:, low], mask.at[1]),
        ],
        sems,
    )
    ahead[0:rows, :] = front[...]
    behind[0:rows, :] = back[...]
    ahead[rows:, :] = (sound[0].astype(F32) * mask[0].astype(F32)).astype(BF)
    behind[rows:, :] = (sound[1].astype(F32) * mask[1].astype(F32)).astype(BF)


def square_kernel(idx, up_v, up_sq):
    total = jnp.zeros((up_v.shape[1], up_v.shape[2]), F32)
    for k in range(up_v.shape[0]):
        rows = up_v[k]
        total = total + rows * rows
    up_sq[...] = jnp.sum(total, axis=0, keepdims=True)


def prep_kernel(
    idx, dil_v, dil_g, dil_b, mix_v, mix_g, out_b, skip_v, skip_g, up_g, up_b, packed, near, far, up_row, bias_row
):
    up_row[...] = up_g[...]
    bias_row[...] = up_b[...]
    local_out = dil_v.shape[2]
    eye = eye_mask(local_out)
    lane = lax.broadcasted_iota(jnp.int32, (local_out, TAIL), 1)
    width = dil_v.shape[3]
    for j in range(dil_v.shape[0]):
        rows = pl.ds(j * local_out, local_out)
        square = jnp.zeros((local_out, 1), F32)
        for k in range(3):
            v = dil_v[j, k]
            square = square + jnp.sum(v * v, axis=1, keepdims=True)
        norm = jnp.sqrt(square)
        scale = to_col(dil_g[j : j + 1, :], eye) / norm
        for k in range(3):
            packed[rows, k * width : (k + 1) * width] = (dil_v[j, k] * scale).astype(BF)
        for number, (vref, gref) in enumerate(((mix_v, mix_g), (skip_v, skip_g))):
            v = vref[j]
            norm = jnp.sqrt(jnp.sum(v * v, axis=1, keepdims=True))
            scale = to_col(gref[j : j + 1, :], eye) / norm
            packed[rows, (3 + number) * width : (4 + number) * width] = (v * scale).astype(BF)
        first = to_col(dil_b[j : j + 1, :], eye)
        second = to_col(out_b[j : j + 1, :], eye)
        high_one = first.astype(BF).astype(F32)
        high_two = second.astype(BF).astype(F32)
        tail = jnp.where(lane == 0, high_one, 0.0) + jnp.where(lane == 1, first - high_one, 0.0)
        tail = tail + jnp.where(lane == 2, high_two, 0.0)
        tail = tail + jnp.where(lane == 3, second - high_two, 0.0)
        packed[rows, 5 * width : 5 * width + TAIL] = tail.astype(BF)
    half = near.shape[0]
    for number, target in enumerate((near, far)):
        target[...] = packed[at(((idx[0] ^ number) & 1) * half, half, 16), :]


def cut_kernel(pieces, idx, cot, sil, low, high, *refs):
    outs, wide = refs[:pieces], refs[pieces]
    count = cot.shape[1]
    own = count // pieces
    rows = cot.shape[0]
    wide[:, 0:HALO] = low[low.shape[0] - rows :, :]
    wide[:, HALO : HALO + count] = (cot[...].astype(F32) * sil[...].astype(F32)).astype(BF)
    wide[:, HALO + count :] = high[high.shape[0] - rows :, :]
    for s in range(pieces):
        outs[s][...] = wide[:, at((idx[1] ^ s) * own, own + 2 * HALO, LANES)]


def weight_kernel(pieces, blocks, idx, *refs):
    *parts, plain, dil_t, point_t = refs
    rows = parts[0].shape[0] // blocks
    part = rows // 2
    for s in range(pieces):
        start = (idx[1] ^ s) * rows
        if s < 2:
            for j in range(blocks):
                plain[j, at(start, rows, 16), :] = parts[s][j * rows : (j + 1) * rows, :]
            continue
        for number in range(2):
            source = parts[2 + 2 * (s - 2) + number]
            first = blocks * ((idx[0] ^ number) & 1)
            for q in range(blocks):
                place = first + q
                plain[
                    lax.div(place, 2), at(start + lax.rem(place, 2) * part, part, 16), :
                ] = source[q * part : (q + 1) * part, :]
    width = plain.shape[1]
    unit_matrix = jnp.where(eye_mask(width), 1.0, 0.0).astype(BF)
    for j in range(blocks):
        for k in range(5):
            turned = dot_rt(unit_matrix, plain[j, :, k * width : (k + 1) * width]).astype(BF)
            if k < 3:
                dil_t[j, :, k * width : (k + 1) * width] = turned
            else:
                point_t[j, :, (k - 3) * width : (k - 2) * width] = turned


def up_kernel(pieces, idx, *refs):
    mains, sides = refs[:pieces], refs[pieces : 2 * pieces]
    up_v, up_sq, up_g, up_b, frame_id, order = refs[2 * pieces : 2 * pieces + 6]
    outs = refs[2 * pieces + 6 : 3 * pieces + 6]
    act_hbm, up_hbm = refs[3 * pieces + 6 : 3 * pieces + 8]
    raw, stacked, phases, wide, act_out, up_w, held_v, held_order, *sems = refs[3 * pieces + 8 :]
    sems, out_sems = sems
    rows, frames = mains[0].shape
    local_out = up_v.shape[1]
    early = [
        pltpu.make_async_copy(up_v, held_v, sems.at[0]),
        pltpu.make_async_copy(order, held_order, sems.at[1]),
    ]
    for copy in early:
        copy.start()
    for s in range(pieces):
        here = at((idx[1] ^ s) * rows, rows, 16)
        raw[here, 0:LANES] = sides[s][:, 0:LANES]
        raw[here, LANES : LANES + frames] = mains[s][...]
        raw[here, LANES + frames :] = sides[s][:, LANES:]
    kept = [
        pltpu.make_async_copy(up_w, up_hbm, out_sems.at[0]),
        pltpu.make_async_copy(act_out, act_hbm, out_sems.at[1]),
    ]
    total = frames + 2 * LANES
    count = stacked.shape[1]
    channels = raw.shape[0]
    shift = total - (LANES - HALO // 8)
    ids = pltpu.roll(jnp.broadcast_to(frame_id[...], (8, total)), shift, axis=1)
    before = pltpu.roll(ids, 1, axis=1)
    after = pltpu.roll(ids, total - 1, axis=1)
    left = jnp.where(before == ids, 1.0, 0.0)[0:1, :].astype(BF)
    right = jnp.where(after == ids, 1.0, 0.0)[0:1, :].astype(BF)
    step = channels
    for r0 in range(0, channels, step):
        part = pl.ds(r0, step)
        acted = unit_act(raw[part, :].astype(F32)).astype(BF)
        act_out[part, :] = acted[:, LANES : LANES + frames]
        moved = pltpu.roll(acted, shift, axis=1)
        one = pltpu.roll(moved, 1, axis=1) * left
        two = pltpu.roll(moved, total - 1, axis=1) * right
        stacked[part, :] = moved[:, 0:count]
        stacked[pl.ds(channels + r0, step), :] = one[:, 0:count]
        stacked[pl.ds(2 * channels + r0, step), :] = two[:, 0:count]
    kept[1].start()
    early[0].wait()
    scale = up_g[...] / jnp.sqrt(up_sq[...])
    for k in range(up_v.shape[0]):
        up_w[k * local_out : (k + 1) * local_out, :] = (held_v[k] * scale).astype(BF)
    kept[0].start()
    eye = eye_mask(local_out)
    bias = to_col(up_b[...], eye)
    bias4 = jnp.concatenate([bias] * 4, axis=0)
    quarter = 4 * local_out
    for c0 in range(0, count, 3 * LANES):
        cols = pl.ds(c0, 3 * LANES)
        center = stacked[0:channels, cols]
        low = dot(up_w[quarter : 2 * quarter, :], center)
        low = low + dot(up_w[3 * quarter : 4 * quarter, :], stacked[channels : 2 * channels, cols])
        high = dot(up_w[2 * quarter : 3 * quarter, :], center)
        high = high + dot(up_w[0:quarter, :], stacked[2 * channels : 3 * channels, cols])
        low = (low + bias4).astype(BF)
        high = (high + bias4).astype(BF)
        for b in range(3):
            block = c0 // LANES + b
            if block * local_out >= phases.shape[0]:
                continue
            for r in range(8):
                source = (low, high)[r // 4]
                phases[block * local_out : (block + 1) * local_out, r * LANES : (r + 1) * LANES] = (
                    source[
                        (r % 4) * local_out : (r % 4 + 1) * local_out,
                        b * LANES : (b + 1) * LANES,
                    ]
                )
    early[1].wait()
    turned = dot(phases[...], held_order[...]).astype(BF)
    for block in range(count // LANES):
        wide[:, block * 1024 : (block + 1) * 1024] = turned[
            block * local_out : (block + 1) * local_out, :
        ]
    own = 8 * frames // pieces
    for s in range(pieces):
        outs[s][...] = wide[:, at((idx[1] ^ s) * own, own + 2 * HALO, LANES)]
    for copy in kept:
        copy.wait()


def sample_masks(sample_id, distance):
    width = sample_id.shape[1]
    ids = jnp.broadcast_to(sample_id[...], (8, width))
    back = pltpu.roll(ids, distance, axis=1)
    ahead = pltpu.roll(ids, width - distance, axis=1)
    return (
        jnp.where(back == ids, 1.0, 0.0)[0:1, :].astype(BF),
        jnp.where(ahead == ids, 1.0, 0.0)[0:1, :].astype(BF),
    )


def forward_kernel(pieces, blocks, idx, *refs):
    parts = refs[:pieces]
    plain, sample_id, silence = refs[pieces : pieces + 3]
    outs = refs[pieces + 3 : 2 * pieces + 3]
    kept = refs[2 * pieces + 3 : 2 * pieces + 8]
    hidden, taps, pair, final = refs[2 * pieces + 8 :]
    keep_h, keep_u, keep_m, keep_sh, keep_sc = kept
    rows, width = parts[0].shape
    channels = pieces * rows
    for s in range(pieces):
        hidden[at((idx[1] ^ s) * rows, rows, 16), :] = parts[s][...]
    for j in range(blocks):
        distance = 3**j
        tail = plain[j, :, 5 * channels : 5 * channels + TAIL].astype(F32)
        dil_b = tail[:, 0:1] + tail[:, 1:2]
        out_b = tail[:, 2:3] + tail[:, 3:4]

        low = hidden[...]
        keep_h[j] = low
        pair[channels : 2 * channels, :] = low
        acted, slope = unit(low.astype(F32))
        acted = acted.astype(BF)
        taps[channels : 2 * channels, :] = acted
        keep_u[j] = acted
        keep_sh[j] = slope.astype(BF)
        back, ahead = sample_masks(sample_id, distance)
        center = taps[channels : 2 * channels, :]
        taps[0:channels, :] = pltpu.roll(center, distance, axis=1) * back
        taps[2 * channels : 3 * channels, :] = pltpu.roll(center, width - distance, axis=1) * ahead

        inner = dot(plain[j, :, 0 : 3 * channels], taps[...]) + dil_b
        acted, slope = unit(inner)
        acted = acted.astype(BF)
        pair[0:channels, :] = acted
        keep_m[j] = acted
        keep_sc[j] = slope.astype(BF)
        after = dot(plain[j, :, 3 * channels : 5 * channels], pair[...]) + out_b
        if j < blocks - 1:
            hidden[...] = after.astype(BF)
        else:
            final[...] = after
    own = width - 2 * HALO
    voiced = silence[:, at(idx[1] * own, own, LANES)].astype(F32)
    for s in range(pieces):
        here = at((idx[1] ^ s) * rows, rows, 16)
        outs[s][...] = (final[here, HALO : HALO + own] * voiced).astype(BF)


def spread_taps(j, center, sample_id, taps):
    channels, width = center.shape
    distance = 3**j
    back, ahead = sample_masks(sample_id, distance)
    taps[channels : 2 * channels, :] = center
    taps[0:channels, :] = pltpu.roll(center, width - distance, axis=1) * ahead
    taps[2 * channels : 3 * channels, :] = pltpu.roll(center, distance, axis=1) * back


def edge_start(pieces, peer):
    return jnp.where(peer < pieces // 2, 0, HALO)


def backward_kernel(pieces, idx, *refs):
    parts = refs[:pieces]
    dil_t, point_t, sample_id, keep_sh, keep_sc = refs[pieces : pieces + 5]
    outs = refs[pieces + 5 : 2 * pieces + 5]
    errs, inners, taps, low = refs[2 * pieces + 5 :]
    rows = parts[0].shape[0]
    blocks, channels, width = errs.shape
    last = blocks - 1
    for s in range(pieces):
        errs[last, at((idx[1] ^ s) * rows, rows, 16), :] = parts[s][...]
    for j in reversed(range(blocks)):
        err = errs[j]
        inner = dot(point_t[j, :, 0:channels], err) * keep_sc[j].astype(F32)
        inner = inner.astype(BF)
        inners[j] = inner
        spread_taps(j, inner, sample_id, taps)
        spread = dot(dil_t[j], taps[...]) * keep_sh[j].astype(F32)
        after = (spread + dot(point_t[j, :, channels : 2 * channels], err)).astype(BF)
        if j > 0:
            errs[j - 1] = after
        else:
            low[...] = after
    lanes = at(edge_start(pieces, idx[1]), width - HALO, LANES)
    for s in range(pieces):
        outs[s][...] = low[at((idx[1] ^ s) * rows, rows, 16), lanes]


def grad_kernel(pieces, sequence, idx, errs, inners, sample_id, keep_h, keep_u, keep_m, *refs):
    keep, send, taps, mats = refs
    blocks, channels, width = errs.shape
    inside = pl.ds(HALO, width - 2 * HALO)
    rows = channels // pieces
    lane = lax.broadcasted_iota(jnp.int32, (channels, channels), 1)
    tail = jnp.zeros((channels, channels), F32)
    for j in range(blocks):
        spread_taps(j, inners[j], sample_id, taps)
        err = errs[j, :, inside]
        mats[5 * j + 3] = dot_rt(err, keep_m[j, :, inside]).astype(BF)
        mats[5 * j + 4] = dot_rt(err, keep_h[j, :, inside]).astype(BF)
        for k in range(3):
            mats[5 * j + k] = dot_rt(
                taps[k * channels : (k + 1) * channels, inside], keep_u[j, :, inside]
            ).astype(BF)
        dil_sum = jnp.sum(inners[j, :, inside].astype(F32), axis=1, keepdims=True)
        out_sum = jnp.sum(err.astype(F32), axis=1, keepdims=True)
        tail = tail + jnp.where(lane == 2 * j, dil_sum, 0.0)
        tail = tail + jnp.where(lane == 2 * j + 1, out_sum, 0.0)
    mats[5 * blocks] = tail.astype(BF)
    size = (5 * blocks + 1) * rows * pieces // len(sequence)
    part = min(size, rows)
    half = len(sequence) // 2
    for position, (s, t) in enumerate(sequence):
        target = (keep, send)[position // half]
        for q in range(size // part):
            place = (idx[0] ^ t) * (size // part) + q
            row = (idx[1] ^ s) * rows + lax.rem(place, rows // part) * part
            start = position % half * size + q * part
            target[start : start + part, :] = mats[
                lax.div(place, rows // part), at(row, part, 16), :
            ]


def halve_kernel(idx, keep, got, next_keep, next_send):
    half = next_keep.shape[0]
    total = keep[...].astype(F32) + got[...].astype(F32)
    next_keep[...] = total[:half].astype(BF)
    next_send[...] = total[half:].astype(BF)


def up_back_kernel(pieces, peers, orders, idx, *refs):
    parts = refs[:pieces]
    up_v, acted, frame_id, order = refs[pieces : pieces + 4]
    cols_grad, *streams = refs[pieces + 4 : pieces + 9]
    wide, stacked, phases, low_grad, held_v, held_act, held_order, sems = refs[pieces + 9 :]
    rows = parts[0].shape[0]
    own = parts[0].shape[1] - HALO
    length = pieces * own
    frames = length // 8
    late = []
    for source, target in ((order, held_order), (acted, held_act), (up_v, held_v)):
        late.append(pltpu.make_async_copy(source, target, sems.at[len(late)]))
        late[-1].start()
    wide[:, HALO + length :] = jnp.zeros((rows, wide.shape[1] - HALO - length), BF)
    for s in range(pieces):
        peer = idx[1] ^ s
        source = parts[s][:, at(HALO - edge_start(pieces, peer), own, LANES)]
        wide[:, at(HALO + peer * own, own, LANES)] = source

        @pl.when(peer == 0)
        def _():
            wide[:, 0:HALO] = parts[s][:, 0:HALO]

        @pl.when(peer == pieces - 1)
        def _():
            wide[:, HALO + length : 2 * HALO + length] = parts[s][:, own:]

    total = wide.shape[1] // 8
    blocks = total // LANES
    for block in range(blocks):
        stacked[block * rows : (block + 1) * rows, :] = wide[:, block * 1024 : (block + 1) * 1024]
    late[0].wait()
    turned = dot_rt(stacked[...], held_order[...]).astype(BF)
    for block in range(blocks):
        for r in range(8):
            phases[r * rows : (r + 1) * rows, block * LANES : (block + 1) * LANES] = turned[
                block * rows : (block + 1) * rows, r * LANES : (r + 1) * LANES
            ]
    ids = jnp.broadcast_to(frame_id[...], (8, frame_id.shape[1]))
    before = pltpu.roll(ids, 1, axis=1)
    after = pltpu.roll(ids, frame_id.shape[1] - 1, axis=1)
    inside = slice(LANES, LANES + frames)
    left = jnp.where(before == ids, 1.0, 0.0)[0:1, inside]
    right = jnp.where(after == ids, 1.0, 0.0)[0:1, inside]
    lead = HALO // 8
    eighth = 4 * rows
    sample_sum = jnp.zeros((rows, 1), F32)
    for part in range(2):
        base = phases[part * eighth : (part + 1) * eighth, :]
        center = pltpu.roll(base, total - lead, axis=1)[:, 0:frames]
        cols_grad[(4 + 4 * part) * rows : (8 + 4 * part) * rows, :] = center
        partial = jnp.sum(center.astype(F32), axis=1, keepdims=True)
        for r in range(4):
            sample_sum = sample_sum + partial[r * rows : (r + 1) * rows]
        if part == 1:
            moved = pltpu.roll(base, total - lead + 1, axis=1)[:, 0:frames]
            cols_grad[0:eighth, :] = (moved.astype(F32) * left).astype(BF)
        else:
            moved = pltpu.roll(base, total - lead - 1, axis=1)[:, 0:frames]
            cols_grad[12 * rows : 16 * rows, :] = (moved.astype(F32) * right).astype(BF)
    taps = up_v.shape[0]
    channels = up_v.shape[2]
    inner = jnp.zeros((rows, channels), F32)
    late[1].wait()
    grad = dot_rt(cols_grad[...], held_act[...])
    low_grad[...] = grad.astype(BF)
    late[2].wait()
    for k in range(taps):
        inner = inner + grad[k * rows : (k + 1) * rows] * held_v[k]
    inner = jnp.sum(inner, axis=0, keepdims=True)
    bias = jnp.concatenate(
        [to_row(sample_sum, eye_mask(rows)), jnp.zeros((1, channels - rows), F32)], axis=1
    )
    side = channels // 2
    line = lax.broadcasted_iota(jnp.int32, (SUMS, side), 0)
    sums = jnp.zeros((SUMS, side), F32)
    for number, value in enumerate((inner[:, :side], inner[:, side:], bias[:, :side])):
        high = value.astype(BF).astype(F32)
        sums = sums + jnp.where(line == 2 * number, high, 0.0)
        sums = sums + jnp.where(line == 2 * number + 1, value - high, 0.0)
    half = peers // 2
    size = taps * rows // peers
    first = (streams[0].shape[0] - SUMS) // half
    second = 2 * size - first
    streams[0][half * first :, :] = sums.astype(BF)
    streams[1][half * first :, :] = sums.astype(BF)
    for position, s in enumerate(orders[0]):
        target = streams[position // half]
        start = position % half * first
        target[start : start + first, :] = low_grad[at((idx[0] ^ s) * size, first, 16), 0:side]
    for position, s in enumerate(orders[1]):
        target = streams[2 + position // half]
        start = position % half * second
        piece = (idx[0] ^ s) * size
        target[start : start + size, :] = low_grad[at(piece, size, 16), side:]
        if size > first:
            target[start + size : start + second, :] = low_grad[
                at(piece + first, size - first, 16), 0:side
            ]


def input_back_kernel(pieces, order, idx, up_w, cols_grad, keep, send, total):
    total[...] = lax.dot_general(
        up_w[...], cols_grad[...], (((0,), (0,)), ((), ())), preferred_element_type=F32
    ).astype(BF)
    size = total.shape[0] // pieces
    for position, s in enumerate(order):
        target = (keep, send)[position // (pieces // 2)]
        start = position % (pieces // 2) * size
        target[start : start + size, :] = total[at((idx[1] ^ s) * size, size, 16), :]


def join_kernel(idx, keep, got, term, other, next_keep, next_send):
    rows = keep.shape[0] - SUMS
    half, part = rows // 2, term.shape[0] // 2
    total = keep[...].astype(F32) + got[...].astype(F32)
    grads = (term[...].astype(F32) + other[...].astype(F32)).astype(BF)
    for number, target in enumerate((next_keep, next_send)):
        target[0:half, :] = total[number * half : (number + 1) * half].astype(BF)
        target[half : half + part, :] = grads[number * part : (number + 1) * part]
        target[half + part :, :] = total[rows:].astype(BF)


def step_kernel(rows, idx, keep, got, *outs):
    total = keep[...].astype(F32) + got[...].astype(F32)
    grads = total.shape[0] - rows - SUMS
    for number, target in enumerate(outs):
        half, part = rows // 2, grads // 2
        target[0:half, :] = total[number * half : (number + 1) * half].astype(BF)
        start = rows + number * part
        target[half : half + part, :] = total[start : start + part].astype(BF)
        target[half + part :, :] = total[rows + grads :].astype(BF)


def meet_kernel(parts, idx, own, got, out, *sums):
    start = 0
    for count in parts:
        half = count // 2
        for number in range(2):
            here = start + number * half
            there = start + (1 - number) * half
            out[here : here + half, :] = (
                own[here : here + half, :].astype(F32) + got[there : there + half, :].astype(F32)
            ).astype(BF)
        start = start + count
    if sums:
        sums[0][...] = own[start:, :].astype(F32) + got[start:, :].astype(F32)


def whole_kernel(rows, joined, idx, keep, got, *refs):
    *terms, out = refs
    total = keep[...].astype(F32) + got[...].astype(F32)
    if not joined:
        out[...] = total.astype(BF)
        return
    count = terms[0].shape[0]
    out[0:rows, :] = total[0:rows].astype(BF)
    out[rows : rows + count, :] = (terms[0][...].astype(F32) + terms[1][...].astype(F32)).astype(BF)
    out[rows + count :, :] = total[rows:].astype(BF)


def double_kernel(rows, idx, own, got, out):
    grads = own.shape[0] - rows
    out[0:rows, :] = own[0:rows, :]
    out[rows : 2 * rows, :] = got[0:rows, :]
    out[2 * rows : 2 * rows + grads, :] = own[rows:, :]
    out[2 * rows + grads :, :] = got[rows:, :]


def final_kernel(orders, first, idx, *refs):
    streams = refs[:4]
    up_v, up_sq, up_g, inner_sum, dil_v, dil_g, mix_v, mix_g, skip_v, skip_g = refs[4:14]
    up_v_grad, up_g_grad, *outs = refs[14:24]
    whole, blocks_whole, staged, *block_staged, out_sems = refs[24:]
    half = len(orders[0]) // 2
    size = whole.shape[0] // (2 * half)
    side = whole.shape[1] // 2
    second = 2 * size - first
    for position, s in enumerate(orders[0]):
        start = position % half * first
        whole[at((idx[0] ^ s) * size, first, 16), 0:side] = streams[position // half][
            start : start + first, :
        ]
    for position, s in enumerate(orders[1]):
        source = streams[2 + position // half]
        start = position % half * second
        piece = (idx[0] ^ s) * size
        whole[at(piece, size, 16), side:] = source[start : start + size, :]
        if size > first:
            whole[at(piece + first, size - first, 16), 0:side] = source[
                start + size : start + second, :
            ]
    size = blocks_whole.shape[0] // (2 * half)
    for position, s in enumerate(orders[0]):
        start = half * first + position % half * size
        blocks_whole[at((idx[0] ^ s) * size, size, 16), :] = streams[position // half][
            start : start + size, :
        ]
    sent = []

    def ship(source, target):
        sent.append(pltpu.make_async_copy(source, target, out_sems.at[len(sent)]))
        sent[-1].start()

    norm = jnp.sqrt(up_sq[...])
    inner = inner_sum[...]
    scale = up_g[...] / norm
    pull = up_g[...] * inner / (norm * norm * norm)
    rows = up_v.shape[1]
    for k in range(up_v.shape[0]):
        grad = whole[k * rows : (k + 1) * rows, :].astype(F32)
        staged[k] = scale * grad - pull * up_v[k]
        ship(staged.at[k], up_v_grad.at[k])
    up_g_grad[...] = inner / norm
    dil_v_hbm, dil_g_out, dil_b_out, mix_v_hbm, mix_g_out, out_b_out, skip_v_hbm, skip_g_out = outs
    dil_v_out, mix_v_out, skip_v_out = block_staged
    eye = eye_mask(rows)
    blocks = dil_v.shape[0]
    tail = blocks_whole[5 * blocks * rows :, :].astype(F32)
    for j in range(blocks):

        def mat(m):
            start = (5 * j + m) * rows
            return blocks_whole[start : start + rows, :].astype(F32)

        square = jnp.zeros((rows, 1), F32)
        inner = jnp.zeros((rows, 1), F32)
        for k in range(3):
            v = dil_v[j, k]
            square = square + jnp.sum(v * v, axis=1, keepdims=True)
            inner = inner + jnp.sum(v * mat(k), axis=1, keepdims=True)
        norm = jnp.sqrt(square)
        gain = to_col(dil_g[j : j + 1, :], eye)
        for k in range(3):
            dil_v_out[j, k] = gain / norm * mat(k) - gain * inner / (norm**3) * dil_v[j, k]
        ship(dil_v_out.at[j], dil_v_hbm.at[j])
        dil_g_out[j : j + 1, :] = to_row(inner / norm, eye)
        for number, (vref, gref, v_out, v_hbm, g_out) in enumerate(
            (
                (mix_v, mix_g, mix_v_out, mix_v_hbm, mix_g_out),
                (skip_v, skip_g, skip_v_out, skip_v_hbm, skip_g_out),
            )
        ):
            v = vref[j]
            grad = mat(3 + number)
            norm = jnp.sqrt(jnp.sum(v * v, axis=1, keepdims=True))
            inner = jnp.sum(v * grad, axis=1, keepdims=True)
            gain = to_col(gref[j : j + 1, :], eye)
            v_out[j] = gain / norm * grad - gain * inner / (norm**3) * v
            ship(v_out.at[j], v_hbm.at[j])
            g_out[j : j + 1, :] = to_row(inner / norm, eye)
        dil_b_out[j : j + 1, :] = to_row(tail[:, 2 * j : 2 * j + 1], eye)
        out_b_out[j : j + 1, :] = to_row(tail[:, 2 * j + 1 : 2 * j + 2], eye)
    for copy in sent:
        copy.wait()


def place_kernel(pieces, idx, *refs):
    parts, out = refs[:pieces], refs[pieces]
    own = parts[0].shape[1]
    for s in range(pieces):
        out[:, at((idx[1] ^ s) * own, own, LANES)] = parts[s][...]


def stage_kernel(idx, *refs):
    *pairs, sems = refs
    half = len(pairs) // 2
    fetch(list(zip(pairs[:half], pairs[half:])), sems)


def input_kernel(idx, *refs):
    *terms, spectrogram, out = refs
    total = terms[0][...].astype(F32)
    for term in terms[1:]:
        total = total + term[...].astype(F32)
    out[...] = (total * unit(spectrogram[...].astype(F32))[1]).astype(BF)


def local(
    spectrogram_input,
    upsample_direction,
    upsample_magnitude,
    upsample_bias,
    dilated_direction,
    dilated_magnitude,
    dilated_bias,
    pointwise_direction,
    pointwise_magnitude,
    block_output_bias,
    shortcut_direction,
    shortcut_magnitude,
    cotangent,
    silence,
    segments,
):
    pieces, peers = lax.axis_size("chan"), lax.axis_size("tm")
    chan, tm = lax.axis_index("chan"), lax.axis_index("tm")
    in_rows, frames = spectrogram_input.shape
    taps, rows, in_channels = upsample_direction.shape
    blocks = dilated_direction.shape[0]
    channels = dilated_direction.shape[3]
    length = 8 * frames
    own = length // pieces
    width = own + 2 * HALO
    packed_width = 5 * channels + TAIL
    forward = [(k, k + 1) for k in range(peers - 1)]
    backward = [(k + 1, k) for k in range(peers - 1)]
    dma = pltpu.SemaphoreType.DMA
    lead = HALO // 8
    tie = lax.optimization_barrier

    spread = np.arange(8 * LANES)
    order = np.zeros((8 * LANES, 8 * LANES), np.float32)
    order[spread, 8 * (spread % LANES) + spread // LANES] = 1.0
    order = jnp.asarray(order, BF)

    silence_row = silence.reshape(1, length)
    up_g = upsample_magnitude.reshape(1, in_channels)
    edge_rows = in_rows + rows
    ahead, behind = kernel_call(
        edge_kernel,
        [((edge_rows, LANES), BF, "V")] * 2,
        [spectrogram_input, cotangent, silence_row],
        "HHH",
        scratch=[
            pltpu.VMEM((in_rows, LANES), BF),
            pltpu.VMEM((in_rows, LANES), BF),
            pltpu.VMEM((2, rows, HALO), BF),
            pltpu.VMEM((2, 1, HALO), jnp.int32),
            dma((6,)),
        ],
    )
    low_edge = lax.ppermute(ahead, "tm", forward)
    high_edge = lax.ppermute(behind, "tm", backward)
    all_mains = gather_chan(spectrogram_input)
    (up_sq,) = kernel_call(
        square_kernel, [((1, in_channels), F32, "V")], [upsample_direction], "F", micros=2
    )
    block_args = [
        dilated_direction,
        dilated_magnitude,
        dilated_bias,
        pointwise_direction,
        pointwise_magnitude,
        block_output_bias,
        shortcut_direction,
        shortcut_magnitude,
    ]
    sides = jnp.concatenate([low_edge[:in_rows], high_edge[:in_rows]], axis=1)
    block_args, sides = tie((block_args, sides))
    packed_half = ((blocks * rows // 2, packed_width), BF, "V")
    bias_in = upsample_bias.reshape(1, rows)
    packed, near, far, up_g, bias_in = kernel_call(
        prep_kernel,
        [((blocks * rows, packed_width), BF, "V"), packed_half, packed_half]
        + [((1, in_channels), F32, "R"), ((1, rows), F32, "R")],
        [*block_args, up_g, bias_in],
        "FFFFFFFFFF",
        micros=3,
    )
    held_sides = {0: sides}
    for bit in reversed(bits_of(pieces)[1:]):
        for slot in list(held_sides):
            held_sides[slot ^ bit] = swap(held_sides[slot], "chan", bit)
    near, held_sides = tie((near, held_sides))
    for slot in list(held_sides):
        held_sides[slot ^ 1] = swap(held_sides[slot], "chan", 1)
    all_sides = [held_sides[slot] for slot in range(pieces)]
    for bit in bits_of(pieces):
        up_sq = up_sq + swap(up_sq, "chan", bit)
    padded_ids = jnp.pad(segments.astype(F32), LANES, constant_values=-1.0)
    frame_id = lax.dynamic_slice_in_dim(padded_ids, tm * frames, frames + 2 * LANES)
    sample_id = jnp.repeat(
        lax.dynamic_slice_in_dim(
            padded_ids, LANES + tm * frames + chan * (own // 8) - lead, width // 8
        ),
        8,
    ).reshape(1, width)
    frame_id = frame_id.reshape(1, frames + 2 * LANES)
    top = pieces // 2
    near, all_sides[top], up_sq = tie((near, all_sides[top], up_sq))

    count = -(-(frames + 2 * lead) // LANES) * LANES
    count = -(-count // (3 * LANES)) * 3 * LANES
    up_outs = kernel_call(
        functools.partial(up_kernel, pieces),
        [((rows, width), BF, "R")]
        + [((rows, width), BF, "V")] * (pieces - 1)
        + [((in_channels, frames), BF, "H"), ((taps * rows, in_channels), BF, "H")],
        all_mains
        + all_sides
        + [upsample_direction, up_sq, up_g, bias_in, frame_id, order],
        "V" * (2 * pieces) + "HVRRVH",
        scratch=[
            pltpu.VMEM((in_channels, frames + 2 * LANES), BF),
            pltpu.VMEM((3 * in_channels, count), BF),
            pltpu.VMEM((count // LANES * rows, 8 * LANES), BF),
            pltpu.VMEM((rows, 8 * count), BF),
            pltpu.VMEM((in_channels, frames), BF),
            pltpu.VMEM((taps * rows, in_channels), BF),
            pltpu.VMEM(upsample_direction.shape, F32),
            pltpu.VMEM(order.shape, BF),
            dma((2,)),
            dma((2,)),
        ],
        micros=6,
    )
    acted, up_w = up_outs[pieces:]
    chan_bits = bits_of(pieces)
    held_near = {0: near}
    for bit in reversed(chan_bits[1:]):
        for slot in list(held_near):
            held_near[slot ^ bit] = swap(held_near[slot], "chan", bit)
    hidden_parts, held_near, low_edge = tie((list(up_outs[:pieces]), held_near, low_edge))
    cut = kernel_call(
        functools.partial(cut_kernel, pieces),
        [((rows, width), BF, "R")] + [((rows, width), BF, "V")] * (pieces - 1),
        [cotangent, silence_row, low_edge, high_edge],
        "FFVV",
        scratch=[pltpu.VMEM((rows, length + 2 * HALO), BF)],
        micros=2,
    )
    all_hidden = exchange_chan(hidden_parts)
    all_packed = [packed, swap(packed, "chan", 1)]
    for slot in range(2, pieces, 2):
        two = [held_near[slot], swap(held_near[slot], "tm", 1)]
        two, all_hidden[top], cut = tie((two, all_hidden[top], list(cut)))
        all_packed += two + [swap(value, "chan", 1) for value in two]

    plain, dil_t, point_t = kernel_call(
        functools.partial(weight_kernel, pieces, blocks),
        [
            ((blocks, channels, packed_width), BF, "R"),
            ((blocks, channels, 3 * channels), BF, "R"),
            ((blocks, channels, 2 * channels), BF, "R"),
        ],
        all_packed,
        "V" * len(all_packed),
        micros=0.1,
    )
    cut, plain = tie((list(cut), plain))
    all_err = exchange_chan(cut)

    kept_shape = ((blocks, channels, width), BF, "R")
    forward_outs = kernel_call(
        functools.partial(forward_kernel, pieces, blocks),
        [((rows, own), BF, "V")] * pieces + [kept_shape] * 5,
        all_hidden + [plain, sample_id, silence_row],
        "R" + "V" * (pieces - 1) + "RVF",
        scratch=[
            pltpu.VMEM((channels, width), BF),
            pltpu.VMEM((3 * channels, width), BF),
            pltpu.VMEM((2 * channels, width), BF),
            pltpu.VMEM((channels, width), F32),
        ],
        micros=10,
    )
    keep_h, keep_u, keep_m, keep_sh, keep_sc = forward_outs[pieces:]
    activation_parts = list(forward_outs[:pieces])

    backward_outs = kernel_call(
        functools.partial(backward_kernel, pieces),
        [((rows, width - HALO), BF, "V")] * pieces + [kept_shape] * 2,
        all_err + [dil_t, point_t, sample_id, keep_sh, keep_sc],
        "R" + "V" * (pieces - 1) + "RRVRR",
        scratch=[
            pltpu.VMEM((3 * channels, width), BF),
            pltpu.VMEM((channels, width), BF),
        ],
        micros=10,
    )
    errs, inners = backward_outs[pieces:]
    all_low = exchange_chan(list(backward_outs[:pieces]))

    chan_order = order_of(chan_bits)
    tm_bits = bits_of(peers)
    path = [("chan", 1), ("tm", 1)] + [("chan", bit) for bit in chan_bits[1:]]
    path_order = [(0, 0)]
    for axis, bit in reversed(path + [("tm", bit) for bit in tm_bits[1:]]):
        other = [
            (s + bit, t) if axis == "chan" else (s, t + bit) for s, t in path_order
        ]
        path_order = path_order + other
    mats = 5 * blocks + 1
    share = pieces // 2 * mats * rows
    keep, send = kernel_call(
        functools.partial(grad_kernel, pieces, path_order),
        [((share, channels), BF, "V")] * 2,
        [errs, inners, sample_id, keep_h, keep_u, keep_m],
        "RRVRRR",
        scratch=[
            pltpu.VMEM((3 * channels, width), BF),
            pltpu.VMEM((mats, channels, channels), BF),
        ],
        micros=0.1,
    )

    def scatter(keep, send, path):
        for axis, bit in path[:-1]:
            got = swap(send, axis, bit)
            next_shape = ((keep.shape[0] // 2, keep.shape[1]), BF, "V")
            keep, send = kernel_call(halve_kernel, [next_shape] * 2, [keep, got], "VV")
        return keep, swap(send, *path[-1])

    keep, send, all_low[top] = tie((keep, send, all_low[top]))
    got = swap(send, *path[0])
    keep, send = kernel_call(
        halve_kernel, [((share // 2, channels), BF, "V")] * 2, [keep, got], "VV"
    )
    block_terms = scatter(keep, send, path[1:])
    send, all_low = tie((send, all_low))

    turned_bits = tm_bits[1:] + tm_bits[:1]
    orders = (order_of(tm_bits), order_of(turned_bits))
    half = peers // 2
    total_rows = taps * rows
    size = total_rows // peers
    side = in_channels // 2
    first = max(16, size // 2 // 16 * 16)
    second = 2 * size - first
    cols_grad, keep_one, send_one, keep_two, send_two = kernel_call(
        functools.partial(up_back_kernel, pieces, peers, orders),
        [((total_rows, frames), BF, "R")]
        + [((half * first + SUMS, side), BF, "V")] * 2
        + [((half * second, side), BF, "V")] * 2,
        all_low + [upsample_direction, acted, frame_id, order],
        "V" * pieces + "HHVH",
        scratch=[
            pltpu.VMEM((rows, 8 * count), BF),
            pltpu.VMEM((count // LANES * rows, 8 * LANES), BF),
            pltpu.VMEM((8 * rows, count), BF),
            pltpu.VMEM((total_rows, in_channels), BF),
            pltpu.VMEM(upsample_direction.shape, F32),
            pltpu.VMEM((in_channels, frames), BF),
            pltpu.VMEM(order.shape, BF),
            dma((3,)),
        ],
        micros=5,
    )

    piece_rows = pieces // 2 * in_rows
    keep, send = kernel_call(
        functools.partial(input_back_kernel, pieces, chan_order),
        [((piece_rows, frames), BF, "V")] * 2,
        [up_w, cols_grad],
        "FR",
        scratch=[pltpu.VMEM((in_channels, frames), BF)],
        micros=3,
    )
    steps = len(tm_bits)
    block_rows = mats * rows
    one_rows, two_rows = half * first, half * second
    for step in range(steps - 1):
        got_one = swap(send_one, "tm", tm_bits[step])
        got_two = swap(send_two, "tm", turned_bits[step])
        if step == 0:
            got_one, got_two, keep, send = tie((got_one, got_two, keep, send))
            activation_parts, got_one = tie((activation_parts, got_one))
            activation_parts = exchange_chan(activation_parts)
            input_terms = scatter(keep, send, [("chan", bit) for bit in chan_bits])
        else:
            got_one, got_two = tie((got_one, got_two))
        one_rows, two_rows, block_rows = one_rows // 2, two_rows // 2, block_rows // 2
        if step < steps - 2:
            next_shape = ((one_rows + block_rows // 2 + SUMS, side), BF, "V")
            if step == 0:
                keep_one, send_one = kernel_call(
                    join_kernel, [next_shape] * 2, [keep_one, got_one, *block_terms], "VVVV"
                )
            else:
                keep_one, send_one = kernel_call(
                    functools.partial(step_kernel, 2 * one_rows),
                    [next_shape] * 2,
                    [keep_one, got_one],
                    "VV",
                )
            keep_two, send_two = kernel_call(
                halve_kernel, [((two_rows, side), BF, "V")] * 2, [keep_two, got_two], "VV"
            )
    joined = steps == 2
    one_rows, two_rows = 2 * one_rows, 2 * two_rows
    (held_one,) = kernel_call(
        functools.partial(whole_kernel, one_rows, joined),
        [((one_rows + block_rows + SUMS, side), BF, "V")],
        [keep_one, got_one, *(block_terms if joined else ())],
        "VVVV" if joined else "VV",
    )
    (held_two,) = kernel_call(
        functools.partial(whole_kernel, two_rows, False),
        [((two_rows, side), BF, "V")],
        [keep_two, got_two],
        "VV",
    )
    got_one = swap(held_one, "tm", tm_bits[-1])
    got_two = swap(held_two, "tm", turned_bits[-1])
    got_one, got_two, input_terms = tie((got_one, got_two, input_terms))
    own_one, sums = kernel_call(
        functools.partial(meet_kernel, (one_rows, block_rows)),
        [((one_rows + block_rows, side), BF, "V"), ((SUMS, side), F32, "V")],
        [held_one, got_one],
        "VV",
    )
    (own_two,) = kernel_call(
        functools.partial(meet_kernel, (two_rows,)),
        [((two_rows, side), BF, "V")],
        [held_two, got_two],
        "VV",
    )
    for step in reversed(range(steps - 1)):
        got_one = swap(own_one, "tm", tm_bits[step])
        got_two = swap(own_two, "tm", turned_bits[step])
        if step == steps - 2:
            got_one, got_two, activation_parts = tie((got_one, got_two, activation_parts))
        else:
            got_one, got_two = tie((got_one, got_two))
        if step > 0:
            (own_one,) = kernel_call(
                functools.partial(double_kernel, one_rows),
                [((2 * own_one.shape[0], side), BF, "V")],
                [own_one, got_one],
                "VV",
            )
            one_rows = 2 * one_rows
            own_two = jnp.concatenate([own_two, got_two], axis=0)

    pair = sums[0:6:2] + sums[1:6:2]
    inner_sum = pair[0:2].reshape(1, in_channels)
    for bit in chan_bits:
        inner_sum = inner_sum + swap(inner_sum, "chan", bit)

    (input_grad,) = kernel_call(
        input_kernel,
        [((in_rows, frames), BF, "V")],
        [*input_terms, spectrogram_input],
        "VVF",
    )
    (activation,) = kernel_call(
        functools.partial(place_kernel, pieces),
        [((rows, length), BF, "V")],
        activation_parts,
        "V" * pieces,
        micros=2,
    )

    late_args = [
        upsample_direction,
        dilated_direction,
        dilated_magnitude,
        pointwise_direction,
        pointwise_magnitude,
        shortcut_direction,
        shortcut_magnitude,
    ]
    late_args, sums = tie((late_args, sums))
    staged = kernel_call(
        stage_kernel,
        [(arg.shape, arg.dtype, "R") for arg in late_args],
        late_args,
        "H" * len(late_args),
        scratch=[dma((len(late_args),))],
        micros=2,
    )
    final_outs = kernel_call(
        functools.partial(final_kernel, orders, first),
        [
            (upsample_direction.shape, F32, "H"),
            ((1, in_channels), F32, "V"),
            (dilated_direction.shape, F32, "H"),
            (dilated_magnitude.shape, F32, "V"),
            (dilated_bias.shape, F32, "V"),
            (pointwise_direction.shape, F32, "H"),
            (pointwise_magnitude.shape, F32, "V"),
            (block_output_bias.shape, F32, "V"),
            (shortcut_direction.shape, F32, "H"),
            (shortcut_magnitude.shape, F32, "V"),
        ],
        [
            own_one,
            got_one,
            own_two,
            got_two,
            staged[0],
            up_sq,
            up_g,
            inner_sum,
            *staged[1:],
        ],
        "VVVVRVRVRRRRRR",
        scratch=[
            pltpu.VMEM((total_rows, in_channels), BF),
            pltpu.VMEM((mats * rows, channels), BF),
            pltpu.VMEM(upsample_direction.shape, F32),
            pltpu.VMEM(dilated_direction.shape, F32),
            pltpu.VMEM(pointwise_direction.shape, F32),
            pltpu.VMEM(shortcut_direction.shape, F32),
            dma((taps + 3 * blocks,)),
        ],
        micros=5,
    )
    up_v_grad, up_g_grad, dil_v_grad, dil_g_grad, dil_b_grad = final_outs[:5]
    mix_v_grad, mix_g_grad, out_b_grad, skip_v_grad, skip_g_grad = final_outs[5:]
    return (
        activation,
        input_grad,
        up_v_grad,
        up_g_grad.reshape(in_channels),
        pair[2, :rows],
        dil_v_grad,
        dil_g_grad,
        dil_b_grad,
        mix_v_grad,
        mix_g_grad,
        out_b_grad,
        skip_v_grad,
        skip_g_grad,
    )


def solution(mesh):
    placed = (
        P("chan", "tm"),
        P(None, "chan", None),
        P(),
        P("chan"),
        P(None, None, "chan", None),
        P(None, "chan"),
        P(None, "chan"),
        P(None, "chan", None),
        P(None, "chan"),
        P(None, "chan"),
        P(None, "chan", None),
        P(None, "chan"),
        P("chan", "tm"),
        P("tm"),
        P(),
    )
    return jax.shard_map(
        local,
        mesh=mesh,
        in_specs=placed,
        out_specs=(
            P("chan", "tm"),
            P("chan", "tm"),
            P(None, "chan", None),
            P(),
            P("chan"),
            P(None, None, "chan", None),
            P(None, "chan"),
            P(None, "chan"),
            P(None, "chan", None),
            P(None, "chan"),
            P(None, "chan"),
            P(None, "chan", None),
            P(None, "chan"),
        ),
        check_vma=False,
    )
```

```python
import functools

import jax
import jax.numpy as jnp
import numpy as np
from jax import lax
from jax.experimental import pallas as pl
from jax.experimental.pallas import tpu as pltpu
from jax.sharding import PartitionSpec as P

BF = jnp.bfloat16
F32 = jnp.float32
LANES = 128
HALO = 128
TAIL = 128
SUMS = 16
VMEM_LIMIT = 20 * 1024 * 1024


def swap(values, axis, bit):
    count = lax.axis_size(axis)
    return lax.ppermute(values, axis, [(k, k ^ bit) for k in range(count)])


def bits_of(count):
    bits = []
    bit = 1
    while bit < count:
        bits.append(bit)
        bit = 2 * bit
    return bits


def order_of(bits):
    order = [0]
    for bit in reversed(bits):
        order = order + [slot + bit for slot in order]
    return order


def gather_chan(own):
    held = {0: own}
    for bit in reversed(bits_of(lax.axis_size("chan"))):
        for slot in list(held):
            held[slot ^ bit] = swap(held[slot], "chan", bit)
    return [held[slot] for slot in range(len(held))]


def exchange_chan(pieces):
    return [pieces[0]] + [swap(pieces[s], "chan", s) for s in range(1, len(pieces))]


HBM = pl.BlockSpec(memory_space=pltpu.HBM)
VMEM = pl.BlockSpec(memory_space=pltpu.VMEM)


def kernel_call(body, outs, args, specs, scratch=(), micros=1.0):
    held = []
    in_specs = []
    operands = []
    for arg, spec in zip(args, specs, strict=True):
        in_specs.append({"H": HBM, "F": HBM, "R": VMEM, "V": VMEM}[spec])
        if spec == "F":
            held.append(pltpu.VMEM(arg.shape, arg.dtype))
        if spec == "R":
            arg = pltpu.with_memory_space_constraint(arg, pltpu.VMEM)
        if spec in "HF":
            arg = pltpu.with_memory_space_constraint(arg, pltpu.HBM)
        operands.append(arg)
    out_shape = []
    out_specs = []
    for shape, dtype, spec in outs:
        out_specs.append(HBM if spec == "H" else VMEM)
        spaced = {"R": pltpu.VMEM, "H": pltpu.HBM, "V": jax.ShapeDtypeStruct}[spec]
        out_shape.append(spaced(shape, dtype))
    fetched = len(held)

    def wrapped(*refs):
        refs = list(refs)
        if fetched:
            sems = refs.pop()
            targets = refs[-fetched:]
            refs = refs[:-fetched]
            sources = [number for number, spec in enumerate(specs) if spec == "F"]
            fetch([(refs[n], target) for n, target in zip(sources, targets)], sems)
            for n, target in zip(sources, targets):
                refs[n] = target
        body((lax.axis_index("tm"), lax.axis_index("chan")), *refs)

    extra = held + ([pltpu.SemaphoreType.DMA((fetched,))] if fetched else [])
    return pl.pallas_call(
        wrapped,
        out_shape=tuple(out_shape),
        in_specs=in_specs,
        out_specs=tuple(out_specs),
        scratch_shapes=list(scratch) + extra,
        compiler_params=pltpu.CompilerParams(vmem_limit_bytes=VMEM_LIMIT),
        cost_estimate=pl.CostEstimate(
            flops=int(micros * 1.1e9), bytes_accessed=0, transcendentals=0
        ),
    )(*operands)


def fetch(pairs, sems):
    copies = [
        pltpu.make_async_copy(source, target, sems.at[number])
        for number, (source, target) in enumerate(pairs)
    ]
    for copy in copies:
        copy.start()
    for copy in copies:
        copy.wait()


def unit(values):
    th = jnp.tanh(0.5 * values)
    base = 0.6 + 0.4 * th
    return values * base, base + 0.2 * values * (1.0 - th * th)


def unit_act(values):
    return values * (0.6 + 0.4 * jnp.tanh(0.5 * values))


def dot(left, right):
    return lax.dot_general(left, right, (((1,), (0,)), ((), ())), preferred_element_type=F32)


def dot_rt(left, right):
    return lax.dot_general(left, right, (((1,), (1,)), ((), ())), preferred_element_type=F32)


def eye_mask(count):
    rows = lax.broadcasted_iota(jnp.int32, (count, count), 0)
    cols = lax.broadcasted_iota(jnp.int32, (count, count), 1)
    return rows == cols


def to_col(row, eye):
    return jnp.sum(jnp.where(eye, row, 0.0), axis=1, keepdims=True)


def to_row(col, eye):
    return jnp.sum(jnp.where(eye, col, 0.0), axis=0, keepdims=True)


def at(start, size, step):
    return pl.ds(pl.multiple_of(start, step), size)


def edge_kernel(idx, spectrogram, cot, sil, ahead, behind, front, back, sound, mask, sems):
    rows = spectrogram.shape[0]
    frames, count = spectrogram.shape[1], cot.shape[1]
    low, high = pl.ds(0, HALO), pl.ds(count - HALO, HALO)
    fetch(
        [
            (spectrogram.at[:, frames - LANES :], front),
            (spectrogram.at[:, :LANES], back),
            (cot.at[:, high], sound.at[0]),
            (cot.at[:, low], sound.at[1]),
            (sil.at[:, high], mask.at[0]),
            (sil.at[:, low], mask.at[1]),
        ],
        sems,
    )
    ahead[0:rows, :] = front[...]
    behind[0:rows, :] = back[...]
    ahead[rows:, :] = (sound[0].astype(F32) * mask[0].astype(F32)).astype(BF)
    behind[rows:, :] = (sound[1].astype(F32) * mask[1].astype(F32)).astype(BF)


def square_kernel(idx, up_v, up_sq):
    total = jnp.zeros((up_v.shape[1], up_v.shape[2]), F32)
    for k in range(up_v.shape[0]):
        rows = up_v[k]
        total = total + rows * rows
    up_sq[...] = jnp.sum(total, axis=0, keepdims=True)


def prep_kernel(
    idx, dil_v, dil_g, dil_b, mix_v, mix_g, out_b, skip_v, skip_g, up_g, up_b, packed, near, far, up_row, bias_row
):
    up_row[...] = up_g[...]
    bias_row[...] = up_b[...]
    local_out = dil_v.shape[2]
    eye = eye_mask(local_out)
    lane = lax.broadcasted_iota(jnp.int32, (local_out, TAIL), 1)
    width = dil_v.shape[3]
    for j in range(dil_v.shape[0]):
        rows = pl.ds(j * local_out, local_out)
        square = jnp.zeros((local_out, 1), F32)
        for k in range(3):
            v = dil_v[j, k]
            square = square + jnp.sum(v * v, axis=1, keepdims=True)
        norm = jnp.sqrt(square)
        scale = to_col(dil_g[j : j + 1, :], eye) / norm
        for k in range(3):
            packed[rows, k * width : (k + 1) * width] = (dil_v[j, k] * scale).astype(BF)
        for number, (vref, gref) in enumerate(((mix_v, mix_g), (skip_v, skip_g))):
            v = vref[j]
            norm = jnp.sqrt(jnp.sum(v * v, axis=1, keepdims=True))
            scale = to_col(gref[j : j + 1, :], eye) / norm
            packed[rows, (3 + number) * width : (4 + number) * width] = (v * scale).astype(BF)
        first = to_col(dil_b[j : j + 1, :], eye)
        second = to_col(out_b[j : j + 1, :], eye)
        high_one = first.astype(BF).astype(F32)
        high_two = second.astype(BF).astype(F32)
        tail = jnp.where(lane == 0, high_one, 0.0) + jnp.where(lane == 1, first - high_one, 0.0)
        tail = tail + jnp.where(lane == 2, high_two, 0.0)
        tail = tail + jnp.where(lane == 3, second - high_two, 0.0)
        packed[rows, 5 * width : 5 * width + TAIL] = tail.astype(BF)
    half = near.shape[0]
    for number, target in enumerate((near, far)):
        target[...] = packed[at(((idx[0] ^ number) & 1) * half, half, 16), :]


def cut_kernel(pieces, idx, cot, sil, low, high, *refs):
    outs, wide = refs[:pieces], refs[pieces]
    count = cot.shape[1]
    own = count // pieces
    rows = cot.shape[0]
    wide[:, 0:HALO] = low[low.shape[0] - rows :, :]
    wide[:, HALO : HALO + count] = (cot[...].astype(F32) * sil[...].astype(F32)).astype(BF)
    wide[:, HALO + count :] = high[high.shape[0] - rows :, :]
    for s in range(pieces):
        outs[s][...] = wide[:, at((idx[1] ^ s) * own, own + 2 * HALO, LANES)]


def weight_kernel(pieces, blocks, idx, *refs):
    *parts, plain, dil_t, point_t = refs
    rows = parts[0].shape[0] // blocks
    part = rows // 2
    for s in range(pieces):
        start = (idx[1] ^ s) * rows
        if s < 2:
            for j in range(blocks):
                plain[j, at(start, rows, 16), :] = parts[s][j * rows : (j + 1) * rows, :]
            continue
        for number in range(2):
            source = parts[2 + 2 * (s - 2) + number]
            first = blocks * ((idx[0] ^ number) & 1)
            for q in range(blocks):
                place = first + q
                plain[
                    lax.div(place, 2), at(start + lax.rem(place, 2) * part, part, 16), :
                ] = source[q * part : (q + 1) * part, :]
    width = plain.shape[1]
    unit_matrix = jnp.where(eye_mask(width), 1.0, 0.0).astype(BF)
    for j in range(blocks):
        for k in range(5):
            turned = dot_rt(unit_matrix, plain[j, :, k * width : (k + 1) * width]).astype(BF)
            if k < 3:
                dil_t[j, :, k * width : (k + 1) * width] = turned
            else:
                point_t[j, :, (k - 3) * width : (k - 2) * width] = turned


def up_kernel(pieces, idx, *refs):
    mains, sides = refs[:pieces], refs[pieces : 2 * pieces]
    up_v, up_sq, up_g, up_b, frame_id, order = refs[2 * pieces : 2 * pieces + 6]
    outs = refs[2 * pieces + 6 : 3 * pieces + 6]
    act_hbm, up_hbm = refs[3 * pieces + 6 : 3 * pieces + 8]
    raw, stacked, phases, wide, act_out, up_w, held_v, held_order, *sems = refs[3 * pieces + 8 :]
    sems, out_sems = sems
    rows, frames = mains[0].shape
    local_out = up_v.shape[1]
    early = [
        pltpu.make_async_copy(up_v, held_v, sems.at[0]),
        pltpu.make_async_copy(order, held_order, sems.at[1]),
    ]
    for copy in early:
        copy.start()
    for s in range(pieces):
        here = at((idx[1] ^ s) * rows, rows, 16)
        raw[here, 0:LANES] = sides[s][:, 0:LANES]
        raw[here, LANES : LANES + frames] = mains[s][...]
        raw[here, LANES + frames :] = sides[s][:, LANES:]
    kept = [
        pltpu.make_async_copy(up_w, up_hbm, out_sems.at[0]),
        pltpu.make_async_copy(act_out, act_hbm, out_sems.at[1]),
    ]
    total = frames + 2 * LANES
    count = stacked.shape[1]
    channels = raw.shape[0]
    shift = total - (LANES - HALO // 8)
    ids = pltpu.roll(jnp.broadcast_to(frame_id[...], (8, total)), shift, axis=1)
    before = pltpu.roll(ids, 1, axis=1)
    after = pltpu.roll(ids, total - 1, axis=1)
    left = jnp.where(before == ids, 1.0, 0.0)[0:1, :].astype(BF)
    right = jnp.where(after == ids, 1.0, 0.0)[0:1, :].astype(BF)
    step = channels
    for r0 in range(0, channels, step):
        part = pl.ds(r0, step)
        acted = unit_act(raw[part, :].astype(F32)).astype(BF)
        act_out[part, :] = acted[:, LANES : LANES + frames]
        moved = pltpu.roll(acted, shift, axis=1)
        one = pltpu.roll(moved, 1, axis=1) * left
        two = pltpu.roll(moved, total - 1, axis=1) * right
        stacked[part, :] = moved[:, 0:count]
        stacked[pl.ds(channels + r0, step), :] = one[:, 0:count]
        stacked[pl.ds(2 * channels + r0, step), :] = two[:, 0:count]
    kept[1].start()
    early[0].wait()
    scale = up_g[...] / jnp.sqrt(up_sq[...])
    for k in range(up_v.shape[0]):
        up_w[k * local_out : (k + 1) * local_out, :] = (held_v[k] * scale).astype(BF)
    kept[0].start()
    eye = eye_mask(local_out)
    bias = to_col(up_b[...], eye)
    bias4 = jnp.concatenate([bias] * 4, axis=0)
    quarter = 4 * local_out
    for c0 in range(0, count, 3 * LANES):
        cols = pl.ds(c0, 3 * LANES)
        center = stacked[0:channels, cols]
        low = dot(up_w[quarter : 2 * quarter, :], center)
        low = low + dot(up_w[3 * quarter : 4 * quarter, :], stacked[channels : 2 * channels, cols])
        high = dot(up_w[2 * quarter : 3 * quarter, :], center)
        high = high + dot(up_w[0:quarter, :], stacked[2 * channels : 3 * channels, cols])
        low = (low + bias4).astype(BF)
        high = (high + bias4).astype(BF)
        for b in range(3):
            block = c0 // LANES + b
            if block * local_out >= phases.shape[0]:
                continue
            for r in range(8):
                source = (low, high)[r // 4]
                phases[block * local_out : (block + 1) * local_out, r * LANES : (r + 1) * LANES] = (
                    source[
                        (r % 4) * local_out : (r % 4 + 1) * local_out,
                        b * LANES : (b + 1) * LANES,
                    ]
                )
    early[1].wait()
    turned = dot(phases[...], held_order[...]).astype(BF)
    for block in range(count // LANES):
        wide[:, block * 1024 : (block + 1) * 1024] = turned[
            block * local_out : (block + 1) * local_out, :
        ]
    own = 8 * frames // pieces
    for s in range(pieces):
        outs[s][...] = wide[:, at((idx[1] ^ s) * own, own + 2 * HALO, LANES)]
    for copy in kept:
        copy.wait()


def sample_masks(sample_id, distance):
    width = sample_id.shape[1]
    ids = jnp.broadcast_to(sample_id[...], (8, width))
    back = pltpu.roll(ids, distance, axis=1)
    ahead = pltpu.roll(ids, width - distance, axis=1)
    return (
        jnp.where(back == ids, 1.0, 0.0)[0:1, :].astype(BF),
        jnp.where(ahead == ids, 1.0, 0.0)[0:1, :].astype(BF),
    )


def forward_kernel(pieces, blocks, idx, *refs):
    parts = refs[:pieces]
    plain, sample_id, silence = refs[pieces : pieces + 3]
    outs = refs[pieces + 3 : 2 * pieces + 3]
    kept = refs[2 * pieces + 3 : 2 * pieces + 8]
    hidden, taps, pair, final = refs[2 * pieces + 8 :]
    keep_h, keep_u, keep_m, keep_sh, keep_sc = kept
    rows, width = parts[0].shape
    channels = pieces * rows
    for s in range(pieces):
        hidden[at((idx[1] ^ s) * rows, rows, 16), :] = parts[s][...]
    for j in range(blocks):
        distance = 3**j
        tail = plain[j, :, 5 * channels : 5 * channels + TAIL].astype(F32)
        dil_b = tail[:, 0:1] + tail[:, 1:2]
        out_b = tail[:, 2:3] + tail[:, 3:4]

        low = hidden[...]
        keep_h[j] = low
        pair[channels : 2 * channels, :] = low
        acted, slope = unit(low.astype(F32))
        acted = acted.astype(BF)
        taps[channels : 2 * channels, :] = acted
        keep_u[j] = acted
        keep_sh[j] = slope.astype(BF)
        back, ahead = sample_masks(sample_id, distance)
        center = taps[channels : 2 * channels, :]
        taps[0:channels, :] = pltpu.roll(center, distance, axis=1) * back
        taps[2 * channels : 3 * channels, :] = pltpu.roll(center, width - distance, axis=1) * ahead

        inner = dot(plain[j, :, 0 : 3 * channels], taps[...]) + dil_b
        acted, slope = unit(inner)
        acted = acted.astype(BF)
        pair[0:channels, :] = acted
        keep_m[j] = acted
        keep_sc[j] = slope.astype(BF)
        after = dot(plain[j, :, 3 * channels : 5 * channels], pair[...]) + out_b
        if j < blocks - 1:
            hidden[...] = after.astype(BF)
        else:
            final[...] = after
    own = width - 2 * HALO
    voiced = silence[:, at(idx[1] * own, own, LANES)].astype(F32)
    for s in range(pieces):
        here = at((idx[1] ^ s) * rows, rows, 16)
        outs[s][...] = (final[here, HALO : HALO + own] * voiced).astype(BF)


def spread_taps(j, center, sample_id, taps):
    channels, width = center.shape
    distance = 3**j
    back, ahead = sample_masks(sample_id, distance)
    taps[channels : 2 * channels, :] = center
    taps[0:channels, :] = pltpu.roll(center, width - distance, axis=1) * ahead
    taps[2 * channels : 3 * channels, :] = pltpu.roll(center, distance, axis=1) * back


def edge_start(pieces, peer):
    return jnp.where(peer < pieces // 2, 0, HALO)


def backward_kernel(pieces, idx, *refs):
    parts = refs[:pieces]
    dil_t, point_t, sample_id, keep_sh, keep_sc = refs[pieces : pieces + 5]
    outs = refs[pieces + 5 : 2 * pieces + 5]
    errs, inners, taps, low = refs[2 * pieces + 5 :]
    rows = parts[0].shape[0]
    blocks, channels, width = errs.shape
    last = blocks - 1
    for s in range(pieces):
        errs[last, at((idx[1] ^ s) * rows, rows, 16), :] = parts[s][...]
    for j in reversed(range(blocks)):
        err = errs[j]
        inner = dot(point_t[j, :, 0:channels], err) * keep_sc[j].astype(F32)
        inner = inner.astype(BF)
        inners[j] = inner
        spread_taps(j, inner, sample_id, taps)
        spread = dot(dil_t[j], taps[...]) * keep_sh[j].astype(F32)
        after = (spread + dot(point_t[j, :, channels : 2 * channels], err)).astype(BF)
        if j > 0:
            errs[j - 1] = after
        else:
            low[...] = after
    lanes = at(edge_start(pieces, idx[1]), width - HALO, LANES)
    for s in range(pieces):
        outs[s][...] = low[at((idx[1] ^ s) * rows, rows, 16), lanes]


def grad_kernel(pieces, sequence, idx, errs, inners, sample_id, keep_h, keep_u, keep_m, *refs):
    keep, send, taps, mats = refs
    blocks, channels, width = errs.shape
    inside = pl.ds(HALO, width - 2 * HALO)
    rows = channels // pieces
    lane = lax.broadcasted_iota(jnp.int32, (channels, channels), 1)
    tail = jnp.zeros((channels, channels), F32)
    for j in range(blocks):
        spread_taps(j, inners[j], sample_id, taps)
        err = errs[j, :, inside]
        mats[5 * j + 3] = dot_rt(err, keep_m[j, :, inside]).astype(BF)
        mats[5 * j + 4] = dot_rt(err, keep_h[j, :, inside]).astype(BF)
        for k in range(3):
            mats[5 * j + k] = dot_rt(
                taps[k * channels : (k + 1) * channels, inside], keep_u[j, :, inside]
            ).astype(BF)
        dil_sum = jnp.sum(inners[j, :, inside].astype(F32), axis=1, keepdims=True)
        out_sum = jnp.sum(err.astype(F32), axis=1, keepdims=True)
        tail = tail + jnp.where(lane == 2 * j, dil_sum, 0.0)
        tail = tail + jnp.where(lane == 2 * j + 1, out_sum, 0.0)
    mats[5 * blocks] = tail.astype(BF)
    size = (5 * blocks + 1) * rows * pieces // len(sequence)
    part = min(size, rows)
    half = len(sequence) // 2
    for position, (s, t) in enumerate(sequence):
        target = (keep, send)[position // half]
        for q in range(size // part):
            place = (idx[0] ^ t) * (size // part) + q
            row = (idx[1] ^ s) * rows + lax.rem(place, rows // part) * part
            start = position % half * size + q * part
            target[start : start + part, :] = mats[
                lax.div(place, rows // part), at(row, part, 16), :
            ]


def halve_kernel(idx, keep, got, next_keep, next_send):
    half = next_keep.shape[0]
    total = keep[...].astype(F32) + got[...].astype(F32)
    next_keep[...] = total[:half].astype(BF)
    next_send[...] = total[half:].astype(BF)


def up_back_kernel(pieces, peers, orders, idx, *refs):
    parts = refs[:pieces]
    up_v, acted, frame_id, order = refs[pieces : pieces + 4]
    cols_grad, *streams = refs[pieces + 4 : pieces + 9]
    wide, stacked, phases, low_grad, held_v, held_act, held_order, sems = refs[pieces + 9 :]
    rows = parts[0].shape[0]
    own = parts[0].shape[1] - HALO
    length = pieces * own
    frames = length // 8
    late = []
    for source, target in ((order, held_order), (acted, held_act), (up_v, held_v)):
        late.append(pltpu.make_async_copy(source, target, sems.at[len(late)]))
        late[-1].start()
    wide[:, HALO + length :] = jnp.zeros((rows, wide.shape[1] - HALO - length), BF)
    for s in range(pieces):
        peer = idx[1] ^ s
        source = parts[s][:, at(HALO - edge_start(pieces, peer), own, LANES)]
        wide[:, at(HALO + peer * own, own, LANES)] = source

        @pl.when(peer == 0)
        def _():
            wide[:, 0:HALO] = parts[s][:, 0:HALO]

        @pl.when(peer == pieces - 1)
        def _():
            wide[:, HALO + length : 2 * HALO + length] = parts[s][:, own:]

    total = wide.shape[1] // 8
    blocks = total // LANES
    for block in range(blocks):
        stacked[block * rows : (block + 1) * rows, :] = wide[:, block * 1024 : (block + 1) * 1024]
    late[0].wait()
    turned = dot_rt(stacked[...], held_order[...]).astype(BF)
    for block in range(blocks):
        for r in range(8):
            phases[r * rows : (r + 1) * rows, block * LANES : (block + 1) * LANES] = turned[
                block * rows : (block + 1) * rows, r * LANES : (r + 1) * LANES
            ]
    ids = jnp.broadcast_to(frame_id[...], (8, frame_id.shape[1]))
    before = pltpu.roll(ids, 1, axis=1)
    after = pltpu.roll(ids, frame_id.shape[1] - 1, axis=1)
    inside = slice(LANES, LANES + frames)
    left = jnp.where(before == ids, 1.0, 0.0)[0:1, inside]
    right = jnp.where(after == ids, 1.0, 0.0)[0:1, inside]
    lead = HALO // 8
    eighth = 4 * rows
    sample_sum = jnp.zeros((rows, 1), F32)
    for part in range(2):
        base = phases[part * eighth : (part + 1) * eighth, :]
        center = pltpu.roll(base, total - lead, axis=1)[:, 0:frames]
        cols_grad[(4 + 4 * part) * rows : (8 + 4 * part) * rows, :] = center
        partial = jnp.sum(center.astype(F32), axis=1, keepdims=True)
        for r in range(4):
            sample_sum = sample_sum + partial[r * rows : (r + 1) * rows]
        if part == 1:
            moved = pltpu.roll(base, total - lead + 1, axis=1)[:, 0:frames]
            cols_grad[0:eighth, :] = (moved.astype(F32) * left).astype(BF)
        else:
            moved = pltpu.roll(base, total - lead - 1, axis=1)[:, 0:frames]
            cols_grad[12 * rows : 16 * rows, :] = (moved.astype(F32) * right).astype(BF)
    taps = up_v.shape[0]
    channels = up_v.shape[2]
    inner = jnp.zeros((rows, channels), F32)
    late[1].wait()
    grad = dot_rt(cols_grad[...], held_act[...])
    low_grad[...] = grad.astype(BF)
    late[2].wait()
    for k in range(taps):
        inner = inner + grad[k * rows : (k + 1) * rows] * held_v[k]
    inner = jnp.sum(inner, axis=0, keepdims=True)
    bias = jnp.concatenate(
        [to_row(sample_sum, eye_mask(rows)), jnp.zeros((1, channels - rows), F32)], axis=1
    )
    side = channels // 2
    line = lax.broadcasted_iota(jnp.int32, (SUMS, side), 0)
    sums = jnp.zeros((SUMS, side), F32)
    for number, value in enumerate((inner[:, :side], inner[:, side:], bias[:, :side])):
        high = value.astype(BF).astype(F32)
        sums = sums + jnp.where(line == 2 * number, high, 0.0)
        sums = sums + jnp.where(line == 2 * number + 1, value - high, 0.0)
    half = peers // 2
    size = taps * rows // peers
    first = (streams[0].shape[0] - SUMS) // half
    second = 2 * size - first
    streams[0][half * first :, :] = sums.astype(BF)
    streams[1][half * first :, :] = sums.astype(BF)
    for position, s in enumerate(orders[0]):
        target = streams[position // half]
        start = position % half * first
        target[start : start + first, :] = low_grad[at((idx[0] ^ s) * size, first, 16), 0:side]
    for position, s in enumerate(orders[1]):
        target = streams[2 + position // half]
        start = position % half * second
        piece = (idx[0] ^ s) * size
        target[start : start + size, :] = low_grad[at(piece, size, 16), side:]
        if size > first:
            target[start + size : start + second, :] = low_grad[
                at(piece + first, size - first, 16), 0:side
            ]


def input_back_kernel(pieces, order, idx, up_w, cols_grad, keep, send, total):
    total[...] = lax.dot_general(
        up_w[...], cols_grad[...], (((0,), (0,)), ((), ())), preferred_element_type=F32
    ).astype(BF)
    size = total.shape[0] // pieces
    for position, s in enumerate(order):
        target = (keep, send)[position // (pieces // 2)]
        start = position % (pieces // 2) * size
        target[start : start + size, :] = total[at((idx[1] ^ s) * size, size, 16), :]


def join_kernel(idx, keep, got, term, other, next_keep, next_send):
    rows = keep.shape[0] - SUMS
    half, part = rows // 2, term.shape[0] // 2
    total = keep[...].astype(F32) + got[...].astype(F32)
    grads = (term[...].astype(F32) + other[...].astype(F32)).astype(BF)
    for number, target in enumerate((next_keep, next_send)):
        target[0:half, :] = total[number * half : (number + 1) * half].astype(BF)
        target[half : half + part, :] = grads[number * part : (number + 1) * part]
        target[half + part :, :] = total[rows:].astype(BF)


def step_kernel(rows, idx, keep, got, *outs):
    total = keep[...].astype(F32) + got[...].astype(F32)
    grads = total.shape[0] - rows - SUMS
    for number, target in enumerate(outs):
        half, part = rows // 2, grads // 2
        target[0:half, :] = total[number * half : (number + 1) * half].astype(BF)
        start = rows + number * part
        target[half : half + part, :] = total[start : start + part].astype(BF)
        target[half + part :, :] = total[rows + grads :].astype(BF)


def meet_kernel(parts, idx, own, got, out, *sums):
    start = 0
    for count in parts:
        half = count // 2
        for number in range(2):
            here = start + number * half
            there = start + (1 - number) * half
            out[here : here + half, :] = (
                own[here : here + half, :].astype(F32) + got[there : there + half, :].astype(F32)
            ).astype(BF)
        start = start + count
    if sums:
        sums[0][...] = own[start:, :].astype(F32) + got[start:, :].astype(F32)


def whole_kernel(rows, joined, idx, keep, got, *refs):
    *terms, out = refs
    total = keep[...].astype(F32) + got[...].astype(F32)
    if not joined:
        out[...] = total.astype(BF)
        return
    count = terms[0].shape[0]
    out[0:rows, :] = total[0:rows].astype(BF)
    out[rows : rows + count, :] = (terms[0][...].astype(F32) + terms[1][...].astype(F32)).astype(BF)
    out[rows + count :, :] = total[rows:].astype(BF)


def double_kernel(rows, idx, own, got, out):
    grads = own.shape[0] - rows
    out[0:rows, :] = own[0:rows, :]
    out[rows : 2 * rows, :] = got[0:rows, :]
    out[2 * rows : 2 * rows + grads, :] = own[rows:, :]
    out[2 * rows + grads :, :] = got[rows:, :]


def final_kernel(orders, first, idx, *refs):
    streams = refs[:4]
    up_v, up_sq, up_g, inner_sum, dil_v, dil_g, mix_v, mix_g, skip_v, skip_g = refs[4:14]
    up_v_grad, up_g_grad, *outs = refs[14:24]
    whole, blocks_whole, staged, *block_staged, out_sems = refs[24:]
    half = len(orders[0]) // 2
    size = whole.shape[0] // (2 * half)
    side = whole.shape[1] // 2
    second = 2 * size - first
    for position, s in enumerate(orders[0]):
        start = position % half * first
        whole[at((idx[0] ^ s) * size, first, 16), 0:side] = streams[position // half][
            start : start + first, :
        ]
    for position, s in enumerate(orders[1]):
        source = streams[2 + position // half]
        start = position % half * second
        piece = (idx[0] ^ s) * size
        whole[at(piece, size, 16), side:] = source[start : start + size, :]
        if size > first:
            whole[at(piece + first, size - first, 16), 0:side] = source[
                start + size : start + second, :
            ]
    size = blocks_whole.shape[0] // (2 * half)
    for position, s in enumerate(orders[0]):
        start = half * first + position % half * size
        blocks_whole[at((idx[0] ^ s) * size, size, 16), :] = streams[position // half][
            start : start + size, :
        ]
    sent = []

    def ship(source, target):
        sent.append(pltpu.make_async_copy(source, target, out_sems.at[len(sent)]))
        sent[-1].start()

    norm = jnp.sqrt(up_sq[...])
    inner = inner_sum[...]
    scale = up_g[...] / norm
    pull = up_g[...] * inner / (norm * norm * norm)
    rows = up_v.shape[1]
    for k in range(up_v.shape[0]):
        grad = whole[k * rows : (k + 1) * rows, :].astype(F32)
        staged[k] = scale * grad - pull * up_v[k]
        ship(staged.at[k], up_v_grad.at[k])
    up_g_grad[...] = inner / norm
    dil_v_hbm, dil_g_out, dil_b_out, mix_v_hbm, mix_g_out, out_b_out, skip_v_hbm, skip_g_out = outs
    dil_v_out, mix_v_out, skip_v_out = block_staged
    eye = eye_mask(rows)
    blocks = dil_v.shape[0]
    tail = blocks_whole[5 * blocks * rows :, :].astype(F32)
    for j in range(blocks):

        def mat(m):
            start = (5 * j + m) * rows
            return blocks_whole[start : start + rows, :].astype(F32)

        square = jnp.zeros((rows, 1), F32)
        inner = jnp.zeros((rows, 1), F32)
        for k in range(3):
            v = dil_v[j, k]
            square = square + jnp.sum(v * v, axis=1, keepdims=True)
            inner = inner + jnp.sum(v * mat(k), axis=1, keepdims=True)
        norm = jnp.sqrt(square)
        gain = to_col(dil_g[j : j + 1, :], eye)
        for k in range(3):
            dil_v_out[j, k] = gain / norm * mat(k) - gain * inner / (norm**3) * dil_v[j, k]
        ship(dil_v_out.at[j], dil_v_hbm.at[j])
        dil_g_out[j : j + 1, :] = to_row(inner / norm, eye)
        for number, (vref, gref, v_out, v_hbm, g_out) in enumerate(
            (
                (mix_v, mix_g, mix_v_out, mix_v_hbm, mix_g_out),
                (skip_v, skip_g, skip_v_out, skip_v_hbm, skip_g_out),
            )
        ):
            v = vref[j]
            grad = mat(3 + number)
            norm = jnp.sqrt(jnp.sum(v * v, axis=1, keepdims=True))
            inner = jnp.sum(v * grad, axis=1, keepdims=True)
            gain = to_col(gref[j : j + 1, :], eye)
            v_out[j] = gain / norm * grad - gain * inner / (norm**3) * v
            ship(v_out.at[j], v_hbm.at[j])
            g_out[j : j + 1, :] = to_row(inner / norm, eye)
        dil_b_out[j : j + 1, :] = to_row(tail[:, 2 * j : 2 * j + 1], eye)
        out_b_out[j : j + 1, :] = to_row(tail[:, 2 * j + 1 : 2 * j + 2], eye)
    for copy in sent:
        copy.wait()


def place_kernel(pieces, idx, *refs):
    parts, out = refs[:pieces], refs[pieces]
    own = parts[0].shape[1]
    for s in range(pieces):
        out[:, at((idx[1] ^ s) * own, own, LANES)] = parts[s][...]


def stage_kernel(idx, *refs):
    *pairs, sems = refs
    half = len(pairs) // 2
    fetch(list(zip(pairs[:half], pairs[half:])), sems)


def input_kernel(idx, *refs):
    *terms, spectrogram, out = refs
    total = terms[0][...].astype(F32)
    for term in terms[1:]:
        total = total + term[...].astype(F32)
    out[...] = (total * unit(spectrogram[...].astype(F32))[1]).astype(BF)


def local(
    spectrogram_input,
    upsample_direction,
    upsample_magnitude,
    upsample_bias,
    dilated_direction,
    dilated_magnitude,
    dilated_bias,
    pointwise_direction,
    pointwise_magnitude,
    block_output_bias,
    shortcut_direction,
    shortcut_magnitude,
    cotangent,
    silence,
    segments,
):
    pieces, peers = lax.axis_size("chan"), lax.axis_size("tm")
    chan, tm = lax.axis_index("chan"), lax.axis_index("tm")
    in_rows, frames = spectrogram_input.shape
    taps, rows, in_channels = upsample_direction.shape
    blocks = dilated_direction.shape[0]
    channels = dilated_direction.shape[3]
    length = 8 * frames
    own = length // pieces
    width = own + 2 * HALO
    packed_width = 5 * channels + TAIL
    forward = [(k, k + 1) for k in range(peers - 1)]
    backward = [(k + 1, k) for k in range(peers - 1)]
    dma = pltpu.SemaphoreType.DMA
    lead = HALO // 8
    tie = lax.optimization_barrier

    spread = np.arange(8 * LANES)
    order = np.zeros((8 * LANES, 8 * LANES), np.float32)
    order[spread, 8 * (spread % LANES) + spread // LANES] = 1.0
    order = jnp.asarray(order, BF)

    silence_row = silence.reshape(1, length)
    up_g = upsample_magnitude.reshape(1, in_channels)
    edge_rows = in_rows + rows
    ahead, behind = kernel_call(
        edge_kernel,
        [((edge_rows, LANES), BF, "V")] * 2,
        [spectrogram_input, cotangent, silence_row],
        "HHH",
        scratch=[
            pltpu.VMEM((in_rows, LANES), BF),
            pltpu.VMEM((in_rows, LANES), BF),
            pltpu.VMEM((2, rows, HALO), BF),
            pltpu.VMEM((2, 1, HALO), jnp.int32),
            dma((6,)),
        ],
    )
    low_edge = lax.ppermute(ahead, "tm", forward)
    high_edge = lax.ppermute(behind, "tm", backward)
    all_mains = gather_chan(spectrogram_input)
    (up_sq,) = kernel_call(
        square_kernel, [((1, in_channels), F32, "V")], [upsample_direction], "F", micros=2
    )
    block_args = [
        dilated_direction,
        dilated_magnitude,
        dilated_bias,
        pointwise_direction,
        pointwise_magnitude,
        block_output_bias,
        shortcut_direction,
        shortcut_magnitude,
    ]
    sides = jnp.concatenate([low_edge[:in_rows], high_edge[:in_rows]], axis=1)
    block_args, sides = tie((block_args, sides))
    packed_half = ((blocks * rows // 2, packed_width), BF, "V")
    bias_in = upsample_bias.reshape(1, rows)
    packed, near, far, up_g, bias_in = kernel_call(
        prep_kernel,
        [((blocks * rows, packed_width), BF, "V"), packed_half, packed_half]
        + [((1, in_channels), F32, "R"), ((1, rows), F32, "R")],
        [*block_args, up_g, bias_in],
        "FFFFFFFFFF",
        micros=3,
    )
    held_sides = {0: sides}
    for bit in reversed(bits_of(pieces)[1:]):
        for slot in list(held_sides):
            held_sides[slot ^ bit] = swap(held_sides[slot], "chan", bit)
    near, held_sides = tie((near, held_sides))
    for slot in list(held_sides):
        held_sides[slot ^ 1] = swap(held_sides[slot], "chan", 1)
    all_sides = [held_sides[slot] for slot in range(pieces)]
    for bit in bits_of(pieces):
        up_sq = up_sq + swap(up_sq, "chan", bit)
    padded_ids = jnp.pad(segments.astype(F32), LANES, constant_values=-1.0)
    frame_id = lax.dynamic_slice_in_dim(padded_ids, tm * frames, frames + 2 * LANES)
    sample_id = jnp.repeat(
        lax.dynamic_slice_in_dim(
            padded_ids, LANES + tm * frames + chan * (own // 8) - lead, width // 8
        ),
        8,
    ).reshape(1, width)
    frame_id = frame_id.reshape(1, frames + 2 * LANES)
    top = pieces // 2
    near, all_sides[top], up_sq = tie((near, all_sides[top], up_sq))

    count = -(-(frames + 2 * lead) // LANES) * LANES
    count = -(-count // (3 * LANES)) * 3 * LANES
    up_outs = kernel_call(
        functools.partial(up_kernel, pieces),
        [((rows, width), BF, "R")]
        + [((rows, width), BF, "V")] * (pieces - 1)
        + [((in_channels, frames), BF, "H"), ((taps * rows, in_channels), BF, "H")],
        all_mains
        + all_sides
        + [upsample_direction, up_sq, up_g, bias_in, frame_id, order],
        "V" * (2 * pieces) + "HVRRVH",
        scratch=[
            pltpu.VMEM((in_channels, frames + 2 * LANES), BF),
            pltpu.VMEM((3 * in_channels, count), BF),
            pltpu.VMEM((count // LANES * rows, 8 * LANES), BF),
            pltpu.VMEM((rows, 8 * count), BF),
            pltpu.VMEM((in_channels, frames), BF),
            pltpu.VMEM((taps * rows, in_channels), BF),
            pltpu.VMEM(upsample_direction.shape, F32),
            pltpu.VMEM(order.shape, BF),
            dma((2,)),
            dma((2,)),
        ],
        micros=6,
    )
    acted, up_w = up_outs[pieces:]
    chan_bits = bits_of(pieces)
    held_near = {0: near}
    for bit in reversed(chan_bits[1:]):
        for slot in list(held_near):
            held_near[slot ^ bit] = swap(held_near[slot], "chan", bit)
    hidden_parts, held_near, low_edge = tie((list(up_outs[:pieces]), held_near, low_edge))
    cut = kernel_call(
        functools.partial(cut_kernel, pieces),
        [((rows, width), BF, "R")] + [((rows, width), BF, "V")] * (pieces - 1),
        [cotangent, silence_row, low_edge, high_edge],
        "FFVV",
        scratch=[pltpu.VMEM((rows, length + 2 * HALO), BF)],
        micros=2,
    )
    all_hidden = exchange_chan(hidden_parts)
    all_packed = [packed, swap(packed, "chan", 1)]
    for slot in range(2, pieces, 2):
        two = [held_near[slot], swap(held_near[slot], "tm", 1)]
        two, all_hidden[top], cut = tie((two, all_hidden[top], list(cut)))
        all_packed += two + [swap(value, "chan", 1) for value in two]

    plain, dil_t, point_t = kernel_call(
        functools.partial(weight_kernel, pieces, blocks),
        [
            ((blocks, channels, packed_width), BF, "R"),
            ((blocks, channels, 3 * channels), BF, "R"),
            ((blocks, channels, 2 * channels), BF, "R"),
        ],
        all_packed,
        "V" * len(all_packed),
        micros=0.1,
    )
    cut, plain = tie((list(cut), plain))
    all_err = exchange_chan(cut)

    kept_shape = ((blocks, channels, width), BF, "R")
    forward_outs = kernel_call(
        functools.partial(forward_kernel, pieces, blocks),
        [((rows, own), BF, "V")] * pieces + [kept_shape] * 5,
        all_hidden + [plain, sample_id, silence_row],
        "R" + "V" * (pieces - 1) + "RVF",
        scratch=[
            pltpu.VMEM((channels, width), BF),
            pltpu.VMEM((3 * channels, width), BF),
            pltpu.VMEM((2 * channels, width), BF),
            pltpu.VMEM((channels, width), F32),
        ],
        micros=10,
    )
    keep_h, keep_u, keep_m, keep_sh, keep_sc = forward_outs[pieces:]
    activation_parts = list(forward_outs[:pieces])

    backward_outs = kernel_call(
        functools.partial(backward_kernel, pieces),
        [((rows, width - HALO), BF, "V")] * pieces + [kept_shape] * 2,
        all_err + [dil_t, point_t, sample_id, keep_sh, keep_sc],
        "R" + "V" * (pieces - 1) + "RRVRR",
        scratch=[
            pltpu.VMEM((3 * channels, width), BF),
            pltpu.VMEM((channels, width), BF),
        ],
        micros=10,
    )
    errs, inners = backward_outs[pieces:]
    all_low = exchange_chan(list(backward_outs[:pieces]))

    chan_order = order_of(chan_bits)
    tm_bits = bits_of(peers)
    path = [("chan", 1), ("tm", 1)] + [("chan", bit) for bit in chan_bits[1:]]
    path_order = [(0, 0)]
    for axis, bit in reversed(path + [("tm", bit) for bit in tm_bits[1:]]):
        other = [
            (s + bit, t) if axis == "chan" else (s, t + bit) for s, t in path_order
        ]
        path_order = path_order + other
    mats = 5 * blocks + 1
    share = pieces // 2 * mats * rows
    keep, send = kernel_call(
        functools.partial(grad_kernel, pieces, path_order),
        [((share, channels), BF, "V")] * 2,
        [errs, inners, sample_id, keep_h, keep_u, keep_m],
        "RRVRRR",
        scratch=[
            pltpu.VMEM((3 * channels, width), BF),
            pltpu.VMEM((mats, channels, channels), BF),
        ],
        micros=0.1,
    )

    def scatter(keep, send, path):
        for axis, bit in path[:-1]:
            got = swap(send, axis, bit)
            next_shape = ((keep.shape[0] // 2, keep.shape[1]), BF, "V")
            keep, send = kernel_call(halve_kernel, [next_shape] * 2, [keep, got], "VV")
        return keep, swap(send, *path[-1])

    keep, send, all_low[top] = tie((keep, send, all_low[top]))
    got = swap(send, *path[0])
    keep, send = kernel_call(
        halve_kernel, [((share // 2, channels), BF, "V")] * 2, [keep, got], "VV"
    )
    block_terms = scatter(keep, send, path[1:])
    send, all_low = tie((send, all_low))

    turned_bits = tm_bits[1:] + tm_bits[:1]
    orders = (order_of(tm_bits), order_of(turned_bits))
    half = peers // 2
    total_rows = taps * rows
    size = total_rows // peers
    side = in_channels // 2
    first = max(16, size // 2 // 16 * 16)
    second = 2 * size - first
    cols_grad, keep_one, send_one, keep_two, send_two = kernel_call(
        functools.partial(up_back_kernel, pieces, peers, orders),
        [((total_rows, frames), BF, "R")]
        + [((half * first + SUMS, side), BF, "V")] * 2
        + [((half * second, side), BF, "V")] * 2,
        all_low + [upsample_direction, acted, frame_id, order],
        "V" * pieces + "HHVH",
        scratch=[
            pltpu.VMEM((rows, 8 * count), BF),
            pltpu.VMEM((count // LANES * rows, 8 * LANES), BF),
            pltpu.VMEM((8 * rows, count), BF),
            pltpu.VMEM((total_rows, in_channels), BF),
            pltpu.VMEM(upsample_direction.shape, F32),
            pltpu.VMEM((in_channels, frames), BF),
            pltpu.VMEM(order.shape, BF),
            dma((3,)),
        ],
        micros=5,
    )

    piece_rows = pieces // 2 * in_rows
    keep, send = kernel_call(
        functools.partial(input_back_kernel, pieces, chan_order),
        [((piece_rows, frames), BF, "V")] * 2,
        [up_w, cols_grad],
        "FR",
        scratch=[pltpu.VMEM((in_channels, frames), BF)],
        micros=3,
    )
    keep, send_one = tie((keep, send_one))

    steps = len(tm_bits)
    block_rows = mats * rows
    one_rows, two_rows = half * first, half * second
    for step in range(steps - 1):
        got_one = swap(send_one, "tm", tm_bits[step])
        got_two = swap(send_two, "tm", turned_bits[step])
        if step == 0:
            got_one, got_two, keep, send = tie((got_one, got_two, keep, send))
            activation_parts, got_one = tie((activation_parts, got_one))
            activation_parts = exchange_chan(activation_parts)
            input_terms = scatter(keep, send, [("chan", bit) for bit in chan_bits])
        else:
            got_one, got_two = tie((got_one, got_two))
        one_rows, two_rows, block_rows = one_rows // 2, two_rows // 2, block_rows // 2
        if step < steps - 2:
            next_shape = ((one_rows + block_rows // 2 + SUMS, side), BF, "V")
            if step == 0:
                keep_one, send_one = kernel_call(
                    join_kernel, [next_shape] * 2, [keep_one, got_one, *block_terms], "VVVV"
                )
            else:
                keep_one, send_one = kernel_call(
                    functools.partial(step_kernel, 2 * one_rows),
                    [next_shape] * 2,
                    [keep_one, got_one],
                    "VV",
                )
            keep_two, send_two = kernel_call(
                halve_kernel, [((two_rows, side), BF, "V")] * 2, [keep_two, got_two], "VV"
            )
    joined = steps == 2
    one_rows, two_rows = 2 * one_rows, 2 * two_rows
    (held_one,) = kernel_call(
        functools.partial(whole_kernel, one_rows, joined),
        [((one_rows + block_rows + SUMS, side), BF, "V")],
        [keep_one, got_one, *(block_terms if joined else ())],
        "VVVV" if joined else "VV",
    )
    (held_two,) = kernel_call(
        functools.partial(whole_kernel, two_rows, False),
        [((two_rows, side), BF, "V")],
        [keep_two, got_two],
        "VV",
    )
    got_one = swap(held_one, "tm", tm_bits[-1])
    got_two = swap(held_two, "tm", turned_bits[-1])
    got_one, got_two, input_terms = tie((got_one, got_two, input_terms))
    own_one, sums = kernel_call(
        functools.partial(meet_kernel, (one_rows, block_rows)),
        [((one_rows + block_rows, side), BF, "V"), ((SUMS, side), F32, "V")],
        [held_one, got_one],
        "VV",
    )
    (own_two,) = kernel_call(
        functools.partial(meet_kernel, (two_rows,)),
        [((two_rows, side), BF, "V")],
        [held_two, got_two],
        "VV",
    )
    for step in reversed(range(steps - 1)):
        got_one = swap(own_one, "tm", tm_bits[step])
        got_two = swap(own_two, "tm", turned_bits[step])
        if step == steps - 2:
            got_one, got_two, activation_parts = tie((got_one, got_two, activation_parts))
        else:
            got_one, got_two = tie((got_one, got_two))
        if step > 0:
            (own_one,) = kernel_call(
                functools.partial(double_kernel, one_rows),
                [((2 * own_one.shape[0], side), BF, "V")],
                [own_one, got_one],
                "VV",
            )
            one_rows = 2 * one_rows
            own_two = jnp.concatenate([own_two, got_two], axis=0)

    pair = sums[0:6:2] + sums[1:6:2]
    inner_sum = pair[0:2].reshape(1, in_channels)
    for bit in chan_bits:
        inner_sum = inner_sum + swap(inner_sum, "chan", bit)

    (input_grad,) = kernel_call(
        input_kernel,
        [((in_rows, frames), BF, "V")],
        [*input_terms, spectrogram_input],
        "VVF",
    )
    (activation,) = kernel_call(
        functools.partial(place_kernel, pieces),
        [((rows, length), BF, "V")],
        activation_parts,
        "V" * pieces,
        micros=2,
    )

    late_args = [
        upsample_direction,
        dilated_direction,
        dilated_magnitude,
        pointwise_direction,
        pointwise_magnitude,
        shortcut_direction,
        shortcut_magnitude,
    ]
    late_args, sums = tie((late_args, sums))
    staged = kernel_call(
        stage_kernel,
        [(arg.shape, arg.dtype, "R") for arg in late_args],
        late_args,
        "H" * len(late_args),
        scratch=[dma((len(late_args),))],
        micros=2,
    )
    final_outs = kernel_call(
        functools.partial(final_kernel, orders, first),
        [
            (upsample_direction.shape, F32, "H"),
            ((1, in_channels), F32, "V"),
            (dilated_direction.shape, F32, "H"),
            (dilated_magnitude.shape, F32, "V"),
            (dilated_bias.shape, F32, "V"),
            (pointwise_direction.shape, F32, "H"),
            (pointwise_magnitude.shape, F32, "V"),
            (block_output_bias.shape, F32, "V"),
            (shortcut_direction.shape, F32, "H"),
            (shortcut_magnitude.shape, F32, "V"),
        ],
        [
            own_one,
            got_one,
            own_two,
            got_two,
            staged[0],
            up_sq,
            up_g,
            inner_sum,
            *staged[1:],
        ],
        "VVVVRVRVRRRRRR",
        scratch=[
            pltpu.VMEM((total_rows, in_channels), BF),
            pltpu.VMEM((mats * rows, channels), BF),
            pltpu.VMEM(upsample_direction.shape, F32),
            pltpu.VMEM(dilated_direction.shape, F32),
            pltpu.VMEM(pointwise_direction.shape, F32),
            pltpu.VMEM(shortcut_direction.shape, F32),
            dma((taps + 3 * blocks,)),
        ],
        micros=5,
    )
    up_v_grad, up_g_grad, dil_v_grad, dil_g_grad, dil_b_grad = final_outs[:5]
    mix_v_grad, mix_g_grad, out_b_grad, skip_v_grad, skip_g_grad = final_outs[5:]
    return (
        activation,
        input_grad,
        up_v_grad,
        up_g_grad.reshape(in_channels),
        pair[2, :rows],
        dil_v_grad,
        dil_g_grad,
        dil_b_grad,
        mix_v_grad,
        mix_g_grad,
        out_b_grad,
        skip_v_grad,
        skip_g_grad,
    )


def solution(mesh):
    placed = (
        P("chan", "tm"),
        P(None, "chan", None),
        P(),
        P("chan"),
        P(None, None, "chan", None),
        P(None, "chan"),
        P(None, "chan"),
        P(None, "chan", None),
        P(None, "chan"),
        P(None, "chan"),
        P(None, "chan", None),
        P(None, "chan"),
        P("chan", "tm"),
        P("tm"),
        P(),
    )
    return jax.shard_map(
        local,
        mesh=mesh,
        in_specs=placed,
        out_specs=(
            P("chan", "tm"),
            P("chan", "tm"),
            P(None, "chan", None),
            P(),
            P("chan"),
            P(None, None, "chan", None),
            P(None, "chan"),
            P(None, "chan"),
            P(None, "chan", None),
            P(None, "chan"),
            P(None, "chan"),
            P(None, "chan", None),
            P(None, "chan"),
        ),
        check_vma=False,
    )
```

```python
import functools

import jax
import jax.numpy as jnp
import numpy as np
from jax import lax
from jax.experimental import pallas as pl
from jax.experimental.pallas import tpu as pltpu
from jax.sharding import PartitionSpec as P

BF = jnp.bfloat16
F32 = jnp.float32
LANES = 128
HALO = 64
TAIL = 128
SUMS = 16
VMEM_LIMIT = 20 * 1024 * 1024


def swap(values, axis, bit):
    count = lax.axis_size(axis)
    return lax.ppermute(values, axis, [(k, k ^ bit) for k in range(count)])


def bits_of(count):
    bits = []
    bit = 1
    while bit < count:
        bits.append(bit)
        bit = 2 * bit
    return bits


def order_of(bits):
    order = [0]
    for bit in reversed(bits):
        order = order + [slot + bit for slot in order]
    return order


def gather_chan(own):
    held = {0: own}
    for bit in reversed(bits_of(lax.axis_size("chan"))):
        for slot in list(held):
            held[slot ^ bit] = swap(held[slot], "chan", bit)
    return [held[slot] for slot in range(len(held))]


def exchange_chan(pieces):
    return [pieces[0]] + [swap(pieces[s], "chan", s) for s in range(1, len(pieces))]


HBM = pl.BlockSpec(memory_space=pltpu.HBM)
VMEM = pl.BlockSpec(memory_space=pltpu.VMEM)


def kernel_call(body, outs, args, specs, scratch=(), micros=1.0):
    held = []
    in_specs = []
    operands = []
    for arg, spec in zip(args, specs, strict=True):
        in_specs.append({"H": HBM, "F": HBM, "R": VMEM, "V": VMEM}[spec])
        if spec == "F":
            held.append(pltpu.VMEM(arg.shape, arg.dtype))
        if spec == "R":
            arg = pltpu.with_memory_space_constraint(arg, pltpu.VMEM)
        if spec in "HF":
            arg = pltpu.with_memory_space_constraint(arg, pltpu.HBM)
        operands.append(arg)
    out_shape = []
    out_specs = []
    for shape, dtype, spec in outs:
        out_specs.append(HBM if spec == "H" else VMEM)
        spaced = {"R": pltpu.VMEM, "H": pltpu.HBM, "V": jax.ShapeDtypeStruct}[spec]
        out_shape.append(spaced(shape, dtype))
    fetched = len(held)

    def wrapped(*refs):
        refs = list(refs)
        if fetched:
            sems = refs.pop()
            targets = refs[-fetched:]
            refs = refs[:-fetched]
            sources = [number for number, spec in enumerate(specs) if spec == "F"]
            fetch([(refs[n], target) for n, target in zip(sources, targets)], sems)
            for n, target in zip(sources, targets):
                refs[n] = target
        body((lax.axis_index("tm"), lax.axis_index("chan")), *refs)

    extra = held + ([pltpu.SemaphoreType.DMA((fetched,))] if fetched else [])
    return pl.pallas_call(
        wrapped,
        out_shape=tuple(out_shape),
        in_specs=in_specs,
        out_specs=tuple(out_specs),
        scratch_shapes=list(scratch) + extra,
        compiler_params=pltpu.CompilerParams(vmem_limit_bytes=VMEM_LIMIT),
        cost_estimate=pl.CostEstimate(
            flops=int(micros * 1.1e9), bytes_accessed=0, transcendentals=0
        ),
    )(*operands)


def fetch(pairs, sems):
    copies = [
        pltpu.make_async_copy(source, target, sems.at[number])
        for number, (source, target) in enumerate(pairs)
    ]
    for copy in copies:
        copy.start()
    for copy in copies:
        copy.wait()


def unit(values):
    th = jnp.tanh(0.5 * values)
    base = 0.6 + 0.4 * th
    return values * base, base + 0.2 * values * (1.0 - th * th)


def unit_act(values):
    return values * (0.6 + 0.4 * jnp.tanh(0.5 * values))


def dot(left, right):
    return lax.dot_general(left, right, (((1,), (0,)), ((), ())), preferred_element_type=F32)


def dot_rt(left, right):
    return lax.dot_general(left, right, (((1,), (1,)), ((), ())), preferred_element_type=F32)


def eye_mask(count):
    rows = lax.broadcasted_iota(jnp.int32, (count, count), 0)
    cols = lax.broadcasted_iota(jnp.int32, (count, count), 1)
    return rows == cols


def to_col(row, eye):
    return jnp.sum(jnp.where(eye, row, 0.0), axis=1, keepdims=True)


def to_row(col, eye):
    return jnp.sum(jnp.where(eye, col, 0.0), axis=0, keepdims=True)


def at(start, size, step):
    return pl.ds(pl.multiple_of(start, step), size)


def edge_kernel(idx, spectrogram, cot, sil, ahead, behind, front, back, sound, mask, sems):
    rows = spectrogram.shape[0]
    frames, count = spectrogram.shape[1], cot.shape[1]
    low, high = pl.ds(0, LANES), pl.ds(count - LANES, LANES)
    fetch(
        [
            (spectrogram.at[:, frames - LANES :], front),
            (spectrogram.at[:, :LANES], back),
            (cot.at[:, high], sound.at[0]),
            (cot.at[:, low], sound.at[1]),
            (sil.at[:, high], mask.at[0]),
            (sil.at[:, low], mask.at[1]),
        ],
        sems,
    )
    ahead[0:rows, :] = front[...]
    behind[0:rows, :] = back[...]
    ahead[rows:, :] = (sound[0].astype(F32) * mask[0].astype(F32)).astype(BF)
    behind[rows:, :] = (sound[1].astype(F32) * mask[1].astype(F32)).astype(BF)


def square_kernel(idx, up_v, up_sq):
    total = jnp.zeros((up_v.shape[1], up_v.shape[2]), F32)
    for k in range(up_v.shape[0]):
        rows = up_v[k]
        total = total + rows * rows
    up_sq[...] = jnp.sum(total, axis=0, keepdims=True)


def prep_kernel(
    idx, dil_v, dil_g, dil_b, mix_v, mix_g, out_b, skip_v, skip_g, up_g, up_b, packed, near, far, up_row, bias_row
):
    up_row[...] = up_g[...]
    bias_row[...] = up_b[...]
    local_out = dil_v.shape[2]
    eye = eye_mask(local_out)
    lane = lax.broadcasted_iota(jnp.int32, (local_out, TAIL), 1)
    width = dil_v.shape[3]
    for j in range(dil_v.shape[0]):
        rows = pl.ds(j * local_out, local_out)
        square = jnp.zeros((local_out, 1), F32)
        for k in range(3):
            v = dil_v[j, k]
            square = square + jnp.sum(v * v, axis=1, keepdims=True)
        norm = jnp.sqrt(square)
        scale = to_col(dil_g[j : j + 1, :], eye) / norm
        for k in range(3):
            packed[rows, k * width : (k + 1) * width] = (dil_v[j, k] * scale).astype(BF)
        for number, (vref, gref) in enumerate(((mix_v, mix_g), (skip_v, skip_g))):
            v = vref[j]
            norm = jnp.sqrt(jnp.sum(v * v, axis=1, keepdims=True))
            scale = to_col(gref[j : j + 1, :], eye) / norm
            packed[rows, (3 + number) * width : (4 + number) * width] = (v * scale).astype(BF)
        first = to_col(dil_b[j : j + 1, :], eye)
        second = to_col(out_b[j : j + 1, :], eye)
        high_one = first.astype(BF).astype(F32)
        high_two = second.astype(BF).astype(F32)
        tail = jnp.where(lane == 0, high_one, 0.0) + jnp.where(lane == 1, first - high_one, 0.0)
        tail = tail + jnp.where(lane == 2, high_two, 0.0)
        tail = tail + jnp.where(lane == 3, second - high_two, 0.0)
        packed[rows, 5 * width : 5 * width + TAIL] = tail.astype(BF)
    half = near.shape[0]
    for number, target in enumerate((near, far)):
        target[...] = packed[at(((idx[0] ^ number) & 1) * half, half, 16), :]


def cut_kernel(pieces, idx, cot, sil, low, high, *refs):
    outs, wide = refs[:pieces], refs[pieces]
    count = cot.shape[1]
    own = count // pieces
    rows = cot.shape[0]
    wide[:, 0:LANES] = low[low.shape[0] - rows :, :]
    wide[:, LANES : LANES + count] = (cot[...].astype(F32) * sil[...].astype(F32)).astype(BF)
    wide[:, LANES + count :] = high[high.shape[0] - rows :, :]
    wide[...] = pltpu.roll(wide[...], wide.shape[1] - (LANES - HALO), axis=1)
    for s in range(pieces):
        outs[s][...] = wide[:, at((idx[1] ^ s) * own, own + 2 * HALO, LANES)]


def weight_kernel(pieces, blocks, idx, *refs):
    *parts, plain, dil_t, point_t = refs
    rows = parts[0].shape[0] // blocks
    part = rows // 2
    for s in range(pieces):
        start = (idx[1] ^ s) * rows
        if s < 2:
            for j in range(blocks):
                plain[j, at(start, rows, 16), :] = parts[s][j * rows : (j + 1) * rows, :]
            continue
        for number in range(2):
            source = parts[2 + 2 * (s - 2) + number]
            first = blocks * ((idx[0] ^ number) & 1)
            for q in range(blocks):
                place = first + q
                plain[
                    lax.div(place, 2), at(start + lax.rem(place, 2) * part, part, 16), :
                ] = source[q * part : (q + 1) * part, :]
    width = plain.shape[1]
    unit_matrix = jnp.where(eye_mask(width), 1.0, 0.0).astype(BF)
    for j in range(blocks):
        for k in range(5):
            turned = dot_rt(unit_matrix, plain[j, :, k * width : (k + 1) * width]).astype(BF)
            if k < 3:
                dil_t[j, :, k * width : (k + 1) * width] = turned
            else:
                point_t[j, :, (k - 3) * width : (k - 2) * width] = turned


def up_kernel(pieces, idx, *refs):
    mains, sides = refs[:pieces], refs[pieces : 2 * pieces]
    up_v, up_sq, up_g, up_b, frame_id, order = refs[2 * pieces : 2 * pieces + 6]
    outs = refs[2 * pieces + 6 : 3 * pieces + 6]
    act_hbm, up_hbm = refs[3 * pieces + 6 : 3 * pieces + 8]
    raw, stacked, phases, wide, act_out, up_w, held_v, held_order, *sems = refs[3 * pieces + 8 :]
    sems, out_sems = sems
    rows, frames = mains[0].shape
    local_out = up_v.shape[1]
    early = [
        pltpu.make_async_copy(up_v, held_v, sems.at[0]),
        pltpu.make_async_copy(order, held_order, sems.at[1]),
    ]
    for copy in early:
        copy.start()
    for s in range(pieces):
        here = at((idx[1] ^ s) * rows, rows, 16)
        raw[here, 0:LANES] = sides[s][:, 0:LANES]
        raw[here, LANES : LANES + frames] = mains[s][...]
        raw[here, LANES + frames :] = sides[s][:, LANES:]
    kept = [
        pltpu.make_async_copy(up_w, up_hbm, out_sems.at[0]),
        pltpu.make_async_copy(act_out, act_hbm, out_sems.at[1]),
    ]
    total = frames + 2 * LANES
    count = stacked.shape[1]
    channels = raw.shape[0]
    shift = total - (LANES - HALO // 8)
    ids = pltpu.roll(jnp.broadcast_to(frame_id[...], (8, total)), shift, axis=1)
    before = pltpu.roll(ids, 1, axis=1)
    after = pltpu.roll(ids, total - 1, axis=1)
    left = jnp.where(before == ids, 1.0, 0.0)[0:1, :].astype(BF)
    right = jnp.where(after == ids, 1.0, 0.0)[0:1, :].astype(BF)
    step = channels
    for r0 in range(0, channels, step):
        part = pl.ds(r0, step)
        acted = unit_act(raw[part, :].astype(F32)).astype(BF)
        act_out[part, :] = acted[:, LANES : LANES + frames]
        moved = pltpu.roll(acted, shift, axis=1)
        one = pltpu.roll(moved, 1, axis=1) * left
        two = pltpu.roll(moved, total - 1, axis=1) * right
        stacked[part, :] = moved[:, 0:count]
        stacked[pl.ds(channels + r0, step), :] = one[:, 0:count]
        stacked[pl.ds(2 * channels + r0, step), :] = two[:, 0:count]
    kept[1].start()
    early[0].wait()
    scale = up_g[...] / jnp.sqrt(up_sq[...])
    for k in range(up_v.shape[0]):
        up_w[k * local_out : (k + 1) * local_out, :] = (held_v[k] * scale).astype(BF)
    kept[0].start()
    eye = eye_mask(local_out)
    bias = to_col(up_b[...], eye)
    bias4 = jnp.concatenate([bias] * 4, axis=0)
    quarter = 4 * local_out
    for c0 in range(0, count, 3 * LANES):
        cols = pl.ds(c0, 3 * LANES)
        center = stacked[0:channels, cols]
        low = dot(up_w[quarter : 2 * quarter, :], center)
        low = low + dot(up_w[3 * quarter : 4 * quarter, :], stacked[channels : 2 * channels, cols])
        high = dot(up_w[2 * quarter : 3 * quarter, :], center)
        high = high + dot(up_w[0:quarter, :], stacked[2 * channels : 3 * channels, cols])
        low = (low + bias4).astype(BF)
        high = (high + bias4).astype(BF)
        for b in range(3):
            block = c0 // LANES + b
            if block * local_out >= phases.shape[0]:
                continue
            for r in range(8):
                source = (low, high)[r // 4]
                phases[block * local_out : (block + 1) * local_out, r * LANES : (r + 1) * LANES] = (
                    source[
                        (r % 4) * local_out : (r % 4 + 1) * local_out,
                        b * LANES : (b + 1) * LANES,
                    ]
                )
    early[1].wait()
    turned = dot(phases[...], held_order[...]).astype(BF)
    for block in range(count // LANES):
        wide[:, block * 1024 : (block + 1) * 1024] = turned[
            block * local_out : (block + 1) * local_out, :
        ]
    own = 8 * frames // pieces
    for s in range(pieces):
        outs[s][...] = wide[:, at((idx[1] ^ s) * own, own + 2 * HALO, LANES)]
    for copy in kept:
        copy.wait()


def sample_masks(sample_id, distance):
    width = sample_id.shape[1]
    ids = jnp.broadcast_to(sample_id[...], (8, width))
    back = pltpu.roll(ids, distance, axis=1)
    ahead = pltpu.roll(ids, width - distance, axis=1)
    return (
        jnp.where(back == ids, 1.0, 0.0)[0:1, :].astype(BF),
        jnp.where(ahead == ids, 1.0, 0.0)[0:1, :].astype(BF),
    )


def forward_kernel(pieces, blocks, idx, *refs):
    parts = refs[:pieces]
    plain, sample_id, silence = refs[pieces : pieces + 3]
    outs = refs[pieces + 3 : 2 * pieces + 3]
    kept = refs[2 * pieces + 3 : 2 * pieces + 8]
    hidden, taps, pair, final = refs[2 * pieces + 8 :]
    keep_h, keep_u, keep_m, keep_sh, keep_sc = kept
    rows, width = parts[0].shape
    channels = pieces * rows
    for s in range(pieces):
        hidden[at((idx[1] ^ s) * rows, rows, 16), :] = parts[s][...]
    for j in range(blocks):
        distance = 3**j
        tail = plain[j, :, 5 * channels : 5 * channels + TAIL].astype(F32)
        dil_b = tail[:, 0:1] + tail[:, 1:2]
        out_b = tail[:, 2:3] + tail[:, 3:4]

        low = hidden[...]
        keep_h[j] = low
        pair[channels : 2 * channels, :] = low
        acted, slope = unit(low.astype(F32))
        acted = acted.astype(BF)
        taps[channels : 2 * channels, :] = acted
        keep_u[j] = acted
        keep_sh[j] = slope.astype(BF)
        back, ahead = sample_masks(sample_id, distance)
        center = taps[channels : 2 * channels, :]
        taps[0:channels, :] = pltpu.roll(center, distance, axis=1) * back
        taps[2 * channels : 3 * channels, :] = pltpu.roll(center, width - distance, axis=1) * ahead

        inner = dot(plain[j, :, 0 : 3 * channels], taps[...]) + dil_b
        acted, slope = unit(inner)
        acted = acted.astype(BF)
        pair[0:channels, :] = acted
        keep_m[j] = acted
        keep_sc[j] = slope.astype(BF)
        after = dot(plain[j, :, 3 * channels : 5 * channels], pair[...]) + out_b
        if j < blocks - 1:
            hidden[...] = after.astype(BF)
        else:
            final[...] = after.astype(BF)
    own = width - 2 * HALO
    voiced = silence[:, at(idx[1] * own, own, LANES)].astype(F32)
    moved = pltpu.roll(final[...], width - HALO, axis=1)[:, 0:own]
    hidden[:, 0:own] = moved * voiced.astype(BF)
    for s in range(pieces):
        outs[s][...] = hidden[at((idx[1] ^ s) * rows, rows, 16), 0:own]


def spread_taps(j, center, sample_id, taps):
    channels, width = center.shape
    distance = 3**j
    back, ahead = sample_masks(sample_id, distance)
    taps[channels : 2 * channels, :] = center
    taps[0:channels, :] = pltpu.roll(center, width - distance, axis=1) * ahead
    taps[2 * channels : 3 * channels, :] = pltpu.roll(center, distance, axis=1) * back


def backward_kernel(pieces, idx, *refs):
    parts = refs[:pieces]
    dil_t, point_t, sample_id, keep_sh, keep_sc = refs[pieces : pieces + 5]
    outs = refs[pieces + 5 : 2 * pieces + 5]
    errs, inners, taps, low = refs[2 * pieces + 5 :]
    rows = parts[0].shape[0]
    blocks, channels, width = errs.shape
    last = blocks - 1
    for s in range(pieces):
        errs[last, at((idx[1] ^ s) * rows, rows, 16), :] = parts[s][...]
    for j in reversed(range(blocks)):
        err = errs[j]
        inner = dot(point_t[j, :, 0:channels], err) * keep_sc[j].astype(F32)
        inner = inner.astype(BF)
        inners[j] = inner
        spread_taps(j, inner, sample_id, taps)
        spread = dot(dil_t[j], taps[...]) * keep_sh[j].astype(F32)
        after = (spread + dot(point_t[j, :, channels : 2 * channels], err)).astype(BF)
        if j > 0:
            errs[j - 1] = after
        else:
            low[...] = after
    for s in range(pieces):
        outs[s][...] = low[at((idx[1] ^ s) * rows, rows, 16), :]


def grad_kernel(pieces, sequence, idx, errs, inners, sample_id, keep_h, keep_u, keep_m, *refs):
    keep, send, taps, mats = refs
    blocks, channels, width = errs.shape
    place = lax.broadcasted_iota(jnp.int32, (8, width), 1)
    inside = jnp.logical_and(place >= HALO, place < width - HALO)
    inside = jnp.where(inside, 1.0, 0.0)[0:1, :].astype(BF)
    rows = channels // pieces
    lane = lax.broadcasted_iota(jnp.int32, (channels, channels), 1)
    tail = jnp.zeros((channels, channels), F32)
    for j in range(blocks):
        spread_taps(j, inners[j], sample_id, taps)
        err = errs[j] * inside
        owned = keep_u[j] * inside
        mats[5 * j + 3] = dot_rt(err, keep_m[j]).astype(BF)
        mats[5 * j + 4] = dot_rt(err, keep_h[j]).astype(BF)
        for k in range(3):
            mats[5 * j + k] = dot_rt(
                taps[k * channels : (k + 1) * channels, :], owned
            ).astype(BF)
        dil_sum = jnp.sum((inners[j] * inside).astype(F32), axis=1, keepdims=True)
        out_sum = jnp.sum(err.astype(F32), axis=1, keepdims=True)
        tail = tail + jnp.where(lane == 2 * j, dil_sum, 0.0)
        tail = tail + jnp.where(lane == 2 * j + 1, out_sum, 0.0)
    mats[5 * blocks] = tail.astype(BF)
    size = (5 * blocks + 1) * rows * pieces // len(sequence)
    part = min(size, rows)
    half = len(sequence) // 2
    for position, (s, t) in enumerate(sequence):
        target = (keep, send)[position // half]
        for q in range(size // part):
            place = (idx[0] ^ t) * (size // part) + q
            row = (idx[1] ^ s) * rows + lax.rem(place, rows // part) * part
            start = position % half * size + q * part
            target[start : start + part, :] = mats[
                lax.div(place, rows // part), at(row, part, 16), :
            ]


def halve_kernel(idx, keep, got, next_keep, next_send):
    half = next_keep.shape[0]
    total = keep[...].astype(F32) + got[...].astype(F32)
    next_keep[...] = total[:half].astype(BF)
    next_send[...] = total[half:].astype(BF)


def up_back_kernel(pieces, peers, orders, idx, *refs):
    parts = refs[:pieces]
    up_v, acted, frame_id, order = refs[pieces : pieces + 4]
    cols_grad, *streams = refs[pieces + 4 : pieces + 9]
    wide, stacked, phases, low_grad, held_v, held_act, held_order, sems = refs[pieces + 9 :]
    rows, width = parts[0].shape
    own = width - 2 * HALO
    length = pieces * own
    frames = length // 8
    late = []
    for source, target in ((order, held_order), (acted, held_act), (up_v, held_v)):
        late.append(pltpu.make_async_copy(source, target, sems.at[len(late)]))
        late[-1].start()
    seam = 2 * HALO
    wide[:, length + seam :] = jnp.zeros((rows, wide.shape[1] - length - seam), BF)
    for k in range(pieces + 1):
        wide[:, k * own : k * own + seam] = jnp.zeros((rows, seam), BF)
    lane = lax.broadcasted_iota(jnp.int32, (rows, seam), 1)
    for s in range(pieces):
        peer = idx[1] ^ s
        wide[:, at(peer * own + seam, own - seam, LANES)] = parts[s][:, seam:own]
        opening = lane >= jnp.where(peer == 0, 0, HALO)
        closing = lane < jnp.where(peer == pieces - 1, seam, HALO)
        here, there = at(peer * own, seam, LANES), at((peer + 1) * own, seam, LANES)
        start, stop = parts[s][:, 0:seam].astype(F32), parts[s][:, own:].astype(F32)
        wide[:, here] = wide[:, here] + jnp.where(opening, start, 0.0).astype(BF)
        wide[:, there] = wide[:, there] + jnp.where(closing, stop, 0.0).astype(BF)

    total = wide.shape[1] // 8
    blocks = total // LANES
    for block in range(blocks):
        stacked[block * rows : (block + 1) * rows, :] = wide[:, block * 1024 : (block + 1) * 1024]
    late[0].wait()
    turned = dot_rt(stacked[...], held_order[...]).astype(BF)
    for block in range(blocks):
        for r in range(8):
            phases[r * rows : (r + 1) * rows, block * LANES : (block + 1) * LANES] = turned[
                block * rows : (block + 1) * rows, r * LANES : (r + 1) * LANES
            ]
    ids = jnp.broadcast_to(frame_id[...], (8, frame_id.shape[1]))
    before = pltpu.roll(ids, 1, axis=1)
    after = pltpu.roll(ids, frame_id.shape[1] - 1, axis=1)
    inside = slice(LANES, LANES + frames)
    left = jnp.where(before == ids, 1.0, 0.0)[0:1, inside]
    right = jnp.where(after == ids, 1.0, 0.0)[0:1, inside]
    lead = HALO // 8
    eighth = 4 * rows
    sample_sum = jnp.zeros((rows, 1), F32)
    for part in range(2):
        base = phases[part * eighth : (part + 1) * eighth, :]
        center = pltpu.roll(base, total - lead, axis=1)[:, 0:frames]
        cols_grad[(4 + 4 * part) * rows : (8 + 4 * part) * rows, :] = center
        partial = jnp.sum(center.astype(F32), axis=1, keepdims=True)
        for r in range(4):
            sample_sum = sample_sum + partial[r * rows : (r + 1) * rows]
        if part == 1:
            moved = pltpu.roll(base, total - lead + 1, axis=1)[:, 0:frames]
            cols_grad[0:eighth, :] = (moved.astype(F32) * left).astype(BF)
        else:
            moved = pltpu.roll(base, total - lead - 1, axis=1)[:, 0:frames]
            cols_grad[12 * rows : 16 * rows, :] = (moved.astype(F32) * right).astype(BF)
    taps = up_v.shape[0]
    channels = up_v.shape[2]
    inner = jnp.zeros((rows, channels), F32)
    late[1].wait()
    grad = dot_rt(cols_grad[...], held_act[...])
    low_grad[...] = grad.astype(BF)
    late[2].wait()
    for k in range(taps):
        inner = inner + grad[k * rows : (k + 1) * rows] * held_v[k]
    inner = jnp.sum(inner, axis=0, keepdims=True)
    bias = jnp.concatenate(
        [to_row(sample_sum, eye_mask(rows)), jnp.zeros((1, channels - rows), F32)], axis=1
    )
    side = channels // 2
    line = lax.broadcasted_iota(jnp.int32, (SUMS, side), 0)
    sums = jnp.zeros((SUMS, side), F32)
    for number, value in enumerate((inner[:, :side], inner[:, side:], bias[:, :side])):
        high = value.astype(BF).astype(F32)
        sums = sums + jnp.where(line == 2 * number, high, 0.0)
        sums = sums + jnp.where(line == 2 * number + 1, value - high, 0.0)
    half = peers // 2
    size = taps * rows // peers
    first = (streams[0].shape[0] - SUMS) // half
    second = 2 * size - first
    streams[0][half * first :, :] = sums.astype(BF)
    streams[1][half * first :, :] = sums.astype(BF)
    for position, s in enumerate(orders[0]):
        target = streams[position // half]
        start = position % half * first
        target[start : start + first, :] = low_grad[at((idx[0] ^ s) * size, first, 16), 0:side]
    for position, s in enumerate(orders[1]):
        target = streams[2 + position // half]
        start = position % half * second
        piece = (idx[0] ^ s) * size
        target[start : start + size, :] = low_grad[at(piece, size, 16), side:]
        if size > first:
            target[start + size : start + second, :] = low_grad[
                at(piece + first, size - first, 16), 0:side
            ]


def input_back_kernel(pieces, order, idx, up_w, cols_grad, keep, send, total):
    total[...] = lax.dot_general(
        up_w[...], cols_grad[...], (((0,), (0,)), ((), ())), preferred_element_type=F32
    ).astype(BF)
    size = total.shape[0] // pieces
    for position, s in enumerate(order):
        target = (keep, send)[position // (pieces // 2)]
        start = position % (pieces // 2) * size
        target[start : start + size, :] = total[at((idx[1] ^ s) * size, size, 16), :]


def join_kernel(idx, keep, got, term, other, next_keep, next_send):
    rows = keep.shape[0] - SUMS
    half, part = rows // 2, term.shape[0] // 2
    total = keep[...].astype(F32) + got[...].astype(F32)
    grads = (term[...].astype(F32) + other[...].astype(F32)).astype(BF)
    for number, target in enumerate((next_keep, next_send)):
        target[0:half, :] = total[number * half : (number + 1) * half].astype(BF)
        target[half : half + part, :] = grads[number * part : (number + 1) * part]
        target[half + part :, :] = total[rows:].astype(BF)


def step_kernel(rows, idx, keep, got, *outs):
    total = keep[...].astype(F32) + got[...].astype(F32)
    grads = total.shape[0] - rows - SUMS
    for number, target in enumerate(outs):
        half, part = rows // 2, grads // 2
        target[0:half, :] = total[number * half : (number + 1) * half].astype(BF)
        start = rows + number * part
        target[half : half + part, :] = total[start : start + part].astype(BF)
        target[half + part :, :] = total[rows + grads :].astype(BF)


def meet_kernel(parts, idx, own, got, out, *sums):
    start = 0
    for count in parts:
        half = count // 2
        for number in range(2):
            here = start + number * half
            there = start + (1 - number) * half
            out[here : here + half, :] = (
                own[here : here + half, :].astype(F32) + got[there : there + half, :].astype(F32)
            ).astype(BF)
        start = start + count
    if sums:
        sums[0][...] = own[start:, :].astype(F32) + got[start:, :].astype(F32)


def whole_kernel(rows, joined, idx, keep, got, *refs):
    *terms, out = refs
    total = keep[...].astype(F32) + got[...].astype(F32)
    if not joined:
        out[...] = total.astype(BF)
        return
    count = terms[0].shape[0]
    out[0:rows, :] = total[0:rows].astype(BF)
    out[rows : rows + count, :] = (terms[0][...].astype(F32) + terms[1][...].astype(F32)).astype(BF)
    out[rows + count :, :] = total[rows:].astype(BF)


def double_kernel(rows, idx, own, got, out):
    grads = own.shape[0] - rows
    out[0:rows, :] = own[0:rows, :]
    out[rows : 2 * rows, :] = got[0:rows, :]
    out[2 * rows : 2 * rows + grads, :] = own[rows:, :]
    out[2 * rows + grads :, :] = got[rows:, :]


def final_kernel(orders, first, idx, *refs):
    streams = refs[:4]
    up_v, up_sq, up_g, inner_sum, dil_v, dil_g, mix_v, mix_g, skip_v, skip_g = refs[4:14]
    up_v_grad, up_g_grad, *outs = refs[14:24]
    whole, blocks_whole, staged, *block_staged, out_sems = refs[24:]
    half = len(orders[0]) // 2
    size = whole.shape[0] // (2 * half)
    side = whole.shape[1] // 2
    second = 2 * size - first
    for position, s in enumerate(orders[0]):
        start = position % half * first
        whole[at((idx[0] ^ s) * size, first, 16), 0:side] = streams[position // half][
            start : start + first, :
        ]
    for position, s in enumerate(orders[1]):
        source = streams[2 + position // half]
        start = position % half * second
        piece = (idx[0] ^ s) * size
        whole[at(piece, size, 16), side:] = source[start : start + size, :]
        if size > first:
            whole[at(piece + first, size - first, 16), 0:side] = source[
                start + size : start + second, :
            ]
    size = blocks_whole.shape[0] // (2 * half)
    for position, s in enumerate(orders[0]):
        start = half * first + position % half * size
        blocks_whole[at((idx[0] ^ s) * size, size, 16), :] = streams[position // half][
            start : start + size, :
        ]
    sent = []

    def ship(source, target):
        sent.append(pltpu.make_async_copy(source, target, out_sems.at[len(sent)]))
        sent[-1].start()

    norm = jnp.sqrt(up_sq[...])
    inner = inner_sum[...]
    scale = up_g[...] / norm
    pull = up_g[...] * inner / (norm * norm * norm)
    rows = up_v.shape[1]
    for k in range(up_v.shape[0]):
        grad = whole[k * rows : (k + 1) * rows, :].astype(F32)
        staged[k] = scale * grad - pull * up_v[k]
        ship(staged.at[k], up_v_grad.at[k])
    up_g_grad[...] = inner / norm
    dil_v_hbm, dil_g_out, dil_b_out, mix_v_hbm, mix_g_out, out_b_out, skip_v_hbm, skip_g_out = outs
    dil_v_out, mix_v_out, skip_v_out = block_staged
    eye = eye_mask(rows)
    blocks = dil_v.shape[0]
    tail = blocks_whole[5 * blocks * rows :, :].astype(F32)
    for j in range(blocks):

        def mat(m):
            start = (5 * j + m) * rows
            return blocks_whole[start : start + rows, :].astype(F32)

        square = jnp.zeros((rows, 1), F32)
        inner = jnp.zeros((rows, 1), F32)
        for k in range(3):
            v = dil_v[j, k]
            square = square + jnp.sum(v * v, axis=1, keepdims=True)
            inner = inner + jnp.sum(v * mat(k), axis=1, keepdims=True)
        norm = jnp.sqrt(square)
        gain = to_col(dil_g[j : j + 1, :], eye)
        for k in range(3):
            dil_v_out[j, k] = gain / norm * mat(k) - gain * inner / (norm**3) * dil_v[j, k]
        ship(dil_v_out.at[j], dil_v_hbm.at[j])
        dil_g_out[j : j + 1, :] = to_row(inner / norm, eye)
        for number, (vref, gref, v_out, v_hbm, g_out) in enumerate(
            (
                (mix_v, mix_g, mix_v_out, mix_v_hbm, mix_g_out),
                (skip_v, skip_g, skip_v_out, skip_v_hbm, skip_g_out),
            )
        ):
            v = vref[j]
            grad = mat(3 + number)
            norm = jnp.sqrt(jnp.sum(v * v, axis=1, keepdims=True))
            inner = jnp.sum(v * grad, axis=1, keepdims=True)
            gain = to_col(gref[j : j + 1, :], eye)
            v_out[j] = gain / norm * grad - gain * inner / (norm**3) * v
            ship(v_out.at[j], v_hbm.at[j])
            g_out[j : j + 1, :] = to_row(inner / norm, eye)
        dil_b_out[j : j + 1, :] = to_row(tail[:, 2 * j : 2 * j + 1], eye)
        out_b_out[j : j + 1, :] = to_row(tail[:, 2 * j + 1 : 2 * j + 2], eye)
    for copy in sent:
        copy.wait()


def place_kernel(pieces, idx, *refs):
    parts, out = refs[:pieces], refs[pieces]
    own = parts[0].shape[1]
    for s in range(pieces):
        out[:, at((idx[1] ^ s) * own, own, LANES)] = parts[s][...]


def stage_kernel(idx, *refs):
    *pairs, sems = refs
    half = len(pairs) // 2
    fetch(list(zip(pairs[:half], pairs[half:])), sems)


def input_kernel(idx, *refs):
    *terms, spectrogram, out = refs
    total = terms[0][...].astype(F32)
    for term in terms[1:]:
        total = total + term[...].astype(F32)
    out[...] = (total * unit(spectrogram[...].astype(F32))[1]).astype(BF)


def local(
    spectrogram_input,
    upsample_direction,
    upsample_magnitude,
    upsample_bias,
    dilated_direction,
    dilated_magnitude,
    dilated_bias,
    pointwise_direction,
    pointwise_magnitude,
    block_output_bias,
    shortcut_direction,
    shortcut_magnitude,
    cotangent,
    silence,
    segments,
):
    pieces, peers = lax.axis_size("chan"), lax.axis_size("tm")
    chan, tm = lax.axis_index("chan"), lax.axis_index("tm")
    in_rows, frames = spectrogram_input.shape
    taps, rows, in_channels = upsample_direction.shape
    blocks = dilated_direction.shape[0]
    channels = dilated_direction.shape[3]
    length = 8 * frames
    own = length // pieces
    width = own + 2 * HALO
    packed_width = 5 * channels + TAIL
    forward = [(k, k + 1) for k in range(peers - 1)]
    backward = [(k + 1, k) for k in range(peers - 1)]
    dma = pltpu.SemaphoreType.DMA
    lead = HALO // 8
    tie = lax.optimization_barrier

    spread = np.arange(8 * LANES)
    order = np.zeros((8 * LANES, 8 * LANES), np.float32)
    order[spread, 8 * (spread % LANES) + spread // LANES] = 1.0
    order = jnp.asarray(order, BF)

    silence_row = silence.reshape(1, length)
    up_g = upsample_magnitude.reshape(1, in_channels)
    edge_rows = in_rows + rows
    ahead, behind = kernel_call(
        edge_kernel,
        [((edge_rows, LANES), BF, "V")] * 2,
        [spectrogram_input, cotangent, silence_row],
        "HHH",
        scratch=[
            pltpu.VMEM((in_rows, LANES), BF),
            pltpu.VMEM((in_rows, LANES), BF),
            pltpu.VMEM((2, rows, LANES), BF),
            pltpu.VMEM((2, 1, LANES), jnp.int32),
            dma((6,)),
        ],
    )
    low_edge = lax.ppermute(ahead, "tm", forward)
    high_edge = lax.ppermute(behind, "tm", backward)
    all_mains = gather_chan(spectrogram_input)
    (up_sq,) = kernel_call(
        square_kernel, [((1, in_channels), F32, "V")], [upsample_direction], "F", micros=2
    )
    block_args = [
        dilated_direction,
        dilated_magnitude,
        dilated_bias,
        pointwise_direction,
        pointwise_magnitude,
        block_output_bias,
        shortcut_direction,
        shortcut_magnitude,
    ]
    sides = jnp.concatenate([low_edge[:in_rows], high_edge[:in_rows]], axis=1)
    block_args, sides = tie((block_args, sides))
    packed_half = ((blocks * rows // 2, packed_width), BF, "V")
    bias_in = upsample_bias.reshape(1, rows)
    packed, near, far, up_g, bias_in = kernel_call(
        prep_kernel,
        [((blocks * rows, packed_width), BF, "V"), packed_half, packed_half]
        + [((1, in_channels), F32, "R"), ((1, rows), F32, "R")],
        [*block_args, up_g, bias_in],
        "FFFFFFFFFF",
        micros=3,
    )
    held_sides = {0: sides}
    for bit in reversed(bits_of(pieces)[1:]):
        for slot in list(held_sides):
            held_sides[slot ^ bit] = swap(held_sides[slot], "chan", bit)
    near, held_sides = tie((near, held_sides))
    for slot in list(held_sides):
        held_sides[slot ^ 1] = swap(held_sides[slot], "chan", 1)
    all_sides = [held_sides[slot] for slot in range(pieces)]
    for bit in bits_of(pieces):
        up_sq = up_sq + swap(up_sq, "chan", bit)
    padded_ids = jnp.pad(segments.astype(F32), LANES, constant_values=-1.0)
    frame_id = lax.dynamic_slice_in_dim(padded_ids, tm * frames, frames + 2 * LANES)
    sample_id = jnp.repeat(
        lax.dynamic_slice_in_dim(
            padded_ids, LANES + tm * frames + chan * (own // 8) - lead, width // 8
        ),
        8,
    ).reshape(1, width)
    frame_id = frame_id.reshape(1, frames + 2 * LANES)
    top = pieces // 2
    near, all_sides[top], up_sq = tie((near, all_sides[top], up_sq))

    count = -(-(frames + 2 * lead) // LANES) * LANES
    count = -(-count // (3 * LANES)) * 3 * LANES
    up_outs = kernel_call(
        functools.partial(up_kernel, pieces),
        [((rows, width), BF, "R")]
        + [((rows, width), BF, "V")] * (pieces - 1)
        + [((in_channels, frames), BF, "H"), ((taps * rows, in_channels), BF, "H")],
        all_mains
        + all_sides
        + [upsample_direction, up_sq, up_g, bias_in, frame_id, order],
        "V" * (2 * pieces) + "HVRRVH",
        scratch=[
            pltpu.VMEM((in_channels, frames + 2 * LANES), BF),
            pltpu.VMEM((3 * in_channels, count), BF),
            pltpu.VMEM((count // LANES * rows, 8 * LANES), BF),
            pltpu.VMEM((rows, 8 * count), BF),
            pltpu.VMEM((in_channels, frames), BF),
            pltpu.VMEM((taps * rows, in_channels), BF),
            pltpu.VMEM(upsample_direction.shape, F32),
            pltpu.VMEM(order.shape, BF),
            dma((2,)),
            dma((2,)),
        ],
        micros=6,
    )
    acted, up_w = up_outs[pieces:]
    chan_bits = bits_of(pieces)
    held_near = {0: near}
    for bit in reversed(chan_bits[1:]):
        for slot in list(held_near):
            held_near[slot ^ bit] = swap(held_near[slot], "chan", bit)
    hidden_parts, held_near, low_edge = tie((list(up_outs[:pieces]), held_near, low_edge))
    cut = kernel_call(
        functools.partial(cut_kernel, pieces),
        [((rows, width), BF, "R")] + [((rows, width), BF, "V")] * (pieces - 1),
        [cotangent, silence_row, low_edge, high_edge],
        "FFVV",
        scratch=[pltpu.VMEM((rows, length + 2 * LANES), BF)],
        micros=0.05,
    )
    all_hidden = exchange_chan(hidden_parts)
    all_packed = [packed, swap(packed, "chan", 1)]
    for slot in range(2, pieces, 2):
        two = [held_near[slot], swap(held_near[slot], "tm", 1)]
        two, all_hidden[top], cut = tie((two, all_hidden[top], list(cut)))
        all_packed += two + [swap(value, "chan", 1) for value in two]

    plain, dil_t, point_t = kernel_call(
        functools.partial(weight_kernel, pieces, blocks),
        [
            ((blocks, channels, packed_width), BF, "R"),
            ((blocks, channels, 3 * channels), BF, "R"),
            ((blocks, channels, 2 * channels), BF, "R"),
        ],
        all_packed,
        "V" * len(all_packed),
        micros=0.001,
    )
    cut, plain = tie((list(cut), plain))
    all_err = exchange_chan(cut)

    kept_shape = ((blocks, channels, width), BF, "R")
    forward_outs = kernel_call(
        functools.partial(forward_kernel, pieces, blocks),
        [((rows, own), BF, "V")] * pieces + [kept_shape] * 5,
        all_hidden + [plain, sample_id, silence_row],
        "R" + "V" * (pieces - 1) + "RVF",
        scratch=[
            pltpu.VMEM((channels, width), BF),
            pltpu.VMEM((3 * channels, width), BF),
            pltpu.VMEM((2 * channels, width), BF),
            pltpu.VMEM((channels, width), BF),
        ],
        micros=10,
    )
    keep_h, keep_u, keep_m, keep_sh, keep_sc = forward_outs[pieces:]
    activation_parts = list(forward_outs[:pieces])

    backward_outs = kernel_call(
        functools.partial(backward_kernel, pieces),
        [((rows, width), BF, "V")] * pieces + [kept_shape] * 2,
        all_err + [dil_t, point_t, sample_id, keep_sh, keep_sc],
        "R" + "V" * (pieces - 1) + "RRVRR",
        scratch=[
            pltpu.VMEM((3 * channels, width), BF),
            pltpu.VMEM((channels, width), BF),
        ],
        micros=10,
    )
    errs, inners = backward_outs[pieces:]
    all_low = exchange_chan(list(backward_outs[:pieces]))

    chan_order = order_of(chan_bits)
    tm_bits = bits_of(peers)
    path = [("chan", 1), ("tm", 1)] + [("chan", bit) for bit in chan_bits[1:]]
    path_order = [(0, 0)]
    for axis, bit in reversed(path + [("tm", bit) for bit in tm_bits[1:]]):
        other = [
            (s + bit, t) if axis == "chan" else (s, t + bit) for s, t in path_order
        ]
        path_order = path_order + other
    mats = 5 * blocks + 1
    share = pieces // 2 * mats * rows
    keep, send = kernel_call(
        functools.partial(grad_kernel, pieces, path_order),
        [((share, channels), BF, "V")] * 2,
        [errs, inners, sample_id, keep_h, keep_u, keep_m],
        "RRVRRR",
        scratch=[
            pltpu.VMEM((3 * channels, width), BF),
            pltpu.VMEM((mats, channels, channels), BF),
        ],
        micros=0.1,
    )

    def scatter(keep, send, path):
        for axis, bit in path[:-1]:
            got = swap(send, axis, bit)
            next_shape = ((keep.shape[0] // 2, keep.shape[1]), BF, "V")
            keep, send = kernel_call(halve_kernel, [next_shape] * 2, [keep, got], "VV")
        return keep, swap(send, *path[-1])

    keep, send, all_low[top] = tie((keep, send, all_low[top]))
    got = swap(send, *path[0])
    keep, send = kernel_call(
        halve_kernel, [((share // 2, channels), BF, "V")] * 2, [keep, got], "VV"
    )
    block_terms = scatter(keep, send, path[1:])
    send, all_low = tie((send, all_low))

    turned_bits = tm_bits[1:] + tm_bits[:1]
    orders = (order_of(tm_bits), order_of(turned_bits))
    half = peers // 2
    total_rows = taps * rows
    size = total_rows // peers
    side = in_channels // 2
    first = max(16, size // 2 // 16 * 16)
    second = 2 * size - first
    cols_grad, keep_one, send_one, keep_two, send_two = kernel_call(
        functools.partial(up_back_kernel, pieces, peers, orders),
        [((total_rows, frames), BF, "R")]
        + [((half * first + SUMS, side), BF, "V")] * 2
        + [((half * second, side), BF, "V")] * 2,
        all_low + [upsample_direction, acted, frame_id, order],
        "V" * pieces + "HHVH",
        scratch=[
            pltpu.VMEM((rows, 8 * count), BF),
            pltpu.VMEM((count // LANES * rows, 8 * LANES), BF),
            pltpu.VMEM((8 * rows, count), BF),
            pltpu.VMEM((total_rows, in_channels), BF),
            pltpu.VMEM(upsample_direction.shape, F32),
            pltpu.VMEM((in_channels, frames), BF),
            pltpu.VMEM(order.shape, BF),
            dma((3,)),
        ],
        micros=5,
    )

    piece_rows = pieces // 2 * in_rows
    keep, send = kernel_call(
        functools.partial(input_back_kernel, pieces, chan_order),
        [((piece_rows, frames), BF, "V")] * 2,
        [up_w, cols_grad],
        "FR",
        scratch=[pltpu.VMEM((in_channels, frames), BF)],
        micros=3,
    )
    keep, send_one = tie((keep, send_one))

    steps = len(tm_bits)
    block_rows = mats * rows
    one_rows, two_rows = half * first, half * second
    for step in range(steps - 1):
        got_one = swap(send_one, "tm", tm_bits[step])
        got_two = swap(send_two, "tm", turned_bits[step])
        if step == 0:
            got_one, got_two, keep, send = tie((got_one, got_two, keep, send))
            activation_parts, got_one = tie((activation_parts, got_one))
            activation_parts = exchange_chan(activation_parts)
            input_terms = scatter(keep, send, [("chan", bit) for bit in chan_bits])
        else:
            got_one, got_two = tie((got_one, got_two))
        one_rows, two_rows, block_rows = one_rows // 2, two_rows // 2, block_rows // 2
        if step < steps - 2:
            next_shape = ((one_rows + block_rows // 2 + SUMS, side), BF, "V")
            if step == 0:
                keep_one, send_one = kernel_call(
                    join_kernel, [next_shape] * 2, [keep_one, got_one, *block_terms], "VVVV"
                )
            else:
                keep_one, send_one = kernel_call(
                    functools.partial(step_kernel, 2 * one_rows),
                    [next_shape] * 2,
                    [keep_one, got_one],
                    "VV",
                )
            keep_two, send_two = kernel_call(
                halve_kernel, [((two_rows, side), BF, "V")] * 2, [keep_two, got_two], "VV"
            )
    joined = steps == 2
    one_rows, two_rows = 2 * one_rows, 2 * two_rows
    (held_one,) = kernel_call(
        functools.partial(whole_kernel, one_rows, joined),
        [((one_rows + block_rows + SUMS, side), BF, "V")],
        [keep_one, got_one, *(block_terms if joined else ())],
        "VVVV" if joined else "VV",
    )
    (held_two,) = kernel_call(
        functools.partial(whole_kernel, two_rows, False),
        [((two_rows, side), BF, "V")],
        [keep_two, got_two],
        "VV",
    )
    got_one = swap(held_one, "tm", tm_bits[-1])
    got_two = swap(held_two, "tm", turned_bits[-1])
    got_one, got_two, input_terms = tie((got_one, got_two, input_terms))
    own_one, sums = kernel_call(
        functools.partial(meet_kernel, (one_rows, block_rows)),
        [((one_rows + block_rows, side), BF, "V"), ((SUMS, side), F32, "V")],
        [held_one, got_one],
        "VV",
    )
    (own_two,) = kernel_call(
        functools.partial(meet_kernel, (two_rows,)),
        [((two_rows, side), BF, "V")],
        [held_two, got_two],
        "VV",
    )
    for step in reversed(range(steps - 1)):
        got_one = swap(own_one, "tm", tm_bits[step])
        got_two = swap(own_two, "tm", turned_bits[step])
        if step == steps - 2:
            got_one, got_two, activation_parts = tie((got_one, got_two, activation_parts))
        else:
            got_one, got_two = tie((got_one, got_two))
        if step > 0:
            (own_one,) = kernel_call(
                functools.partial(double_kernel, one_rows),
                [((2 * own_one.shape[0], side), BF, "V")],
                [own_one, got_one],
                "VV",
            )
            one_rows = 2 * one_rows
            own_two = jnp.concatenate([own_two, got_two], axis=0)

    pair = sums[0:6:2] + sums[1:6:2]
    inner_sum = pair[0:2].reshape(1, in_channels)
    for bit in chan_bits:
        inner_sum = inner_sum + swap(inner_sum, "chan", bit)

    (input_grad,) = kernel_call(
        input_kernel,
        [((in_rows, frames), BF, "V")],
        [*input_terms, spectrogram_input],
        "VVF",
    )
    (activation,) = kernel_call(
        functools.partial(place_kernel, pieces),
        [((rows, length), BF, "V")],
        activation_parts,
        "V" * pieces,
        micros=2,
    )

    late_args = [
        upsample_direction,
        dilated_direction,
        dilated_magnitude,
        pointwise_direction,
        pointwise_magnitude,
        shortcut_direction,
        shortcut_magnitude,
    ]
    late_args, sums = tie((late_args, sums))
    staged = kernel_call(
        stage_kernel,
        [(arg.shape, arg.dtype, "R") for arg in late_args],
        late_args,
        "H" * len(late_args),
        scratch=[dma((len(late_args),))],
        micros=2,
    )
    final_outs = kernel_call(
        functools.partial(final_kernel, orders, first),
        [
            (upsample_direction.shape, F32, "H"),
            ((1, in_channels), F32, "V"),
            (dilated_direction.shape, F32, "H"),
            (dilated_magnitude.shape, F32, "V"),
            (dilated_bias.shape, F32, "V"),
            (pointwise_direction.shape, F32, "H"),
            (pointwise_magnitude.shape, F32, "V"),
            (block_output_bias.shape, F32, "V"),
            (shortcut_direction.shape, F32, "H"),
            (shortcut_magnitude.shape, F32, "V"),
        ],
        [
            own_one,
            got_one,
            own_two,
            got_two,
            staged[0],
            up_sq,
            up_g,
            inner_sum,
            *staged[1:],
        ],
        "VVVVRVRVRRRRRR",
        scratch=[
            pltpu.VMEM((total_rows, in_channels), BF),
            pltpu.VMEM((mats * rows, channels), BF),
            pltpu.VMEM(upsample_direction.shape, F32),
            pltpu.VMEM(dilated_direction.shape, F32),
            pltpu.VMEM(pointwise_direction.shape, F32),
            pltpu.VMEM(shortcut_direction.shape, F32),
            dma((taps + 3 * blocks,)),
        ],
        micros=5,
    )
    up_v_grad, up_g_grad, dil_v_grad, dil_g_grad, dil_b_grad = final_outs[:5]
    mix_v_grad, mix_g_grad, out_b_grad, skip_v_grad, skip_g_grad = final_outs[5:]
    return (
        activation,
        input_grad,
        up_v_grad,
        up_g_grad.reshape(in_channels),
        pair[2, :rows],
        dil_v_grad,
        dil_g_grad,
        dil_b_grad,
        mix_v_grad,
        mix_g_grad,
        out_b_grad,
        skip_v_grad,
        skip_g_grad,
    )


def solution(mesh):
    placed = (
        P("chan", "tm"),
        P(None, "chan", None),
        P(),
        P("chan"),
        P(None, None, "chan", None),
        P(None, "chan"),
        P(None, "chan"),
        P(None, "chan", None),
        P(None, "chan"),
        P(None, "chan"),
        P(None, "chan", None),
        P(None, "chan"),
        P("chan", "tm"),
        P("tm"),
        P(),
    )
    return jax.shard_map(
        local,
        mesh=mesh,
        in_specs=placed,
        out_specs=(
            P("chan", "tm"),
            P("chan", "tm"),
            P(None, "chan", None),
            P(),
            P("chan"),
            P(None, None, "chan", None),
            P(None, "chan"),
            P(None, "chan"),
            P(None, "chan", None),
            P(None, "chan"),
            P(None, "chan"),
            P(None, "chan", None),
            P(None, "chan"),
        ),
        check_vma=False,
    )
```

```python
import functools

import jax
import jax.numpy as jnp
import numpy as np
from jax import lax
from jax.experimental import pallas as pl
from jax.experimental.pallas import tpu as pltpu
from jax.sharding import PartitionSpec as P

BF = jnp.bfloat16
F32 = jnp.float32
LANES = 128
HALO = 128
TAIL = 128
SUMS = 16
VMEM_LIMIT = 20 * 1024 * 1024


def swap(values, axis, bit):
    count = lax.axis_size(axis)
    return lax.ppermute(values, axis, [(k, k ^ bit) for k in range(count)])


def bits_of(count):
    bits = []
    bit = 1
    while bit < count:
        bits.append(bit)
        bit = 2 * bit
    return bits


def order_of(bits):
    order = [0]
    for bit in reversed(bits):
        order = order + [slot + bit for slot in order]
    return order


def gather_chan(own):
    held = {0: own}
    for bit in reversed(bits_of(lax.axis_size("chan"))):
        for slot in list(held):
            held[slot ^ bit] = swap(held[slot], "chan", bit)
    return [held[slot] for slot in range(len(held))]


def exchange_chan(pieces):
    return [pieces[0]] + [swap(pieces[s], "chan", s) for s in range(1, len(pieces))]


HBM = pl.BlockSpec(memory_space=pltpu.HBM)
VMEM = pl.BlockSpec(memory_space=pltpu.VMEM)


def kernel_call(body, outs, args, specs, scratch=(), micros=1.0):
    held = []
    in_specs = []
    operands = []
    for arg, spec in zip(args, specs, strict=True):
        in_specs.append({"H": HBM, "F": HBM, "R": VMEM, "V": VMEM}[spec])
        if spec == "F":
            held.append(pltpu.VMEM(arg.shape, arg.dtype))
        if spec == "R":
            arg = pltpu.with_memory_space_constraint(arg, pltpu.VMEM)
        if spec in "HF":
            arg = pltpu.with_memory_space_constraint(arg, pltpu.HBM)
        operands.append(arg)
    out_shape = []
    out_specs = []
    for shape, dtype, spec in outs:
        out_specs.append(HBM if spec == "H" else VMEM)
        spaced = {"R": pltpu.VMEM, "H": pltpu.HBM, "V": jax.ShapeDtypeStruct}[spec]
        out_shape.append(spaced(shape, dtype))
    fetched = len(held)

    def wrapped(*refs):
        refs = list(refs)
        if fetched:
            sems = refs.pop()
            targets = refs[-fetched:]
            refs = refs[:-fetched]
            sources = [number for number, spec in enumerate(specs) if spec == "F"]
            fetch([(refs[n], target) for n, target in zip(sources, targets)], sems)
            for n, target in zip(sources, targets):
                refs[n] = target
        body((lax.axis_index("tm"), lax.axis_index("chan")), *refs)

    extra = held + ([pltpu.SemaphoreType.DMA((fetched,))] if fetched else [])
    return pl.pallas_call(
        wrapped,
        out_shape=tuple(out_shape),
        in_specs=in_specs,
        out_specs=tuple(out_specs),
        scratch_shapes=list(scratch) + extra,
        compiler_params=pltpu.CompilerParams(vmem_limit_bytes=VMEM_LIMIT),
        cost_estimate=pl.CostEstimate(
            flops=int(micros * 1.1e9), bytes_accessed=0, transcendentals=0
        ),
    )(*operands)


def fetch(pairs, sems):
    copies = [
        pltpu.make_async_copy(source, target, sems.at[number])
        for number, (source, target) in enumerate(pairs)
    ]
    for copy in copies:
        copy.start()
    for copy in copies:
        copy.wait()


def unit(values):
    th = jnp.tanh(0.5 * values)
    base = 0.6 + 0.4 * th
    return values * base, base + 0.2 * values * (1.0 - th * th)


def unit_act(values):
    return values * (0.6 + 0.4 * jnp.tanh(0.5 * values))


def dot(left, right):
    return lax.dot_general(left, right, (((1,), (0,)), ((), ())), preferred_element_type=F32)


def dot_rt(left, right):
    return lax.dot_general(left, right, (((1,), (1,)), ((), ())), preferred_element_type=F32)


def eye_mask(count):
    rows = lax.broadcasted_iota(jnp.int32, (count, count), 0)
    cols = lax.broadcasted_iota(jnp.int32, (count, count), 1)
    return rows == cols


def to_col(row, eye):
    return jnp.sum(jnp.where(eye, row, 0.0), axis=1, keepdims=True)


def to_row(col, eye):
    return jnp.sum(jnp.where(eye, col, 0.0), axis=0, keepdims=True)


def at(start, size, step):
    return pl.ds(pl.multiple_of(start, step), size)


def edge_kernel(idx, spectrogram, cot, sil, ahead, behind, front, back, sound, mask, sems):
    rows = spectrogram.shape[0]
    frames, count = spectrogram.shape[1], cot.shape[1]
    low, high = pl.ds(0, HALO), pl.ds(count - HALO, HALO)
    fetch(
        [
            (spectrogram.at[:, frames - LANES :], front),
            (spectrogram.at[:, :LANES], back),
            (cot.at[:, high], sound.at[0]),
            (cot.at[:, low], sound.at[1]),
            (sil.at[:, high], mask.at[0]),
            (sil.at[:, low], mask.at[1]),
        ],
        sems,
    )
    ahead[0:rows, :] = front[...]
    behind[0:rows, :] = back[...]
    ahead[rows:, :] = (sound[0].astype(F32) * mask[0].astype(F32)).astype(BF)
    behind[rows:, :] = (sound[1].astype(F32) * mask[1].astype(F32)).astype(BF)


def square_kernel(idx, up_v, up_sq):
    total = jnp.zeros((up_v.shape[1], up_v.shape[2]), F32)
    for k in range(up_v.shape[0]):
        rows = up_v[k]
        total = total + rows * rows
    up_sq[...] = jnp.sum(total, axis=0, keepdims=True)


def prep_kernel(
    idx, dil_v, dil_g, dil_b, mix_v, mix_g, out_b, skip_v, skip_g, up_g, up_b, packed, near, far, up_row, bias_row
):
    up_row[...] = up_g[...]
    bias_row[...] = up_b[...]
    local_out = dil_v.shape[2]
    eye = eye_mask(local_out)
    lane = lax.broadcasted_iota(jnp.int32, (local_out, TAIL), 1)
    width = dil_v.shape[3]
    for j in range(dil_v.shape[0]):
        rows = pl.ds(j * local_out, local_out)
        square = jnp.zeros((local_out, 1), F32)
        for k in range(3):
            v = dil_v[j, k]
            square = square + jnp.sum(v * v, axis=1, keepdims=True)
        norm = jnp.sqrt(square)
        scale = to_col(dil_g[j : j + 1, :], eye) / norm
        for k in range(3):
            packed[rows, k * width : (k + 1) * width] = (dil_v[j, k] * scale).astype(BF)
        for number, (vref, gref) in enumerate(((mix_v, mix_g), (skip_v, skip_g))):
            v = vref[j]
            norm = jnp.sqrt(jnp.sum(v * v, axis=1, keepdims=True))
            scale = to_col(gref[j : j + 1, :], eye) / norm
            packed[rows, (3 + number) * width : (4 + number) * width] = (v * scale).astype(BF)
        first = to_col(dil_b[j : j + 1, :], eye)
        second = to_col(out_b[j : j + 1, :], eye)
        high_one = first.astype(BF).astype(F32)
        high_two = second.astype(BF).astype(F32)
        tail = jnp.where(lane == 0, high_one, 0.0) + jnp.where(lane == 1, first - high_one, 0.0)
        tail = tail + jnp.where(lane == 2, high_two, 0.0)
        tail = tail + jnp.where(lane == 3, second - high_two, 0.0)
        packed[rows, 5 * width : 5 * width + TAIL] = tail.astype(BF)
    half = near.shape[0]
    for number, target in enumerate((near, far)):
        target[...] = packed[at(((idx[0] ^ number) & 1) * half, half, 16), :]


def cut_kernel(pieces, idx, cot, sil, low, high, *refs):
    outs, wide = refs[:pieces], refs[pieces]
    count = cot.shape[1]
    own = count // pieces
    rows = cot.shape[0]
    wide[:, 0:HALO] = low[low.shape[0] - rows :, :]
    wide[:, HALO : HALO + count] = (cot[...].astype(F32) * sil[...].astype(F32)).astype(BF)
    wide[:, HALO + count :] = high[high.shape[0] - rows :, :]
    for s in range(pieces):
        outs[s][...] = wide[:, at((idx[1] ^ s) * own, own + 2 * HALO, LANES)]


def weight_kernel(pieces, blocks, idx, *refs):
    *parts, plain, dil_t, point_t = refs
    rows = parts[0].shape[0] // blocks
    part = rows // 2
    for s in range(pieces):
        start = (idx[1] ^ s) * rows
        if s < 2:
            for j in range(blocks):
                plain[j, at(start, rows, 16), :] = parts[s][j * rows : (j + 1) * rows, :]
            continue
        for number in range(2):
            source = parts[2 + 2 * (s - 2) + number]
            first = blocks * ((idx[0] ^ number) & 1)
            for q in range(blocks):
                place = first + q
                plain[
                    lax.div(place, 2), at(start + lax.rem(place, 2) * part, part, 16), :
                ] = source[q * part : (q + 1) * part, :]
    width = plain.shape[1]
    unit_matrix = jnp.where(eye_mask(width), 1.0, 0.0).astype(BF)
    for j in range(blocks):
        for k in range(5):
            turned = dot_rt(unit_matrix, plain[j, :, k * width : (k + 1) * width]).astype(BF)
            if k < 3:
                dil_t[j, :, k * width : (k + 1) * width] = turned
            else:
                point_t[j, :, (k - 3) * width : (k - 2) * width] = turned


def up_kernel(pieces, idx, *refs):
    mains, sides = refs[:pieces], refs[pieces : 2 * pieces]
    up_v, up_sq, up_g, up_b, frame_id, order = refs[2 * pieces : 2 * pieces + 6]
    outs = refs[2 * pieces + 6 : 3 * pieces + 6]
    act_hbm, up_hbm = refs[3 * pieces + 6 : 3 * pieces + 8]
    raw, stacked, phases, wide, act_out, up_w, held_v, held_order, *sems = refs[3 * pieces + 8 :]
    sems, out_sems = sems
    rows, frames = mains[0].shape
    local_out = up_v.shape[1]
    early = [
        pltpu.make_async_copy(up_v, held_v, sems.at[0]),
        pltpu.make_async_copy(order, held_order, sems.at[1]),
    ]
    for copy in early:
        copy.start()
    for s in range(pieces):
        here = at((idx[1] ^ s) * rows, rows, 16)
        raw[here, 0:LANES] = sides[s][:, 0:LANES]
        raw[here, LANES : LANES + frames] = mains[s][...]
        raw[here, LANES + frames :] = sides[s][:, LANES:]
    kept = [
        pltpu.make_async_copy(up_w, up_hbm, out_sems.at[0]),
        pltpu.make_async_copy(act_out, act_hbm, out_sems.at[1]),
    ]
    total = frames + 2 * LANES
    count = stacked.shape[1]
    channels = raw.shape[0]
    shift = total - (LANES - HALO // 8)
    ids = pltpu.roll(jnp.broadcast_to(frame_id[...], (8, total)), shift, axis=1)
    before = pltpu.roll(ids, 1, axis=1)
    after = pltpu.roll(ids, total - 1, axis=1)
    left = jnp.where(before == ids, 1.0, 0.0)[0:1, :].astype(BF)
    right = jnp.where(after == ids, 1.0, 0.0)[0:1, :].astype(BF)
    step = channels
    for r0 in range(0, channels, step):
        part = pl.ds(r0, step)
        acted = unit_act(raw[part, :].astype(F32)).astype(BF)
        act_out[part, :] = acted[:, LANES : LANES + frames]
        moved = pltpu.roll(acted, shift, axis=1)
        one = pltpu.roll(moved, 1, axis=1) * left
        two = pltpu.roll(moved, total - 1, axis=1) * right
        stacked[part, :] = moved[:, 0:count]
        stacked[pl.ds(channels + r0, step), :] = one[:, 0:count]
        stacked[pl.ds(2 * channels + r0, step), :] = two[:, 0:count]
    kept[1].start()
    early[0].wait()
    scale = up_g[...] / jnp.sqrt(up_sq[...])
    for k in range(up_v.shape[0]):
        up_w[k * local_out : (k + 1) * local_out, :] = (held_v[k] * scale).astype(BF)
    kept[0].start()
    eye = eye_mask(local_out)
    bias = to_col(up_b[...], eye)
    bias4 = jnp.concatenate([bias] * 4, axis=0)
    quarter = 4 * local_out
    for c0 in range(0, count, 3 * LANES):
        cols = pl.ds(c0, 3 * LANES)
        center = stacked[0:channels, cols]
        low = dot(up_w[quarter : 2 * quarter, :], center)
        low = low + dot(up_w[3 * quarter : 4 * quarter, :], stacked[channels : 2 * channels, cols])
        high = dot(up_w[2 * quarter : 3 * quarter, :], center)
        high = high + dot(up_w[0:quarter, :], stacked[2 * channels : 3 * channels, cols])
        low = (low + bias4).astype(BF)
        high = (high + bias4).astype(BF)
        for b in range(3):
            block = c0 // LANES + b
            if block * local_out >= phases.shape[0]:
                continue
            for r in range(8):
                source = (low, high)[r // 4]
                phases[block * local_out : (block + 1) * local_out, r * LANES : (r + 1) * LANES] = (
                    source[
                        (r % 4) * local_out : (r % 4 + 1) * local_out,
                        b * LANES : (b + 1) * LANES,
                    ]
                )
    early[1].wait()
    turned = dot(phases[...], held_order[...]).astype(BF)
    for block in range(count // LANES):
        wide[:, block * 1024 : (block + 1) * 1024] = turned[
            block * local_out : (block + 1) * local_out, :
        ]
    own = 8 * frames // pieces
    for s in range(pieces):
        outs[s][...] = wide[:, at((idx[1] ^ s) * own, own + 2 * HALO, LANES)]
    for copy in kept:
        copy.wait()


def sample_masks(sample_id, distance):
    width = sample_id.shape[1]
    ids = jnp.broadcast_to(sample_id[...], (8, width))
    back = pltpu.roll(ids, distance, axis=1)
    ahead = pltpu.roll(ids, width - distance, axis=1)
    return (
        jnp.where(back == ids, 1.0, 0.0)[0:1, :].astype(BF),
        jnp.where(ahead == ids, 1.0, 0.0)[0:1, :].astype(BF),
    )


def forward_kernel(pieces, blocks, idx, *refs):
    parts = refs[:pieces]
    plain, sample_id, silence = refs[pieces : pieces + 3]
    outs = refs[pieces + 3 : 2 * pieces + 3]
    kept = refs[2 * pieces + 3 : 2 * pieces + 8]
    hidden, taps, pair, final = refs[2 * pieces + 8 :]
    keep_h, keep_u, keep_m, keep_sh, keep_sc = kept
    rows, width = parts[0].shape
    channels = pieces * rows
    for s in range(pieces):
        hidden[at((idx[1] ^ s) * rows, rows, 16), :] = parts[s][...]
    for j in range(blocks):
        distance = 3**j
        tail = plain[j, :, 5 * channels : 5 * channels + TAIL].astype(F32)
        dil_b = tail[:, 0:1] + tail[:, 1:2]
        out_b = tail[:, 2:3] + tail[:, 3:4]

        low = hidden[...]
        keep_h[j] = low
        pair[channels : 2 * channels, :] = low
        acted, slope = unit(low.astype(F32))
        acted = acted.astype(BF)
        taps[channels : 2 * channels, :] = acted
        keep_u[j] = acted
        keep_sh[j] = slope.astype(BF)
        back, ahead = sample_masks(sample_id, distance)
        center = taps[channels : 2 * channels, :]
        taps[0:channels, :] = pltpu.roll(center, distance, axis=1) * back
        taps[2 * channels : 3 * channels, :] = pltpu.roll(center, width - distance, axis=1) * ahead

        inner = dot(plain[j, :, 0 : 3 * channels], taps[...]) + dil_b
        acted, slope = unit(inner)
        acted = acted.astype(BF)
        pair[0:channels, :] = acted
        keep_m[j] = acted
        keep_sc[j] = slope.astype(BF)
        after = dot(plain[j, :, 3 * channels : 5 * channels], pair[...]) + out_b
        if j < blocks - 1:
            hidden[...] = after.astype(BF)
        else:
            final[...] = after
    own = width - 2 * HALO
    voiced = silence[:, at(idx[1] * own, own, LANES)].astype(F32)
    for s in range(pieces):
        here = at((idx[1] ^ s) * rows, rows, 16)
        outs[s][...] = (final[here, HALO : HALO + own] * voiced).astype(BF)


def spread_taps(j, center, sample_id, taps):
    channels, width = center.shape
    distance = 3**j
    back, ahead = sample_masks(sample_id, distance)
    taps[channels : 2 * channels, :] = center
    taps[0:channels, :] = pltpu.roll(center, width - distance, axis=1) * ahead
    taps[2 * channels : 3 * channels, :] = pltpu.roll(center, distance, axis=1) * back


def edge_start(pieces, peer):
    return jnp.where(peer < pieces // 2, 0, HALO)


def backward_kernel(pieces, idx, *refs):
    parts = refs[:pieces]
    dil_t, point_t, sample_id, keep_sh, keep_sc = refs[pieces : pieces + 5]
    outs = refs[pieces + 5 : 2 * pieces + 5]
    errs, inners, taps, low = refs[2 * pieces + 5 :]
    rows = parts[0].shape[0]
    blocks, channels, width = errs.shape
    last = blocks - 1
    for s in range(pieces):
        errs[last, at((idx[1] ^ s) * rows, rows, 16), :] = parts[s][...]
    for j in reversed(range(blocks)):
        err = errs[j]
        inner = dot(point_t[j, :, 0:channels], err) * keep_sc[j].astype(F32)
        inner = inner.astype(BF)
        inners[j] = inner
        spread_taps(j, inner, sample_id, taps)
        spread = dot(dil_t[j], taps[...]) * keep_sh[j].astype(F32)
        after = (spread + dot(point_t[j, :, channels : 2 * channels], err)).astype(BF)
        if j > 0:
            errs[j - 1] = after
        else:
            low[...] = after
    lanes = at(edge_start(pieces, idx[1]), width - HALO, LANES)
    for s in range(pieces):
        outs[s][...] = low[at((idx[1] ^ s) * rows, rows, 16), lanes]


def grad_kernel(pieces, sequence, idx, errs, inners, sample_id, keep_h, keep_u, keep_m, *refs):
    keep, send, taps, mats = refs
    blocks, channels, width = errs.shape
    inside = pl.ds(HALO, width - 2 * HALO)
    rows = channels // pieces
    lane = lax.broadcasted_iota(jnp.int32, (channels, channels), 1)
    tail = jnp.zeros((channels, channels), F32)
    for j in range(blocks):
        spread_taps(j, inners[j], sample_id, taps)
        err = errs[j, :, inside]
        mats[5 * j + 3] = dot_rt(err, keep_m[j, :, inside]).astype(BF)
        mats[5 * j + 4] = dot_rt(err, keep_h[j, :, inside]).astype(BF)
        for k in range(3):
            mats[5 * j + k] = dot_rt(
                taps[k * channels : (k + 1) * channels, inside], keep_u[j, :, inside]
            ).astype(BF)
        dil_sum = jnp.sum(inners[j, :, inside].astype(F32), axis=1, keepdims=True)
        out_sum = jnp.sum(err.astype(F32), axis=1, keepdims=True)
        tail = tail + jnp.where(lane == 2 * j, dil_sum, 0.0)
        tail = tail + jnp.where(lane == 2 * j + 1, out_sum, 0.0)
    mats[5 * blocks] = tail.astype(BF)
    size = (5 * blocks + 1) * rows * pieces // len(sequence)
    part = min(size, rows)
    half = len(sequence) // 2
    for position, (s, t) in enumerate(sequence):
        target = (keep, send)[position // half]
        for q in range(size // part):
            place = (idx[0] ^ t) * (size // part) + q
            row = (idx[1] ^ s) * rows + lax.rem(place, rows // part) * part
            start = position % half * size + q * part
            target[start : start + part, :] = mats[
                lax.div(place, rows // part), at(row, part, 16), :
            ]


def halve_kernel(idx, keep, got, next_keep, next_send):
    half = next_keep.shape[0]
    total = keep[...].astype(F32) + got[...].astype(F32)
    next_keep[...] = total[:half].astype(BF)
    next_send[...] = total[half:].astype(BF)


def up_back_kernel(pieces, peers, orders, idx, *refs):
    parts = refs[:pieces]
    up_v, acted, frame_id, order = refs[pieces : pieces + 4]
    cols_grad, *streams = refs[pieces + 4 : pieces + 9]
    wide, stacked, phases, low_grad, held_v, held_act, held_order, sems = refs[pieces + 9 :]
    rows = parts[0].shape[0]
    own = parts[0].shape[1] - HALO
    length = pieces * own
    frames = length // 8
    late = []
    for source, target in ((order, held_order), (acted, held_act), (up_v, held_v)):
        late.append(pltpu.make_async_copy(source, target, sems.at[len(late)]))
        late[-1].start()
    wide[:, HALO + length :] = jnp.zeros((rows, wide.shape[1] - HALO - length), BF)
    for s in range(pieces):
        peer = idx[1] ^ s
        source = parts[s][:, at(HALO - edge_start(pieces, peer), own, LANES)]
        wide[:, at(HALO + peer * own, own, LANES)] = source

        @pl.when(peer == 0)
        def _():
            wide[:, 0:HALO] = parts[s][:, 0:HALO]

        @pl.when(peer == pieces - 1)
        def _():
            wide[:, HALO + length : 2 * HALO + length] = parts[s][:, own:]

    total = wide.shape[1] // 8
    blocks = total // LANES
    for block in range(blocks):
        stacked[block * rows : (block + 1) * rows, :] = wide[:, block * 1024 : (block + 1) * 1024]
    late[0].wait()
    turned = dot_rt(stacked[...], held_order[...]).astype(BF)
    for block in range(blocks):
        for r in range(8):
            phases[r * rows : (r + 1) * rows, block * LANES : (block + 1) * LANES] = turned[
                block * rows : (block + 1) * rows, r * LANES : (r + 1) * LANES
            ]
    ids = jnp.broadcast_to(frame_id[...], (8, frame_id.shape[1]))
    before = pltpu.roll(ids, 1, axis=1)
    after = pltpu.roll(ids, frame_id.shape[1] - 1, axis=1)
    inside = slice(LANES, LANES + frames)
    left = jnp.where(before == ids, 1.0, 0.0)[0:1, inside]
    right = jnp.where(after == ids, 1.0, 0.0)[0:1, inside]
    lead = HALO // 8
    eighth = 4 * rows
    sample_sum = jnp.zeros((rows, 1), F32)
    for part in range(2):
        base = phases[part * eighth : (part + 1) * eighth, :]
        center = pltpu.roll(base, total - lead, axis=1)[:, 0:frames]
        cols_grad[(4 + 4 * part) * rows : (8 + 4 * part) * rows, :] = center
        partial = jnp.sum(center.astype(F32), axis=1, keepdims=True)
        for r in range(4):
            sample_sum = sample_sum + partial[r * rows : (r + 1) * rows]
        if part == 1:
            moved = pltpu.roll(base, total - lead + 1, axis=1)[:, 0:frames]
            cols_grad[0:eighth, :] = (moved.astype(F32) * left).astype(BF)
        else:
            moved = pltpu.roll(base, total - lead - 1, axis=1)[:, 0:frames]
            cols_grad[12 * rows : 16 * rows, :] = (moved.astype(F32) * right).astype(BF)
    taps = up_v.shape[0]
    channels = up_v.shape[2]
    inner = jnp.zeros((rows, channels), F32)
    late[1].wait()
    grad = dot_rt(cols_grad[...], held_act[...])
    low_grad[...] = grad.astype(BF)
    late[2].wait()
    for k in range(taps):
        inner = inner + grad[k * rows : (k + 1) * rows] * held_v[k]
    inner = jnp.sum(inner, axis=0, keepdims=True)
    bias = jnp.concatenate(
        [to_row(sample_sum, eye_mask(rows)), jnp.zeros((1, channels - rows), F32)], axis=1
    )
    side = channels // 2
    line = lax.broadcasted_iota(jnp.int32, (SUMS, side), 0)
    sums = jnp.zeros((SUMS, side), F32)
    for number, value in enumerate((inner[:, :side], inner[:, side:], bias[:, :side])):
        high = value.astype(BF).astype(F32)
        sums = sums + jnp.where(line == 2 * number, high, 0.0)
        sums = sums + jnp.where(line == 2 * number + 1, value - high, 0.0)
    half = peers // 2
    size = taps * rows // peers
    first = (streams[0].shape[0] - SUMS) // half
    second = 2 * size - first
    streams[0][half * first :, :] = sums.astype(BF)
    streams[1][half * first :, :] = sums.astype(BF)
    for position, s in enumerate(orders[0]):
        target = streams[position // half]
        start = position % half * first
        target[start : start + first, :] = low_grad[at((idx[0] ^ s) * size, first, 16), 0:side]
    for position, s in enumerate(orders[1]):
        target = streams[2 + position // half]
        start = position % half * second
        piece = (idx[0] ^ s) * size
        target[start : start + size, :] = low_grad[at(piece, size, 16), side:]
        if size > first:
            target[start + size : start + second, :] = low_grad[
                at(piece + first, size - first, 16), 0:side
            ]


def input_back_kernel(pieces, order, idx, up_w, cols_grad, keep, send, total):
    total[...] = lax.dot_general(
        up_w[...], cols_grad[...], (((0,), (0,)), ((), ())), preferred_element_type=F32
    ).astype(BF)
    size = total.shape[0] // pieces
    for position, s in enumerate(order):
        target = (keep, send)[position // (pieces // 2)]
        start = position % (pieces // 2) * size
        target[start : start + size, :] = total[at((idx[1] ^ s) * size, size, 16), :]


def join_kernel(idx, keep, got, term, other, next_keep, next_send):
    rows = keep.shape[0] - SUMS
    half, part = rows // 2, term.shape[0] // 2
    total = keep[...].astype(F32) + got[...].astype(F32)
    grads = (term[...].astype(F32) + other[...].astype(F32)).astype(BF)
    for number, target in enumerate((next_keep, next_send)):
        target[0:half, :] = total[number * half : (number + 1) * half].astype(BF)
        target[half : half + part, :] = grads[number * part : (number + 1) * part]
        target[half + part :, :] = total[rows:].astype(BF)


def step_kernel(rows, idx, keep, got, *outs):
    total = keep[...].astype(F32) + got[...].astype(F32)
    grads = total.shape[0] - rows - SUMS
    for number, target in enumerate(outs):
        half, part = rows // 2, grads // 2
        target[0:half, :] = total[number * half : (number + 1) * half].astype(BF)
        start = rows + number * part
        target[half : half + part, :] = total[start : start + part].astype(BF)
        target[half + part :, :] = total[rows + grads :].astype(BF)


def meet_kernel(parts, idx, own, got, out, *sums):
    start = 0
    for count in parts:
        half = count // 2
        for number in range(2):
            here = start + number * half
            there = start + (1 - number) * half
            out[here : here + half, :] = (
                own[here : here + half, :].astype(F32) + got[there : there + half, :].astype(F32)
            ).astype(BF)
        start = start + count
    if sums:
        sums[0][...] = own[start:, :].astype(F32) + got[start:, :].astype(F32)


def whole_kernel(rows, joined, idx, keep, got, *refs):
    *terms, out = refs
    total = keep[...].astype(F32) + got[...].astype(F32)
    if not joined:
        out[...] = total.astype(BF)
        return
    count = terms[0].shape[0]
    out[0:rows, :] = total[0:rows].astype(BF)
    out[rows : rows + count, :] = (terms[0][...].astype(F32) + terms[1][...].astype(F32)).astype(BF)
    out[rows + count :, :] = total[rows:].astype(BF)


def double_kernel(rows, idx, own, got, out):
    grads = own.shape[0] - rows
    out[0:rows, :] = own[0:rows, :]
    out[rows : 2 * rows, :] = got[0:rows, :]
    out[2 * rows : 2 * rows + grads, :] = own[rows:, :]
    out[2 * rows + grads :, :] = got[rows:, :]


def final_kernel(orders, first, idx, *refs):
    streams = refs[:4]
    up_v, up_sq, up_g, inner_sum, dil_v, dil_g, mix_v, mix_g, skip_v, skip_g = refs[4:14]
    up_v_grad, up_g_grad, *outs = refs[14:24]
    whole, blocks_whole, staged, *block_staged, out_sems = refs[24:]
    half = len(orders[0]) // 2
    size = whole.shape[0] // (2 * half)
    side = whole.shape[1] // 2
    second = 2 * size - first
    for position, s in enumerate(orders[0]):
        start = position % half * first
        whole[at((idx[0] ^ s) * size, first, 16), 0:side] = streams[position // half][
            start : start + first, :
        ]
    for position, s in enumerate(orders[1]):
        source = streams[2 + position // half]
        start = position % half * second
        piece = (idx[0] ^ s) * size
        whole[at(piece, size, 16), side:] = source[start : start + size, :]
        if size > first:
            whole[at(piece + first, size - first, 16), 0:side] = source[
                start + size : start + second, :
            ]
    size = blocks_whole.shape[0] // (2 * half)
    for position, s in enumerate(orders[0]):
        start = half * first + position % half * size
        blocks_whole[at((idx[0] ^ s) * size, size, 16), :] = streams[position // half][
            start : start + size, :
        ]
    sent = []

    def ship(source, target):
        sent.append(pltpu.make_async_copy(source, target, out_sems.at[len(sent)]))
        sent[-1].start()

    norm = jnp.sqrt(up_sq[...])
    inner = inner_sum[...]
    scale = up_g[...] / norm
    pull = up_g[...] * inner / (norm * norm * norm)
    rows = up_v.shape[1]
    for k in range(up_v.shape[0]):
        grad = whole[k * rows : (k + 1) * rows, :].astype(F32)
        staged[k] = scale * grad - pull * up_v[k]
        ship(staged.at[k], up_v_grad.at[k])
    up_g_grad[...] = inner / norm
    dil_v_hbm, dil_g_out, dil_b_out, mix_v_hbm, mix_g_out, out_b_out, skip_v_hbm, skip_g_out = outs
    dil_v_out, mix_v_out, skip_v_out = block_staged
    eye = eye_mask(rows)
    blocks = dil_v.shape[0]
    tail = blocks_whole[5 * blocks * rows :, :].astype(F32)
    for j in range(blocks):

        def mat(m):
            start = (5 * j + m) * rows
            return blocks_whole[start : start + rows, :].astype(F32)

        square = jnp.zeros((rows, 1), F32)
        inner = jnp.zeros((rows, 1), F32)
        for k in range(3):
            v = dil_v[j, k]
            square = square + jnp.sum(v * v, axis=1, keepdims=True)
            inner = inner + jnp.sum(v * mat(k), axis=1, keepdims=True)
        norm = jnp.sqrt(square)
        gain = to_col(dil_g[j : j + 1, :], eye)
        for k in range(3):
            dil_v_out[j, k] = gain / norm * mat(k) - gain * inner / (norm**3) * dil_v[j, k]
        ship(dil_v_out.at[j], dil_v_hbm.at[j])
        dil_g_out[j : j + 1, :] = to_row(inner / norm, eye)
        for number, (vref, gref, v_out, v_hbm, g_out) in enumerate(
            (
                (mix_v, mix_g, mix_v_out, mix_v_hbm, mix_g_out),
                (skip_v, skip_g, skip_v_out, skip_v_hbm, skip_g_out),
            )
        ):
            v = vref[j]
            grad = mat(3 + number)
            norm = jnp.sqrt(jnp.sum(v * v, axis=1, keepdims=True))
            inner = jnp.sum(v * grad, axis=1, keepdims=True)
            gain = to_col(gref[j : j + 1, :], eye)
            v_out[j] = gain / norm * grad - gain * inner / (norm**3) * v
            ship(v_out.at[j], v_hbm.at[j])
            g_out[j : j + 1, :] = to_row(inner / norm, eye)
        dil_b_out[j : j + 1, :] = to_row(tail[:, 2 * j : 2 * j + 1], eye)
        out_b_out[j : j + 1, :] = to_row(tail[:, 2 * j + 1 : 2 * j + 2], eye)
    for copy in sent:
        copy.wait()


def place_kernel(pieces, idx, *refs):
    parts, out = refs[:pieces], refs[pieces]
    own = parts[0].shape[1]
    for s in range(pieces):
        out[:, at((idx[1] ^ s) * own, own, LANES)] = parts[s][...]


def stage_kernel(idx, *refs):
    *pairs, sems = refs
    half = len(pairs) // 2
    fetch(list(zip(pairs[:half], pairs[half:])), sems)


def input_kernel(idx, *refs):
    *terms, spectrogram, out = refs
    total = terms[0][...].astype(F32)
    for term in terms[1:]:
        total = total + term[...].astype(F32)
    out[...] = (total * unit(spectrogram[...].astype(F32))[1]).astype(BF)


def local(
    spectrogram_input,
    upsample_direction,
    upsample_magnitude,
    upsample_bias,
    dilated_direction,
    dilated_magnitude,
    dilated_bias,
    pointwise_direction,
    pointwise_magnitude,
    block_output_bias,
    shortcut_direction,
    shortcut_magnitude,
    cotangent,
    silence,
    segments,
):
    pieces, peers = lax.axis_size("chan"), lax.axis_size("tm")
    chan, tm = lax.axis_index("chan"), lax.axis_index("tm")
    in_rows, frames = spectrogram_input.shape
    taps, rows, in_channels = upsample_direction.shape
    blocks = dilated_direction.shape[0]
    channels = dilated_direction.shape[3]
    length = 8 * frames
    own = length // pieces
    width = own + 2 * HALO
    packed_width = 5 * channels + TAIL
    forward = [(k, k + 1) for k in range(peers - 1)]
    backward = [(k + 1, k) for k in range(peers - 1)]
    dma = pltpu.SemaphoreType.DMA
    lead = HALO // 8
    tie = lax.optimization_barrier

    spread = np.arange(8 * LANES)
    order = np.zeros((8 * LANES, 8 * LANES), np.float32)
    order[spread, 8 * (spread % LANES) + spread // LANES] = 1.0
    order = jnp.asarray(order, BF)

    silence_row = silence.reshape(1, length)
    up_g = upsample_magnitude.reshape(1, in_channels)
    edge_rows = in_rows + rows
    ahead, behind = kernel_call(
        edge_kernel,
        [((edge_rows, LANES), BF, "V")] * 2,
        [spectrogram_input, cotangent, silence_row],
        "HHH",
        scratch=[
            pltpu.VMEM((in_rows, LANES), BF),
            pltpu.VMEM((in_rows, LANES), BF),
            pltpu.VMEM((2, rows, HALO), BF),
            pltpu.VMEM((2, 1, HALO), jnp.int32),
            dma((6,)),
        ],
    )
    low_edge = lax.ppermute(ahead, "tm", forward)
    high_edge = lax.ppermute(behind, "tm", backward)
    all_mains = gather_chan(spectrogram_input)
    (up_sq,) = kernel_call(
        square_kernel, [((1, in_channels), F32, "V")], [upsample_direction], "F", micros=2
    )
    block_args = [
        dilated_direction,
        dilated_magnitude,
        dilated_bias,
        pointwise_direction,
        pointwise_magnitude,
        block_output_bias,
        shortcut_direction,
        shortcut_magnitude,
    ]
    sides = jnp.concatenate([low_edge[:in_rows], high_edge[:in_rows]], axis=1)
    block_args, sides = tie((block_args, sides))
    packed_half = ((blocks * rows // 2, packed_width), BF, "V")
    bias_in = upsample_bias.reshape(1, rows)
    packed, near, far, up_g, bias_in = kernel_call(
        prep_kernel,
        [((blocks * rows, packed_width), BF, "V"), packed_half, packed_half]
        + [((1, in_channels), F32, "R"), ((1, rows), F32, "R")],
        [*block_args, up_g, bias_in],
        "FFFFFFFFFF",
        micros=3,
    )
    held_sides = {0: sides}
    for bit in reversed(bits_of(pieces)[1:]):
        for slot in list(held_sides):
            held_sides[slot ^ bit] = swap(held_sides[slot], "chan", bit)
    near, held_sides = tie((near, held_sides))
    for slot in list(held_sides):
        held_sides[slot ^ 1] = swap(held_sides[slot], "chan", 1)
    all_sides = [held_sides[slot] for slot in range(pieces)]
    for bit in bits_of(pieces):
        up_sq = up_sq + swap(up_sq, "chan", bit)
    padded_ids = jnp.pad(segments.astype(F32), LANES, constant_values=-1.0)
    frame_id = lax.dynamic_slice_in_dim(padded_ids, tm * frames, frames + 2 * LANES)
    sample_id = jnp.repeat(
        lax.dynamic_slice_in_dim(
            padded_ids, LANES + tm * frames + chan * (own // 8) - lead, width // 8
        ),
        8,
    ).reshape(1, width)
    frame_id = frame_id.reshape(1, frames + 2 * LANES)
    top = pieces // 2
    near, all_sides[top], up_sq = tie((near, all_sides[top], up_sq))

    count = -(-(frames + 2 * lead) // LANES) * LANES
    count = -(-count // (3 * LANES)) * 3 * LANES
    up_outs = kernel_call(
        functools.partial(up_kernel, pieces),
        [((rows, width), BF, "R")]
        + [((rows, width), BF, "V")] * (pieces - 1)
        + [((in_channels, frames), BF, "H"), ((taps * rows, in_channels), BF, "H")],
        all_mains
        + all_sides
        + [upsample_direction, up_sq, up_g, bias_in, frame_id, order],
        "V" * (2 * pieces) + "HVRRVH",
        scratch=[
            pltpu.VMEM((in_channels, frames + 2 * LANES), BF),
            pltpu.VMEM((3 * in_channels, count), BF),
            pltpu.VMEM((count // LANES * rows, 8 * LANES), BF),
            pltpu.VMEM((rows, 8 * count), BF),
            pltpu.VMEM((in_channels, frames), BF),
            pltpu.VMEM((taps * rows, in_channels), BF),
            pltpu.VMEM(upsample_direction.shape, F32),
            pltpu.VMEM(order.shape, BF),
            dma((2,)),
            dma((2,)),
        ],
        micros=6,
    )
    acted, up_w = up_outs[pieces:]
    chan_bits = bits_of(pieces)
    held_near = {0: near}
    for bit in reversed(chan_bits[1:]):
        for slot in list(held_near):
            held_near[slot ^ bit] = swap(held_near[slot], "chan", bit)
    hidden_parts, held_near, low_edge = tie((list(up_outs[:pieces]), held_near, low_edge))
    cut = kernel_call(
        functools.partial(cut_kernel, pieces),
        [((rows, width), BF, "R")] + [((rows, width), BF, "V")] * (pieces - 1),
        [cotangent, silence_row, low_edge, high_edge],
        "FFVV",
        scratch=[pltpu.VMEM((rows, length + 2 * HALO), BF)],
        micros=0.05,
    )
    all_hidden = exchange_chan(hidden_parts)
    all_packed = [packed, swap(packed, "chan", 1)]
    for slot in range(2, pieces, 2):
        two = [held_near[slot], swap(held_near[slot], "tm", 1)]
        two, all_hidden[top], cut = tie((two, all_hidden[top], list(cut)))
        all_packed += two + [swap(value, "chan", 1) for value in two]

    plain, dil_t, point_t = kernel_call(
        functools.partial(weight_kernel, pieces, blocks),
        [
            ((blocks, channels, packed_width), BF, "R"),
            ((blocks, channels, 3 * channels), BF, "R"),
            ((blocks, channels, 2 * channels), BF, "R"),
        ],
        all_packed,
        "V" * len(all_packed),
        micros=0.001,
    )
    cut, plain = tie((list(cut), plain))
    all_err = exchange_chan(cut)

    kept_shape = ((blocks, channels, width), BF, "R")
    forward_outs = kernel_call(
        functools.partial(forward_kernel, pieces, blocks),
        [((rows, own), BF, "V")] * pieces + [kept_shape] * 5,
        all_hidden + [plain, sample_id, silence_row],
        "R" + "V" * (pieces - 1) + "RVF",
        scratch=[
            pltpu.VMEM((channels, width), BF),
            pltpu.VMEM((3 * channels, width), BF),
            pltpu.VMEM((2 * channels, width), BF),
            pltpu.VMEM((channels, width), F32),
        ],
        micros=10,
    )
    keep_h, keep_u, keep_m, keep_sh, keep_sc = forward_outs[pieces:]
    activation_parts = list(forward_outs[:pieces])

    backward_outs = kernel_call(
        functools.partial(backward_kernel, pieces),
        [((rows, width - HALO), BF, "V")] * pieces + [kept_shape] * 2,
        all_err + [dil_t, point_t, sample_id, keep_sh, keep_sc],
        "R" + "V" * (pieces - 1) + "RRVRR",
        scratch=[
            pltpu.VMEM((3 * channels, width), BF),
            pltpu.VMEM((channels, width), BF),
        ],
        micros=10,
    )
    errs, inners = backward_outs[pieces:]
    all_low = exchange_chan(list(backward_outs[:pieces]))

    chan_order = order_of(chan_bits)
    tm_bits = bits_of(peers)
    path = [("chan", 1), ("tm", 1)] + [("chan", bit) for bit in chan_bits[1:]]
    path_order = [(0, 0)]
    for axis, bit in reversed(path + [("tm", bit) for bit in tm_bits[1:]]):
        other = [
            (s + bit, t) if axis == "chan" else (s, t + bit) for s, t in path_order
        ]
        path_order = path_order + other
    mats = 5 * blocks + 1
    share = pieces // 2 * mats * rows
    keep, send = kernel_call(
        functools.partial(grad_kernel, pieces, path_order),
        [((share, channels), BF, "V")] * 2,
        [errs, inners, sample_id, keep_h, keep_u, keep_m],
        "RRVRRR",
        scratch=[
            pltpu.VMEM((3 * channels, width), BF),
            pltpu.VMEM((mats, channels, channels), BF),
        ],
        micros=0.1,
    )

    def scatter(keep, send, path):
        for axis, bit in path[:-1]:
            got = swap(send, axis, bit)
            next_shape = ((keep.shape[0] // 2, keep.shape[1]), BF, "V")
            keep, send = kernel_call(halve_kernel, [next_shape] * 2, [keep, got], "VV")
        return keep, swap(send, *path[-1])

    keep, send, all_low[top] = tie((keep, send, all_low[top]))
    got = swap(send, *path[0])
    keep, send = kernel_call(
        halve_kernel, [((share // 2, channels), BF, "V")] * 2, [keep, got], "VV"
    )
    block_terms = scatter(keep, send, path[1:])
    send, all_low = tie((send, all_low))

    turned_bits = tm_bits[1:] + tm_bits[:1]
    orders = (order_of(tm_bits), order_of(turned_bits))
    half = peers // 2
    total_rows = taps * rows
    size = total_rows // peers
    side = in_channels // 2
    first = max(16, size // 2 // 16 * 16)
    second = 2 * size - first
    cols_grad, keep_one, send_one, keep_two, send_two = kernel_call(
        functools.partial(up_back_kernel, pieces, peers, orders),
        [((total_rows, frames), BF, "R")]
        + [((half * first + SUMS, side), BF, "V")] * 2
        + [((half * second, side), BF, "V")] * 2,
        all_low + [upsample_direction, acted, frame_id, order],
        "V" * pieces + "HHVH",
        scratch=[
            pltpu.VMEM((rows, 8 * count), BF),
            pltpu.VMEM((count // LANES * rows, 8 * LANES), BF),
            pltpu.VMEM((8 * rows, count), BF),
            pltpu.VMEM((total_rows, in_channels), BF),
            pltpu.VMEM(upsample_direction.shape, F32),
            pltpu.VMEM((in_channels, frames), BF),
            pltpu.VMEM(order.shape, BF),
            dma((3,)),
        ],
        micros=5,
    )

    piece_rows = pieces // 2 * in_rows
    keep, send = kernel_call(
        functools.partial(input_back_kernel, pieces, chan_order),
        [((piece_rows, frames), BF, "V")] * 2,
        [up_w, cols_grad],
        "FR",
        scratch=[pltpu.VMEM((in_channels, frames), BF)],
        micros=3,
    )
    keep, send_one = tie((keep, send_one))

    steps = len(tm_bits)
    block_rows = mats * rows
    one_rows, two_rows = half * first, half * second
    for step in range(steps - 1):
        got_one = swap(send_one, "tm", tm_bits[step])
        got_two = swap(send_two, "tm", turned_bits[step])
        if step == 0:
            got_one, got_two, keep, send = tie((got_one, got_two, keep, send))
            activation_parts, got_one = tie((activation_parts, got_one))
            activation_parts = exchange_chan(activation_parts)
            input_terms = scatter(keep, send, [("chan", bit) for bit in chan_bits])
        else:
            got_one, got_two = tie((got_one, got_two))
        one_rows, two_rows, block_rows = one_rows // 2, two_rows // 2, block_rows // 2
        if step < steps - 2:
            next_shape = ((one_rows + block_rows // 2 + SUMS, side), BF, "V")
            if step == 0:
                keep_one, send_one = kernel_call(
                    join_kernel, [next_shape] * 2, [keep_one, got_one, *block_terms], "VVVV"
                )
            else:
                keep_one, send_one = kernel_call(
                    functools.partial(step_kernel, 2 * one_rows),
                    [next_shape] * 2,
                    [keep_one, got_one],
                    "VV",
                )
            keep_two, send_two = kernel_call(
                halve_kernel, [((two_rows, side), BF, "V")] * 2, [keep_two, got_two], "VV"
            )
    joined = steps == 2
    one_rows, two_rows = 2 * one_rows, 2 * two_rows
    (held_one,) = kernel_call(
        functools.partial(whole_kernel, one_rows, joined),
        [((one_rows + block_rows + SUMS, side), BF, "V")],
        [keep_one, got_one, *(block_terms if joined else ())],
        "VVVV" if joined else "VV",
    )
    (held_two,) = kernel_call(
        functools.partial(whole_kernel, two_rows, False),
        [((two_rows, side), BF, "V")],
        [keep_two, got_two],
        "VV",
    )
    got_one = swap(held_one, "tm", tm_bits[-1])
    got_two = swap(held_two, "tm", turned_bits[-1])
    got_one, got_two, input_terms = tie((got_one, got_two, input_terms))
    own_one, sums = kernel_call(
        functools.partial(meet_kernel, (one_rows, block_rows)),
        [((one_rows + block_rows, side), BF, "V"), ((SUMS, side), F32, "V")],
        [held_one, got_one],
        "VV",
    )
    (own_two,) = kernel_call(
        functools.partial(meet_kernel, (two_rows,)),
        [((two_rows, side), BF, "V")],
        [held_two, got_two],
        "VV",
    )
    for step in reversed(range(steps - 1)):
        got_one = swap(own_one, "tm", tm_bits[step])
        got_two = swap(own_two, "tm", turned_bits[step])
        if step == steps - 2:
            got_one, got_two, activation_parts = tie((got_one, got_two, activation_parts))
        else:
            got_one, got_two = tie((got_one, got_two))
        if step > 0:
            (own_one,) = kernel_call(
                functools.partial(double_kernel, one_rows),
                [((2 * own_one.shape[0], side), BF, "V")],
                [own_one, got_one],
                "VV",
            )
            one_rows = 2 * one_rows
            own_two = jnp.concatenate([own_two, got_two], axis=0)

    pair = sums[0:6:2] + sums[1:6:2]
    inner_sum = pair[0:2].reshape(1, in_channels)
    for bit in chan_bits:
        inner_sum = inner_sum + swap(inner_sum, "chan", bit)

    (input_grad,) = kernel_call(
        input_kernel,
        [((in_rows, frames), BF, "V")],
        [*input_terms, spectrogram_input],
        "VVF",
    )
    (activation,) = kernel_call(
        functools.partial(place_kernel, pieces),
        [((rows, length), BF, "V")],
        activation_parts,
        "V" * pieces,
        micros=2,
    )

    late_args = [
        upsample_direction,
        dilated_direction,
        dilated_magnitude,
        pointwise_direction,
        pointwise_magnitude,
        shortcut_direction,
        shortcut_magnitude,
    ]
    late_args, sums = tie((late_args, sums))
    staged = kernel_call(
        stage_kernel,
        [(arg.shape, arg.dtype, "R") for arg in late_args],
        late_args,
        "H" * len(late_args),
        scratch=[dma((len(late_args),))],
        micros=2,
    )
    final_outs = kernel_call(
        functools.partial(final_kernel, orders, first),
        [
            (upsample_direction.shape, F32, "H"),
            ((1, in_channels), F32, "V"),
            (dilated_direction.shape, F32, "H"),
            (dilated_magnitude.shape, F32, "V"),
            (dilated_bias.shape, F32, "V"),
            (pointwise_direction.shape, F32, "H"),
            (pointwise_magnitude.shape, F32, "V"),
            (block_output_bias.shape, F32, "V"),
            (shortcut_direction.shape, F32, "H"),
            (shortcut_magnitude.shape, F32, "V"),
        ],
        [
            own_one,
            got_one,
            own_two,
            got_two,
            staged[0],
            up_sq,
            up_g,
            inner_sum,
            *staged[1:],
        ],
        "VVVVRVRVRRRRRR",
        scratch=[
            pltpu.VMEM((total_rows, in_channels), BF),
            pltpu.VMEM((mats * rows, channels), BF),
            pltpu.VMEM(upsample_direction.shape, F32),
            pltpu.VMEM(dilated_direction.shape, F32),
            pltpu.VMEM(pointwise_direction.shape, F32),
            pltpu.VMEM(shortcut_direction.shape, F32),
            dma((taps + 3 * blocks,)),
        ],
        micros=5,
    )
    up_v_grad, up_g_grad, dil_v_grad, dil_g_grad, dil_b_grad = final_outs[:5]
    mix_v_grad, mix_g_grad, out_b_grad, skip_v_grad, skip_g_grad = final_outs[5:]
    return (
        activation,
        input_grad,
        up_v_grad,
        up_g_grad.reshape(in_channels),
        pair[2, :rows],
        dil_v_grad,
        dil_g_grad,
        dil_b_grad,
        mix_v_grad,
        mix_g_grad,
        out_b_grad,
        skip_v_grad,
        skip_g_grad,
    )


def solution(mesh):
    placed = (
        P("chan", "tm"),
        P(None, "chan", None),
        P(),
        P("chan"),
        P(None, None, "chan", None),
        P(None, "chan"),
        P(None, "chan"),
        P(None, "chan", None),
        P(None, "chan"),
        P(None, "chan"),
        P(None, "chan", None),
        P(None, "chan"),
        P("chan", "tm"),
        P("tm"),
        P(),
    )
    return jax.shard_map(
        local,
        mesh=mesh,
        in_specs=placed,
        out_specs=(
            P("chan", "tm"),
            P("chan", "tm"),
            P(None, "chan", None),
            P(),
            P("chan"),
            P(None, None, "chan", None),
            P(None, "chan"),
            P(None, "chan"),
            P(None, "chan", None),
            P(None, "chan"),
            P(None, "chan"),
            P(None, "chan", None),
            P(None, "chan"),
        ),
        check_vma=False,
    )
```
